32 devices in a mesh: dp: 8 (over z, y), mp: 4 (over x, core).
Axes of the slice: x: 2, y: 2, z: 4, core: 2. Of those that a mesh axis runs over, the one named last changes fastest.
Arguments:
- tokens: bfloat16 [8192, 1152], P('dp'), may hold values from -6 to 6
- timesteps: int32 [32], P('dp'), may hold values from 0 to 999
- relative_index: int32 [256, 256], replicated, may hold values from 0 to 960, as said below
- time_table: bfloat16 [1000, 1152], replicated, may hold values from -6 to 6
- query_weight: bfloat16 [1152, 1152], replicated, may hold values from -0.1875 to 0.1875
- key_weight: bfloat16 [1152, 1152], replicated, may hold values from -0.1875 to 0.1875
- value_weight: bfloat16 [1152, 1152], replicated, may hold values from -0.1875 to 0.1875
- time_query_weight: bfloat16 [1152, 1152], replicated, may hold values from -0.1875 to 0.1875
- time_value_weight: bfloat16 [1152, 1152], replicated, may hold values from -0.09375 to 0.09375
- out_weight: bfloat16 [1152, 1152], replicated, may hold values from -0.5 to 0.5
- out_bias: float32 [1152], replicated, may hold values from -3 to 3
- first_gain: float32 [1152], replicated, may hold values from 0.5 to 1.5
- first_shift: float32 [1152], replicated, may hold values from -3 to 3
- second_gain: float32 [1152], replicated, may hold values from 0.5 to 1.5
- second_shift: float32 [1152], replicated, may hold values from -3 to 3
- up_weight: bfloat16 [1152, 4608], P(None, 'mp'), may hold values from -0.1875 to 0.1875
- up_bias: float32 [4608], P('mp'), may hold values from -3 to 3
- down_weight: bfloat16 [4608, 1152], P('mp'), may hold values from -0.09375 to 0.09375
- down_bias: float32 [1152], replicated, may hold values from -3 to 3
- bias_table: float32 [961, 16], replicated, may hold values from -4 to 4
- cotangent: bfloat16 [8192, 1152], P(('dp', 'mp')), may hold values from -6 to 6
Outputs:
- block_out: bfloat16 [8192, 1152], P(('dp', 'mp'))
- tokens_grad: float32 [8192, 1152], P(('dp', 'mp'))
- time_table_grad: float32 [1000, 1152], P(None, 'mp')
- query_weight_grad: float32 [1152, 1152], P(None, 'mp')
- key_weight_grad: float32 [1152, 1152], P(None, 'mp')
- value_weight_grad: float32 [1152, 1152], P(None, 'mp')
- time_query_grad: float32 [1152, 1152], P(None, 'mp')
- time_value_grad: float32 [1152, 1152], P(None, 'mp')
- out_weight_grad: float32 [1152, 1152], P('mp')
- out_bias_grad: float32 [1152], P('mp')
- first_gain_grad: float32 [1152], P('mp')
- first_shift_grad: float32 [1152], P('mp')
- second_gain_grad: float32 [1152], P('mp')
- second_shift_grad: float32 [1152], P('mp')
- up_weight_grad: float32 [1152, 4608], P(None, 'mp')
- up_bias_grad: float32 [4608], P('mp')
- down_weight_grad: float32 [4608, 1152], P('mp')
- down_bias_grad: float32 [1152], P('mp')
- bias_table_grad: float32 [961, 16], P(None, 'mp')
The draws below stay inside these ranges and needn't reach their ends.
Inputs may be any that keep to these rules, and one draw needn't show every extreme that they name: `relative_index`: the tokens of an image sit on distinct cells of a 16 x 16 grid; entry (i, j) is (row_i - row_j + 15) * 31 + column_i - column_j + 15.
All inputs are finite; a program needn't handle non-finite values.
Results may differ from the reference program's by a relative error of at most 0.013.
Values may be sent and summed in bfloat16 or wider, within the bound.
No kernel may reach another device: no remote copies, remote signals or barrier semaphores. Data moves between devices by JAX's collectives and lax.ppermute only.
A program may use at most 256 MiB of HBM per device.

```python
import math
import jax
import jax.numpy as jnp
from jax import lax

D = 1152
HEADS = 16
HEAD_DIM = 72
FF = 4608
NSTEPS = 1000
SIDE = 16
SEQ = 256
NREL = 961
IMAGES = 32
TOKENS = 8192


def draw_relative_index(key, part):
    key = jax.random.fold_in(key, 7)
    order = jax.random.permutation(key, SIDE * SIDE).astype(jnp.int32)
    row_of = order // SIDE
    column_of = order % SIDE
    row_stride = 2 * SIDE - 1
    return ((row_of[:, None] - row_of[None, :] + SIDE - 1) * row_stride + column_of[:, None] - column_of[None, :] + SIDE - 1).astype(jnp.int32)


def with_ends(result, own_key, low, largest):
    longest = result.shape.index(max(result.shape))
    spots = []
    for shift in (0, 1):
        where = [jax.random.randint(jax.random.fold_in(own_key, axis), (), 0, length) for axis, length in enumerate(result.shape)]
        where[longest] = (where[longest] + shift) % result.shape[longest]
        spots.append(tuple(where))
    return result.at[spots[0]].set(low).at[spots[1]].set(largest)


def shard_levels(own_key, shape, pieces, smallest, largest):
    gain = 1.0
    for position, blocks in pieces:
        draws = jax.random.uniform(jax.random.fold_in(jax.random.fold_in(own_key, 6), position), (blocks,), jnp.float32, smallest / len(pieces), largest / len(pieces))
        gain = gain * jnp.repeat(jnp.exp(draws), shape[position] // blocks).reshape((-1,) + (1,) * (len(shape) - 1 - position))
    return gain


def bell_draw(stream_key, extent, width, most, shards=(), held_as=jnp.bfloat16):
    entries = width * jax.random.normal(stream_key, extent, jnp.float32)
    if shards:
        entries = entries * shard_levels(stream_key, extent, shards, -0.22, 0.18)
    return jnp.clip(entries, -most, most).astype(held_as)


def setup_inputs(seed: int = 0) -> dict:
    streams_of = jax.random.split(jax.random.key(seed), 22)
    return {
        "tokens": bell_draw(streams_of[0], (TOKENS, D), 1.0, 6.0, ((0, 8),)),
        "timesteps": with_ends(jax.random.randint(streams_of[1], (IMAGES,), 0, NSTEPS), jax.random.fold_in(streams_of[1], 1), 0, NSTEPS - 1).astype(jnp.int32),
        "relative_index": draw_relative_index(jax.random.fold_in(streams_of[21], 71), 0),
        "time_table": bell_draw(streams_of[3], (NSTEPS, D), 1.0, 6.0),
        "query_weight": bell_draw(streams_of[4], (D, D), D ** -0.5, 0.1875),
        "key_weight": bell_draw(streams_of[5], (D, D), D ** -0.5, 0.1875),
        "value_weight": bell_draw(streams_of[6], (D, D), D ** -0.5, 0.1875),
        "time_query_weight": bell_draw(streams_of[7], (D, D), D ** -0.5, 0.1875),
        "time_value_weight": bell_draw(streams_of[8], (D, D), (4 * D) ** -0.5, 0.09375),
        "out_weight": bell_draw(streams_of[9], (D, D), (D // 8) ** -0.5, 0.5),
        "out_bias": bell_draw(streams_of[10], (D,), 0.5, 3.0, (), jnp.float32),
        "first_gain": jnp.clip(1.0 + 0.1 * jax.random.normal(streams_of[11], (D,), jnp.float32), 0.5, 1.5),
        "first_shift": bell_draw(streams_of[12], (D,), 0.5, 3.0, (), jnp.float32),
        "second_gain": jnp.clip(1.0 + 0.1 * jax.random.normal(streams_of[13], (D,), jnp.float32), 0.5, 1.5),
        "second_shift": bell_draw(streams_of[14], (D,), 0.5, 3.0, (), jnp.float32),
        "up_weight": bell_draw(streams_of[15], (D, FF), D ** -0.5, 0.1875, ((1, 4),)),
        "up_bias": bell_draw(streams_of[16], (FF,), 0.5, 3.0, ((0, 4),), jnp.float32),
        "down_weight": bell_draw(streams_of[17], (FF, D), FF ** -0.5, 0.09375, ((0, 4),)),
        "down_bias": bell_draw(streams_of[18], (D,), 0.5, 3.0, (), jnp.float32),
        "bias_table": bell_draw(streams_of[19], (NREL, HEADS), 1.0, 4.0, (), jnp.float32),
        "cotangent": bell_draw(streams_of[20], (TOKENS, D), 1.0, 6.0, ((0, 32),)),
    }


EPSILON = 1e-06
HIGHEST = lax.Precision.HIGHEST

@jax.custom_vjp
def low(v):
    return lax.optimization_barrier(v.astype(jnp.bfloat16)).astype(jnp.float32)

@jax.custom_vjp
def low_back(v):
    return v

def low_keep(v):
    return (low(v), None)

def low_pass(kept, grad):
    return (grad,)

def back_keep(v):
    return (v, None)

def back_low(kept, grad):
    return (low(grad),)
low.defvjp(low_keep, low_pass)
low_back.defvjp(back_keep, back_low)

def layer_norm(values, gain_row, shift_row):
    average = lax.optimization_barrier(jnp.mean(values, axis=-1, keepdims=True))
    centred = values - average
    variance = lax.optimization_barrier(jnp.mean(centred * centred, axis=-1, keepdims=True))
    return centred * lax.rsqrt(variance + EPSILON) * gain_row + shift_row

def attend_group(query_rows, key_rows, value_rows, bias_full):
    scores = jnp.einsum('gqhe,gkhe->ghqk', query_rows, key_rows, precision=HIGHEST) * HEAD_DIM ** (-0.5) + bias_full[None]
    scores = low_back(scores)
    row_top = lax.optimization_barrier(jnp.max(scores, axis=-1, keepdims=True))
    weights = jnp.exp(scores - row_top)
    probabilities = low(weights / lax.optimization_barrier(jnp.sum(weights, axis=-1, keepdims=True)))
    return jnp.einsum('ghqk,gkhe->gqhe', probabilities, value_rows, precision=HIGHEST)

def reference(tokens, timesteps, relative_index, time_table, query_weight, key_weight, value_weight, time_query_weight, time_value_weight, out_weight, out_bias, first_gain, first_shift, second_gain, second_shift, up_weight, up_bias, down_weight, down_bias, bias_table, cotangent):
    images = tokens.shape[0] // SEQ
    group_size = math.gcd(images, max(1, 4096 // SEQ))
    checkpointed = jax.checkpoint(attend_group)

    def split_heads(rows):
        return rows.reshape(images // group_size, group_size, SEQ, HEADS, HEAD_DIM)

    def forward(tokens, time_table, query_weight, key_weight, value_weight, time_query_weight, time_value_weight, out_weight, out_bias, first_gain, first_shift, second_gain, second_shift, up_weight, up_bias, down_weight, down_bias, bias_table):
        embedding = jnp.take(time_table, timesteps, axis=0)
        normed_first = low(layer_norm(tokens, first_gain, first_shift))
        time_query = jnp.dot(embedding, time_query_weight, precision=HIGHEST)
        time_value = jnp.dot(embedding, time_value_weight, precision=HIGHEST)
        query_rows = jnp.dot(normed_first, query_weight, precision=HIGHEST).reshape(images, SEQ, D) + time_query[:, None, :]
        query_rows = low(low_back(query_rows.reshape(-1, D)))
        key_rows = low(low_back(jnp.dot(normed_first, key_weight, precision=HIGHEST)))
        value_rows = jnp.dot(normed_first, value_weight, precision=HIGHEST).reshape(images, SEQ, D) + time_value[:, None, :]
        value_rows = low(low_back(value_rows.reshape(-1, D)))
        bias_full = jnp.transpose(jnp.take(bias_table, relative_index, axis=0), (2, 0, 1))

        def one_group(block_rows):
            return checkpointed(block_rows[0], block_rows[1], block_rows[2], bias_full)
        mixed = lax.map(one_group, (split_heads(query_rows), split_heads(key_rows), split_heads(value_rows)))
        mixed = low(low_back(mixed.reshape(-1, D)))
        middle = tokens + low_back(jnp.dot(mixed, out_weight, precision=HIGHEST)) + out_bias
        normed_second = low(layer_norm(middle, second_gain, second_shift))
        hidden = low_back(jnp.dot(normed_second, up_weight, precision=HIGHEST) + up_bias)
        active = low(jax.nn.gelu(hidden, approximate=True))
        return middle + jnp.dot(active, down_weight, precision=HIGHEST) + down_bias
    inputs_list = (tokens, time_table, query_weight, key_weight, value_weight, time_query_weight, time_value_weight, out_weight, out_bias, first_gain, first_shift, second_gain, second_shift, up_weight, up_bias, down_weight, down_bias, bias_table)
    widened = [member.astype(jnp.float32) for member in inputs_list]
    output, pullback = jax.vjp(forward, *widened)
    grads = pullback(cotangent.astype(jnp.float32))
    return (output.astype(jnp.bfloat16), grads[0], grads[1], grads[2], grads[3], grads[4], grads[5], grads[6], grads[7], grads[8], grads[9], grads[10], grads[11], grads[12], grads[13], grads[14], grads[15], grads[16], grads[17])
```

```python
import math
from functools import partial

import jax
import jax.numpy as jnp
from jax import lax
from jax.experimental import pallas as pl
from jax.experimental.pallas import tpu as pltpu
from jax.sharding import PartitionSpec as P

EPSILON = 1e-06
HIGHEST = lax.Precision.HIGHEST
F32 = jnp.float32
BF16 = jnp.bfloat16
LANES = 128
VMEM_BYTES = 60 * 1024 * 1024


def mm(left, right):
    return lax.dot_general(left, right, (((1,), (0,)), ((), ())), preferred_element_type=F32)


def mm_nt(left, right):
    return lax.dot_general(left, right, (((1,), (1,)), ((), ())), preferred_element_type=F32)


def mm_tn(left, right):
    return lax.dot_general(left, right, (((0,), (0,)), ((), ())), preferred_element_type=F32)


def round_up(value, step):
    return -(-value // step) * step


def head_window(slot, head_width):
    first = slot * head_width // LANES * LANES
    last = round_up((slot + 1) * head_width, LANES)
    return first, last - first, slot * head_width - first


def head_mask(lanes, offset, head_width):
    lane = lax.broadcasted_iota(jnp.int32, (1, lanes), 1)
    return jnp.where((lane >= offset) & (lane < offset + head_width), 1.0, 0.0).astype(BF16)


def unit_rows(values):
    centred = values - jnp.mean(values, axis=-1, keepdims=True)
    inverse = lax.rsqrt(jnp.mean(centred * centred, axis=-1, keepdims=True) + EPSILON)
    return centred * inverse, inverse


def norm_back(grad_out, unit, inverse, gain_row):
    grad_unit = grad_out * gain_row
    first_mean = jnp.mean(grad_unit, axis=-1, keepdims=True)
    second_mean = jnp.mean(grad_unit * unit, axis=-1, keepdims=True)
    return inverse * (grad_unit - first_mean - unit * second_mean)


def add_tiles(tiles, product, first):
    for part in range(product.shape[1] // LANES):
        place = first // LANES + part
        piece = product[:, part * LANES : (part + 1) * LANES]
        tiles[place] = piece if tiles[place] is None else tiles[place] + piece


def squeeze_matrix(side):
    wide = lax.broadcasted_iota(jnp.int32, (2 * LANES, LANES), 0)
    close = lax.broadcasted_iota(jnp.int32, (2 * LANES, LANES), 1)
    same = (wide // (2 * side) == close // side) & (wide % (2 * side) == close % side)
    return jnp.where(same, 1.0, 0.0).astype(BF16)


def split_two(values):
    high = values.astype(BF16)
    return high, (values - high.astype(F32)).astype(BF16)


def attend_kernel(
    dims,
    place_ref,
    tokens_ref,
    embed_ref,
    table_ref,
    first_gain,
    first_shift,
    second_gain,
    second_shift,
    out_bias,
    query_hbm,
    key_hbm,
    value_hbm,
    time_query_hbm,
    time_value_hbm,
    out_hbm,
    query_ref,
    key_ref,
    value_ref,
    probs_ref,
    mixed_ref,
    middle_ref,
    normed_ref,
    weights,
    wide_high,
    wide_low,
    windows,
    flat,
    sems,
):
    groups, slots, head_width, side, scale = dims
    group_width = slots * head_width
    sources = (query_hbm, key_hbm, value_hbm, time_query_hbm, time_value_hbm, out_hbm)
    order = (0, 3, 1, 2, 4, 5)
    copies = {}
    for item in order:
        copies[item] = pltpu.make_async_copy(sources[item], weights.at[item], sems.at[item])
        copies[item].start()
    heads = groups * slots
    row_lanes = table_ref.shape[1]
    for head in range(heads):
        row = jnp.broadcast_to(table_ref[head : head + 1, :], (side, row_lanes))
        shifted = pltpu.roll(row, row_lanes - (side - 1), 1, stride=1, stride_axis=0)
        high, low = split_two(shifted)
        wide_high[head * side : (head + 1) * side, :] = high
        wide_low[head * side : (head + 1) * side, :] = low
    squeeze = squeeze_matrix(side)
    for part in range(row_lanes // (2 * LANES)):
        span = slice(part * 2 * LANES, (part + 1) * 2 * LANES)
        narrow = mm(wide_high[:, span], squeeze) + mm(wide_low[:, span], squeeze)
        windows[:, :, part * LANES : (part + 1) * LANES] = narrow.reshape(heads, side, LANES)
    own = mm(place_ref[...], tokens_ref[...])
    unit, _ = unit_rows(own)
    normed = (unit * first_gain[...] + first_shift[...]).astype(BF16)

    def into_groups(rows, target):
        fill = jnp.zeros((rows.shape[0], target.shape[2] - group_width), rows.dtype)
        for group in range(groups):
            piece = rows[:, group * group_width : (group + 1) * group_width]
            target[group] = jnp.concatenate([piece, fill], axis=1)

    copies[0].wait()
    product = mm(normed, weights[0])
    copies[3].wait()
    product = product + mm(embed_ref[...], weights[3])[0:1]
    into_groups(product.astype(BF16), query_ref)
    copies[1].wait()
    into_groups(mm(normed, weights[1]).astype(BF16), key_ref)
    copies[2].wait()
    product = mm(normed, weights[2])
    copies[4].wait()
    product = product + mm(embed_ref[...], weights[4])[0:1]
    into_groups(product.astype(BF16), value_ref)
    length = own.shape[0]
    span_lanes = windows.shape[2]

    def one_group(group, carry):
        tiles = [None] * (query_ref.shape[2] // LANES)
        for slot in range(slots):
            head = group * slots + slot
            first, lanes, offset = head_window(slot, head_width)
            mask = head_mask(lanes, offset, head_width)
            window = windows[head]
            blocks = [None] * side
            steps = LANES // side
            for turn in range(steps):
                turned = window
                if turn:
                    turned = pltpu.roll(window, span_lanes - turn * side, 1)
                for jump in range(-(-side // steps)):
                    block = side - 1 - (jump * steps + turn)
                    if block >= 0:
                        blocks[block] = turned[:, jump * LANES : jump * LANES + length]
            bias = jnp.concatenate(blocks, axis=0)
            keys = key_ref[group, :, first : first + lanes]
            queries = query_ref[group, :, first : first + lanes] * mask
            scores = mm_nt(keys, queries) * scale + bias
            weights_now = jnp.exp(scores - jnp.max(scores, axis=0, keepdims=True))
            totals = jnp.sum(weights_now, axis=0, keepdims=True)
            probs = (weights_now * (1.0 / totals)).astype(BF16)
            probs_ref[head] = probs
            values = value_ref[group, :, first : first + lanes] * mask
            add_tiles(tiles, mm_tn(probs, values), first)
        mixed_ref[group] = jnp.concatenate(tiles, axis=1).astype(BF16)
        return carry

    lax.fori_loop(0, groups, one_group, 0)
    for group in range(groups):
        flat[:, group * group_width : (group + 1) * group_width] = mixed_ref[group][:, :group_width]
    copies[5].wait()
    middle = own + mm(flat[...], weights[5]) + out_bias[...]
    middle_ref[...] = middle
    unit, _ = unit_rows(middle)
    normed_ref[...] = (unit * second_gain[...] + second_shift[...]).astype(BF16)


def normed_kernel(rank_ref, place_ref, tokens_ref, gain, shift, normed_ref):
    unit, _ = unit_rows(mm(place_ref[...], tokens_ref[...]))
    normed_ref[...] = (unit * gain[...] + shift[...]).astype(BF16)


def gelu_pair(hidden):
    root = math.sqrt(2.0 / math.pi)
    square = hidden * hidden
    bend = jnp.tanh(hidden * (root + (root * 0.044715) * square))
    half = 0.5 + 0.5 * bend
    slope = half + (0.5 * hidden) * (1.0 - bend * bend) * (root + (3.0 * root * 0.044715) * square)
    return hidden * half, slope


def feed_kernel(chunks, *refs):
    normed = refs[:chunks]
    cotangent = refs[chunks : 2 * chunks]
    up_ref, up_bias, down_ref = refs[2 * chunks : 2 * chunks + 3]
    outs = refs[2 * chunks + 3 :]
    out_parts = outs[:chunks]
    grad_parts = outs[chunks : 2 * chunks]
    down_grad, up_grad, up_bias_grad = outs[2 * chunks : 2 * chunks + 3]
    active, grad_hidden, all_normed, all_cotangent = outs[2 * chunks + 3 :]
    rows = normed[0].shape[0]
    bias_total = None
    for chunk in range(chunks):
        span = slice(chunk * rows, (chunk + 1) * rows)
        all_normed[span, :] = normed[chunk][...]
        all_cotangent[span, :] = cotangent[chunk][...]
        hidden = mm(normed[chunk][...], up_ref[...]) + up_bias[...]
        gelu_out, slope = gelu_pair(hidden)
        active[span, :] = gelu_out.astype(BF16)
        back = mm_nt(cotangent[chunk][...], down_ref[...]) * slope
        rounded = back.astype(BF16)
        grad_hidden[span, :] = rounded
        total = jnp.sum(rounded.astype(F32), axis=0, keepdims=True)
        bias_total = total if bias_total is None else bias_total + total
    up_bias_grad[...] = jnp.broadcast_to(bias_total, up_bias_grad.shape)
    down_grad[...] = mm_tn(active[...], all_cotangent[...]).astype(BF16)
    up_grad[...] = mm_tn(all_normed[...], grad_hidden[...]).astype(BF16)
    for chunk in range(chunks):
        span = slice(chunk * rows, (chunk + 1) * rows)
        grad_parts[chunk][...] = mm_nt(grad_hidden[span, :], up_ref[...]).astype(BF16)
    for chunk in range(chunks):
        span = slice(chunk * rows, (chunk + 1) * rows)
        out_parts[chunk][...] = mm(active[span, :], down_ref[...]).astype(BF16)


def middle_kernel(
    own_ref, far_ref, middle_ref, cotangent_ref, gain, grad_ref, branch_ref, sums_ref
):
    grad_normed = own_ref[...].astype(F32) + far_ref[...].astype(F32)
    unit, inverse = unit_rows(middle_ref[...])
    cotangent = cotangent_ref[...].astype(F32)
    grad_middle = cotangent + norm_back(grad_normed, unit, inverse, gain[...])
    grad_ref[...] = grad_middle
    branch_ref[...] = grad_middle.astype(BF16)
    sums_ref[...] = jnp.zeros_like(sums_ref)
    sums_ref[0:1, :] = jnp.sum(grad_normed * unit, axis=0, keepdims=True)
    sums_ref[1:2, :] = jnp.sum(grad_normed, axis=0, keepdims=True)
    sums_ref[2:3, :] = jnp.sum(grad_middle, axis=0, keepdims=True)
    sums_ref[3:4, :] = jnp.sum(cotangent, axis=0, keepdims=True)


def attend_back_kernel(
    dims,
    rank_ref,
    branch_ref,
    query_ref,
    key_ref,
    value_ref,
    probs_ref,
    out_ref,
    packed_ref,
    flat_ref,
    sums_ref,
    table_ref,
    grad_mixed,
    sheared,
    grads,
):
    groups, slots, head_width, side, scale = dims
    group_width = slots * head_width
    rank = rank_ref[0]
    length = branch_ref.shape[0]
    fill = jnp.zeros((length, grad_mixed.shape[2] - group_width), BF16)
    product = mm_nt(branch_ref[...], out_ref[...]).astype(BF16)
    for group in range(groups):
        piece = product[:, group * group_width : (group + 1) * group_width]
        grad_mixed[group] = jnp.concatenate([piece, fill], axis=1)
    span_lanes = sheared.shape[2]

    def one_group(group, carry):
        wide = grad_mixed.shape[2] // LANES
        query_tiles, key_tiles, value_tiles = [None] * wide, [None] * wide, [None] * wide
        for slot in range(slots):
            head = group * slots + slot
            first, lanes, offset = head_window(slot, head_width)
            mask = head_mask(lanes, offset, head_width)
            span = slice(first, first + lanes)
            mixed_now = grad_mixed[group, :, span] * mask
            probs = probs_ref[head]
            grad_probs = mm_nt(value_ref[group, :, span], mixed_now)
            probs_wide = probs.astype(F32)
            weighted = probs_wide * grad_probs
            grad_scores = weighted - probs_wide * jnp.sum(weighted, axis=0, keepdims=True)
            rounded = grad_scores.astype(BF16)
            add_tiles(value_tiles, mm(probs, mixed_now), first)
            add_tiles(key_tiles, mm(rounded, query_ref[group, :, span] * mask), first)
            add_tiles(query_tiles, mm_tn(rounded, key_ref[group, :, span] * mask), first)
            steps = LANES // side
            shear = jnp.zeros((side, span_lanes), F32)
            for turn in range(steps):
                summed = None
                for jump in range(-(-side // steps)):
                    block = side - 1 - (jump * steps + turn)
                    if block >= 0:
                        piece = grad_scores[block * side : (block + 1) * side, :]
                        parts = []
                        if jump:
                            parts.append(jnp.zeros((side, jump * LANES), F32))
                        parts.append(piece)
                        rest = span_lanes - jump * LANES - length
                        if rest:
                            parts.append(jnp.zeros((side, rest), F32))
                        piece = jnp.concatenate(parts, axis=1)
                        summed = piece if summed is None else summed + piece
                shear = shear + (pltpu.roll(summed, turn * side, 1) if turn else summed)
            sheared[:, pl.ds(head, 1), :] = shear[:, None, :]
        grads[0, group] = (jnp.concatenate(query_tiles, axis=1) * scale).astype(BF16)
        grads[1, group] = (jnp.concatenate(key_tiles, axis=1) * scale).astype(BF16)
        grads[2, group] = jnp.concatenate(value_tiles, axis=1).astype(BF16)
        return carry

    lax.fori_loop(0, groups, one_group, 0)
    packed_lanes = packed_ref.shape[2]
    for group in range(groups):
        pieces = [grads[item, group][:, :group_width] for item in range(3)]
        for item in range(3):
            flat_ref[item, :, group * group_width : (group + 1) * group_width] = pieces[item]
        if packed_lanes > 3 * group_width:
            pieces.append(jnp.zeros((length, packed_lanes - 3 * group_width), BF16))
        packed_ref[group ^ rank] = jnp.concatenate(pieces, axis=1)
    sums_ref[...] = jnp.zeros_like(sums_ref)
    sums_ref[0:1, :] = jnp.sum(flat_ref[0].astype(F32), axis=0, keepdims=True)
    sums_ref[1:2, :] = jnp.sum(flat_ref[2].astype(F32), axis=0, keepdims=True)
    squeeze = squeeze_matrix(side)
    heads = groups * slots
    table = jnp.zeros(table_ref.shape, F32)
    for column in range(side):
        high, low = split_two(sheared[column])
        parts = []
        for part in range(span_lanes // LANES):
            span = slice(part * LANES, (part + 1) * LANES)
            parts.append(mm_nt(high[:, span], squeeze) + mm_nt(low[:, span], squeeze))
        spread = jnp.concatenate(parts, axis=1)
        turn = side - 1 - column
        table = table + (pltpu.roll(spread, turn, 1) if turn else spread)
    table_ref[...] = table


def tokens_kernel(
    flat_ref,
    query_ref,
    key_ref,
    value_ref,
    tokens_ref,
    place_ref,
    gain,
    middle_ref,
    grad_ref,
    sums_ref,
):
    grad_normed = (
        mm_nt(flat_ref[0], query_ref[...])
        + mm_nt(flat_ref[1], key_ref[...])
        + mm_nt(flat_ref[2], value_ref[...])
    )
    unit, inverse = unit_rows(mm(place_ref[...], tokens_ref[...]))
    total = middle_ref[...] + norm_back(grad_normed, unit, inverse, gain[...])
    high, low = split_two(total)
    grad_ref[...] = mm_tn(place_ref[...], high) + mm_tn(place_ref[...], low)
    sums_ref[...] = jnp.zeros_like(sums_ref)
    sums_ref[0:1, :] = jnp.sum(grad_normed * unit, axis=0, keepdims=True)
    sums_ref[1:2, :] = jnp.sum(grad_normed, axis=0, keepdims=True)


def weights_kernel(chunks, group_width, *refs):
    normed = refs[0]
    packed = refs[1 : 1 + chunks]
    branch = refs[1 + chunks : 1 + 2 * chunks]
    mixed = refs[1 + 2 * chunks : 1 + 3 * chunks]
    out_ref, all_packed, all_branch, all_mixed = refs[1 + 3 * chunks :]
    rows = packed[0].shape[0]
    for chunk in range(chunks):
        span = slice(chunk * rows, (chunk + 1) * rows)
        all_packed[span, :] = packed[chunk][...]
        all_branch[span, :] = branch[chunk][...]
        all_mixed[span, :] = mixed[chunk][...]
    left = mm_tn(normed[...], all_packed[...]).astype(BF16)
    right = mm_tn(all_branch[...], all_mixed[...]).astype(BF16)
    out_ref[...] = jnp.concatenate([left[:, : 3 * group_width], right[:, :group_width]], axis=1)


def call(kernel, outs, scratch=(), flops=0, moved=0, **extra):
    return pl.pallas_call(
        kernel,
        out_shape=outs,
        scratch_shapes=list(scratch),
        compiler_params=pltpu.CompilerParams(vmem_limit_bytes=VMEM_BYTES),
        cost_estimate=pl.CostEstimate(flops=flops, bytes_accessed=moved, transcendentals=0),
        **extra,
    )


def shape_of(*sizes, dtype=BF16):
    return jax.ShapeDtypeStruct(sizes, dtype)


VMEM = pl.BlockSpec(memory_space=pltpu.VMEM)
HBM = pl.BlockSpec(memory_space=pl.ANY)
SMEM = pl.BlockSpec(memory_space=pltpu.SMEM)


def swap(array, axis, distance):
    size = lax.axis_size(axis)
    return lax.ppermute(array, axis, [(i, i ^ distance) for i in range(size)])


def add_low(left, right):
    return (left.astype(F32) + right.astype(F32)).astype(BF16)


def reduce_over_dp(unit, order):
    rank = lax.axis_index("dp")
    halves = order[:2]
    current = unit
    for level in halves:
        bit = (rank >> level) & 1
        half = current.shape[0] // 2
        sent = lax.dynamic_slice_in_dim(current, (1 - bit) * half, half, 0)
        kept = lax.dynamic_slice_in_dim(current, bit * half, half, 0)
        current = add_low(kept, swap(sent, "dp", 1 << level))
    for level in order[2:]:
        current = add_low(current, swap(current, "dp", 1 << level))
    for level in halves[::-1]:
        bit = (rank >> level) & 1
        other = swap(current, "dp", 1 << level)
        current = jnp.where(
            bit == 0,
            jnp.concatenate([current, other], axis=0),
            jnp.concatenate([other, current], axis=0),
        )
    return current


def on_device(
    tokens,
    timesteps,
    relative_index,
    time_table,
    query_weight,
    key_weight,
    value_weight,
    time_query_weight,
    time_value_weight,
    out_weight,
    out_bias,
    first_gain,
    first_shift,
    second_gain,
    second_shift,
    up_weight,
    up_bias,
    down_weight,
    down_bias,
    bias_table,
    cotangent,
):
    length = relative_index.shape[0]
    width = tokens.shape[1]
    heads = bias_table.shape[1]
    head_width = width // heads
    side = math.isqrt(length)
    groups = lax.axis_size("mp")
    dp_size = lax.axis_size("dp")
    rank = lax.axis_index("mp")
    slots = heads // groups
    group_width = slots * head_width
    group_lanes = round_up(group_width, LANES)
    packed_lanes = round_up(3 * group_width, LANES)
    hidden_width = up_weight.shape[1]
    dims = (groups, slots, head_width, side, head_width ** (-0.5))
    ranks = jnp.reshape(rank, (1,)).astype(jnp.int32)
    row = lambda vector: vector.reshape(1, -1)

    stride = 2 * side - 1
    first_row = relative_index[0]
    row_part = first_row // stride
    column_part = first_row % stride
    cells = (jnp.max(row_part) - row_part) * side + jnp.max(column_part) - column_part
    place = (jnp.arange(length, dtype=jnp.int32)[:, None] == cells[None, :]).astype(BF16)
    own_cotangent = mm(place, cotangent).astype(BF16)

    def gather_mp(own):
        near = swap(own, "mp", 1)
        far = swap(own, "mp", 2)
        return [own, near, far, swap(far, "mp", 1)]

    all_cotangent = gather_mp(own_cotangent)
    own_tokens = lax.dynamic_slice_in_dim(tokens, rank * length, length, 0)
    own_step = lax.dynamic_index_in_dim(timesteps, rank, 0, keepdims=False)
    own_embed = lax.dynamic_slice_in_dim(time_table, own_step, 1, 0)
    embed_rows = jnp.broadcast_to(own_embed, (16, width))
    table_lanes = 2 * side
    table = jnp.pad(
        bias_table.T.reshape(heads, stride, stride), ((0, 0), (0, 1), (0, 1))
    ).reshape(heads, table_lanes * table_lanes)
    span_lanes = table_lanes * side
    outs = call(
        partial(attend_kernel, dims),
        [
            shape_of(groups, length, group_lanes),
            shape_of(groups, length, group_lanes),
            shape_of(groups, length, group_lanes),
            shape_of(heads, length, length),
            shape_of(groups, length, group_lanes),
            shape_of(length, width, dtype=F32),
            shape_of(length, width),
        ],
        [
            pltpu.VMEM((6, width, width), BF16),
            pltpu.VMEM((heads * side, table_lanes * table_lanes), BF16),
            pltpu.VMEM((heads * side, table_lanes * table_lanes), BF16),
            pltpu.VMEM((heads, side, span_lanes), F32),
            pltpu.VMEM((length, width), BF16),
            pltpu.SemaphoreType.DMA((6,)),
        ],
        flops=8 * length * width * width,
        moved=24 * width * width,
        in_specs=[VMEM] * 9 + [HBM] * 6,
    )(
        place,
        own_tokens,
        embed_rows,
        table,
        row(first_gain),
        row(first_shift),
        row(second_gain),
        row(second_shift),
        row(out_bias),
        query_weight,
        key_weight,
        value_weight,
        time_query_weight,
        time_value_weight,
        out_weight,
    )
    query_rows, key_rows, value_rows, probs, mixed, middle, normed_second = outs
    all_normed = gather_mp(normed_second)

    normed_first = pl.pallas_call(
        normed_kernel,
        out_shape=shape_of(groups * length, width),
        grid_spec=pltpu.PrefetchScalarGridSpec(
            num_scalar_prefetch=1,
            grid=(groups,),
            in_specs=[
                pl.BlockSpec((length, length), lambda i, me: (0, 0)),
                pl.BlockSpec((length, width), lambda i, me: (i ^ me[0], 0)),
                pl.BlockSpec((1, width), lambda i, me: (0, 0)),
                pl.BlockSpec((1, width), lambda i, me: (0, 0)),
            ],
            out_specs=pl.BlockSpec((length, width), lambda i, me: (i, 0)),
        ),
    )(ranks, place, tokens, row(first_gain), row(first_shift))

    rows = groups * length
    feed = call(
        partial(feed_kernel, groups),
        [shape_of(length, width)] * (2 * groups)
        + [
            shape_of(hidden_width, width),
            shape_of(width, hidden_width),
            shape_of(8, hidden_width, dtype=F32),
        ],
        [
            pltpu.VMEM((rows, hidden_width), BF16),
            pltpu.VMEM((rows, hidden_width), BF16),
            pltpu.VMEM((rows, width), BF16),
            pltpu.VMEM((rows, width), BF16),
        ],
        flops=12 * rows * width * hidden_width,
        moved=8 * width * hidden_width,
    )(*all_normed, *all_cotangent, up_weight, row(up_bias), down_weight)
    out_parts = feed[:groups]
    grad_parts = feed[groups : 2 * groups]
    down_grad, up_grad, up_bias_sum = feed[2 * groups :]

    levels = list(range(dp_size.bit_length() - 1))
    other_order = levels[1:2] + levels[:1] + levels[2:]

    def scatter_mp(parts):
        kept = parts[0].astype(F32) + swap(parts[1], "mp", 1).astype(F32)
        sent = add_low(parts[2], swap(parts[3], "mp", 1))
        return kept, swap(sent, "mp", 2)

    grad_own, grad_far = scatter_mp(grad_parts)
    down_total = reduce_over_dp(down_grad, levels)
    up_total = reduce_over_dp(up_grad, other_order)

    grad_middle, grad_branch, middle_sums = call(
        middle_kernel,
        [
            shape_of(length, width, dtype=F32),
            shape_of(length, width),
            shape_of(8, width, dtype=F32),
        ],
    )(grad_own, grad_far, middle, own_cotangent, row(second_gain))
    all_branch = gather_mp(grad_branch)

    packed, flat_grads, head_sums, table_grad = call(
        partial(attend_back_kernel, dims),
        [
            shape_of(groups, length, packed_lanes),
            shape_of(3, length, width),
            shape_of(8, width, dtype=F32),
            shape_of(heads, table_lanes * table_lanes, dtype=F32),
        ],
        [
            pltpu.VMEM((groups, length, group_lanes), BF16),
            pltpu.VMEM((side, heads, span_lanes), F32),
            pltpu.VMEM((3, groups, length, group_lanes), BF16),
        ],
        flops=2 * length * width * width,
        moved=4 * width * width,
        in_specs=[SMEM] + [VMEM] * 6,
    )(ranks, grad_branch, query_rows, key_rows, value_rows, probs, out_weight)

    def exchange_mp(parts):
        return [parts[0]] + [swap(parts[j], "mp", j) for j in range(1, groups)]

    all_packed = exchange_mp([packed[j] for j in range(groups)])
    mixed_turned = [
        lax.dynamic_index_in_dim(mixed, rank ^ j, 0, keepdims=False) for j in range(groups)
    ]
    all_mixed = exchange_mp(mixed_turned)

    tokens_grad, token_sums = call(
        tokens_kernel,
        [shape_of(length, width, dtype=F32), shape_of(8, width, dtype=F32)],
        flops=6 * length * width * width,
        moved=6 * width * width,
    )(
        flat_grads,
        query_weight,
        key_weight,
        value_weight,
        own_tokens,
        place,
        row(first_gain),
        grad_middle,
    )

    unit = call(
        partial(weights_kernel, groups, group_width),
        shape_of(width, 4 * group_width),
        [
            pltpu.VMEM((rows, packed_lanes), BF16),
            pltpu.VMEM((rows, width), BF16),
            pltpu.VMEM((rows, group_lanes), BF16),
        ],
        flops=8 * rows * width * group_width,
        moved=8 * rows * width,
    )(normed_first, *all_packed, *all_branch, *all_mixed)
    unit_total = reduce_over_dp(unit, levels).astype(F32)
    query_grad, key_grad, value_grad, out_grad = [
        unit_total[:, j * group_width : (j + 1) * group_width] for j in range(4)
    ]
    out_grad = out_grad.T

    step_row = jnp.full((1, width), own_step, F32)
    image_rows = jnp.concatenate(
        [head_sums[0:2], own_embed.astype(F32), step_row, jnp.zeros((4, width), F32)], axis=0
    )
    image_all = lax.all_gather(image_rows, ("dp", "mp"), axis=0, tiled=True)
    image_all = image_all.reshape(-1, 8, width)
    query_sums, value_sums, embed_all = image_all[:, 0], image_all[:, 1], image_all[:, 2]
    steps_all = image_all[:, 3, 0].astype(jnp.int32)

    def own_block(array, axis_number):
        extent = array.shape[axis_number] // groups
        return lax.dynamic_slice_in_dim(array, rank * extent, extent, axis_number)

    contract_first = (((0,), (0,)), ((), ()))
    contract_last = (((1,), (1,)), ((), ()))
    time_query_grad = lax.dot_general(
        embed_all, own_block(query_sums, 1), contract_first, precision=HIGHEST
    )
    time_value_grad = lax.dot_general(
        embed_all, own_block(value_sums, 1), contract_first, precision=HIGHEST
    )
    grad_embed = lax.dot_general(
        query_sums, own_block(time_query_weight, 0).astype(F32), contract_last, precision=HIGHEST
    ) + lax.dot_general(
        value_sums, own_block(time_value_weight, 0).astype(F32), contract_last, precision=HIGHEST
    )
    onehot = jnp.arange(time_table.shape[0], dtype=jnp.int32)[:, None] == steps_all[None, :]
    time_table_grad = jnp.dot(onehot.astype(F32), grad_embed, precision=HIGHEST)

    vectors = jnp.concatenate([middle_sums[0:4], token_sums[0:2]], axis=0)
    vectors = vectors.reshape(6, groups, group_width).transpose(1, 0, 2).reshape(groups, -1)
    short = jnp.concatenate([vectors, table_grad.reshape(groups, -1)], axis=1)
    for level in range(groups.bit_length() - 1):
        short = short + swap(short, "mp", 1 << level)
    short = lax.dynamic_index_in_dim(short, rank, 0, keepdims=False)
    short = jnp.concatenate([short, up_bias_sum[0]])
    for level in levels:
        short = short + swap(short, "dp", 1 << level)
    parts = [short[j * group_width : (j + 1) * group_width] for j in range(6)]
    second_gain_grad, second_shift_grad, out_bias_grad, down_bias_grad = parts[:4]
    first_gain_grad, first_shift_grad = parts[4:]
    table_size = slots * table_lanes * table_lanes
    table_own = short[6 * group_width : 6 * group_width + table_size]
    table_own = table_own.reshape(slots, table_lanes, table_lanes)[:, :stride, :stride]
    bias_table_grad = table_own.reshape(slots, stride * stride).T
    up_bias_grad = short[6 * group_width + table_size :]

    out_own, out_far = scatter_mp(out_parts)
    block_out = (middle + out_own + out_far.astype(F32) + down_bias).astype(BF16)
    block_out = mm_tn(place, block_out).astype(BF16)
    return (
        block_out,
        tokens_grad,
        time_table_grad,
        query_grad,
        key_grad,
        value_grad,
        time_query_grad,
        time_value_grad,
        out_grad,
        out_bias_grad,
        first_gain_grad,
        first_shift_grad,
        second_gain_grad,
        second_shift_grad,
        up_total.astype(F32),
        up_bias_grad,
        down_total.astype(F32),
        down_bias_grad,
        bias_table_grad,
    )


def solution(mesh):
    whole = P()
    rows = P(("dp", "mp"), None)
    columns = P(None, "mp")
    split = P("mp")
    placed = (
        (P("dp", None), P("dp"))
        + (whole,) * 13
        + (columns, split, P("mp", None), whole, whole, rows)
    )
    return jax.shard_map(
        on_device,
        mesh=mesh,
        in_specs=placed,
        out_specs=(rows, rows)
        + (columns,) * 6
        + (P("mp", None),)
        + (split,) * 5
        + (columns, split, P("mp", None), split, columns),
        check_vma=False,
    )
```

```python
import math
from functools import partial

import jax
import jax.numpy as jnp
from jax import lax
from jax.experimental import pallas as pl
from jax.experimental.pallas import tpu as pltpu
from jax.sharding import PartitionSpec as P

EPSILON = 1e-06
HIGHEST = lax.Precision.HIGHEST
F32 = jnp.float32
BF16 = jnp.bfloat16
LANES = 128


def mm(left, right):
    return lax.dot_general(left, right, (((1,), (0,)), ((), ())), preferred_element_type=F32)


def mm_nt(left, right):
    return lax.dot_general(left, right, (((1,), (1,)), ((), ())), preferred_element_type=F32)


def mm_tn(left, right):
    return lax.dot_general(left, right, (((0,), (0,)), ((), ())), preferred_element_type=F32)


def round_up(value, step):
    return -(-value // step) * step


def head_window(slot, head_width):
    first = slot * head_width // LANES * LANES
    last = round_up((slot + 1) * head_width, LANES)
    return first, last - first, slot * head_width - first


def head_mask(lanes, offset, head_width):
    lane = lax.broadcasted_iota(jnp.int32, (1, lanes), 1)
    return jnp.where((lane >= offset) & (lane < offset + head_width), 1.0, 0.0).astype(BF16)


def unit_rows(values):
    centred = values - jnp.mean(values, axis=-1, keepdims=True)
    inverse = lax.rsqrt(jnp.mean(centred * centred, axis=-1, keepdims=True) + EPSILON)
    return centred * inverse, inverse


def norm_back(grad_out, unit, inverse, gain_row):
    grad_unit = grad_out * gain_row
    first_mean = jnp.mean(grad_unit, axis=-1, keepdims=True)
    second_mean = jnp.mean(grad_unit * unit, axis=-1, keepdims=True)
    return inverse * (grad_unit - first_mean - unit * second_mean)


def add_tiles(tiles, product, first):
    for part in range(product.shape[1] // LANES):
        place = first // LANES + part
        piece = product[:, part * LANES : (part + 1) * LANES]
        tiles[place] = piece if tiles[place] is None else tiles[place] + piece


def squeeze_part(part, side, stride):
    each = LANES // side
    first = part * each * stride // LANES * LANES
    last = round_up((part * each + each - 1) * stride + side, LANES)
    wide = lax.broadcasted_iota(jnp.int32, (last - first, LANES), 0) + first
    close = lax.broadcasted_iota(jnp.int32, (last - first, LANES), 1)
    same = wide == (part * each + close // side) * stride + close % side
    return first, last - first, jnp.where(same, 1.0, 0.0).astype(BF16)


def place_matrix(relative_row, side):
    stride = 2 * side - 1
    entry = relative_row.astype(F32)
    row_part = jnp.floor((entry + 0.5) * (1.0 / stride))
    column_part = entry - row_part * stride
    row_part = jnp.max(row_part, axis=1, keepdims=True) - row_part
    column_part = jnp.max(column_part, axis=1, keepdims=True) - column_part
    cells = (row_part * side + column_part).astype(jnp.int32)
    length = side * side
    cell = lax.broadcasted_iota(jnp.int32, (length, length), 0)
    return jnp.where(cell == cells, 1.0, 0.0).astype(BF16)


def split_two(values):
    high = values.astype(BF16)
    return high, (values - high.astype(F32)).astype(BF16)


def attend_kernel(
    dims,
    ranks,
    steps_ref,
    relative_ref,
    table_ref,
    first_gain,
    first_shift,
    second_gain,
    second_shift,
    out_bias,
    tokens_hbm,
    times_hbm,
    query_hbm,
    key_hbm,
    value_hbm,
    time_query_hbm,
    time_value_hbm,
    out_hbm,
    query_ref,
    key_ref,
    value_ref,
    probs_ref,
    mixed_ref,
    middle_ref,
    normed_ref,
    embed_ref,
    weights,
    own_tokens,
    times,
    table,
    wide_high,
    wide_low,
    windows,
    flat,
    sems,
):
    groups, slots, head_width, side, scale = dims
    group_width = slots * head_width
    rank = ranks[0]
    length = side * side
    step = steps_ref[rank]
    own_copy = pltpu.make_async_copy(
        tokens_hbm.at[pl.ds(pl.multiple_of(rank * length, length), length)], own_tokens, sems.at[6]
    )
    own_copy.start()
    sources = (query_hbm, key_hbm, value_hbm, time_query_hbm, time_value_hbm, out_hbm)
    copies = {}
    for item in (0, 1, 3, 2, 4, 5):
        copies[item] = pltpu.make_async_copy(sources[item], weights.at[item], sems.at[item])
        copies[item].start()
    times_copy = pltpu.make_async_copy(times_hbm.at[step // 8], times, sems.at[7])
    times_copy.start()
    stride = 2 * side - 1
    heads = groups * slots
    row_lanes = table.shape[1]
    table[...] = jnp.zeros_like(table)
    table[:, : stride * stride] = table_ref[...]
    for head in range(heads):
        row = jnp.broadcast_to(table[head : head + 1, :], (side, row_lanes))
        shifted = pltpu.roll(row, row_lanes - (side - 1), 1, stride=1, stride_axis=0)
        high, low = split_two(shifted)
        wide_high[head * side : (head + 1) * side, :] = high
        wide_low[head * side : (head + 1) * side, :] = low
    span_lanes = windows.shape[2]
    for part in range(span_lanes // LANES):
        first, lanes, squeeze = squeeze_part(part, side, stride)
        span = slice(first, first + lanes)
        narrow = mm(wide_high[:, span], squeeze) + mm(wide_low[:, span], squeeze)
        windows[:, :, part * LANES : (part + 1) * LANES] = narrow.reshape(heads, side, LANES)
    place = place_matrix(relative_ref[0:1, :], side)
    own_copy.wait()
    own = mm(place, own_tokens[...])
    unit, _ = unit_rows(own)
    normed = (unit * first_gain[...] + first_shift[...]).astype(BF16)

    def into_groups(rows, target):
        fill = jnp.zeros((rows.shape[0], target.shape[2] - group_width), rows.dtype)
        for group in range(groups):
            piece = rows[:, group * group_width : (group + 1) * group_width]
            target[group] = jnp.concatenate([piece, fill], axis=1)

    copies[0].wait()
    query = mm(normed, weights[0])
    copies[1].wait()
    into_groups(mm(normed, weights[1]).astype(BF16), key_ref)
    times_copy.wait()
    line = lax.broadcasted_iota(jnp.int32, times.shape, 0)
    chosen = jnp.where(line == step % 8, times[...].astype(F32), 0.0)
    embed = jnp.broadcast_to(jnp.sum(chosen, axis=0, keepdims=True), times.shape)
    embed_ref[...] = embed
    embed = embed.astype(BF16)
    copies[3].wait()
    into_groups((query + mm(embed, weights[3])[0:1]).astype(BF16), query_ref)
    copies[2].wait()
    value = mm(normed, weights[2])
    copies[4].wait()
    into_groups((value + mm(embed, weights[4])[0:1]).astype(BF16), value_ref)

    def one_group(group, carry):
        tiles = [None] * (query_ref.shape[2] // LANES)
        for slot in range(slots):
            head = group * slots + slot
            first, lanes, offset = head_window(slot, head_width)
            mask = head_mask(lanes, offset, head_width)
            window = windows[head]
            blocks = [None] * side
            steps = LANES // side
            for turn in range(steps):
                turned = window
                if turn:
                    turned = pltpu.roll(window, span_lanes - turn * side, 1)
                for jump in range(-(-side // steps)):
                    block = side - 1 - (jump * steps + turn)
                    if block >= 0:
                        blocks[block] = turned[:, jump * LANES : jump * LANES + length]
            bias = jnp.concatenate(blocks, axis=0)
            keys = key_ref[group, :, first : first + lanes]
            queries = query_ref[group, :, first : first + lanes] * mask
            scores = mm_nt(keys, queries) * scale + bias
            weights_now = jnp.exp(scores - jnp.max(scores, axis=0, keepdims=True))
            totals = jnp.sum(weights_now, axis=0, keepdims=True)
            probs = (weights_now * (1.0 / totals)).astype(BF16)
            probs_ref[head] = probs
            values = value_ref[group, :, first : first + lanes] * mask
            add_tiles(tiles, mm_tn(probs, values), first)
        mixed_ref[group] = jnp.concatenate(tiles, axis=1).astype(BF16)
        return carry

    lax.fori_loop(0, groups, one_group, 0)
    for group in range(groups):
        flat[:, group * group_width : (group + 1) * group_width] = mixed_ref[group][:, :group_width]
    copies[5].wait()
    middle = own + mm(flat[...], weights[5]) + out_bias[...]
    middle_ref[...] = middle
    unit, _ = unit_rows(middle)
    normed_ref[...] = (unit * second_gain[...] + second_shift[...]).astype(BF16)


def normed_kernel(side, ranks, relative_ref, tokens_ref, gain, shift, dep, normed_ref):
    unit, _ = unit_rows(mm(place_matrix(relative_ref[0:1, :], side), tokens_ref[...]))
    normed_ref[...] = (unit * gain[...] + shift[...]).astype(BF16)


def gelu_pair(hidden):
    root = math.sqrt(2.0 / math.pi)
    square = hidden * hidden
    bend = jnp.tanh(hidden * (root + (root * 0.044715) * square))
    half = 0.5 + 0.5 * bend
    slope = half + (0.5 * hidden) * (1.0 - bend * bend) * (root + (3.0 * root * 0.044715) * square)
    return hidden * half, slope


def feed_rows(side, relative_ref, normed, cotangent, up_ref, up_bias, down_ref, active, hidden, moved):
    place = place_matrix(relative_ref[0:1, :], side)
    rows = place.shape[0]
    for chunk in range(len(normed)):
        span = slice(chunk * rows, (chunk + 1) * rows)
        turned = mm(place, cotangent[chunk][...]).astype(BF16)
        moved[span, :] = turned
        gelu_out, slope = gelu_pair(mm(normed[chunk][...], up_ref[...]) + up_bias[...])
        active[span, :] = gelu_out.astype(BF16)
        hidden[span, :] = (mm_nt(turned, down_ref[...]) * slope).astype(BF16)


def feed_near_kernel(
    side,
    relative_ref,
    normed_own,
    normed_near,
    cot_own,
    cot_near,
    up_ref,
    up_bias,
    down_ref,
    active,
    hidden,
    moved,
    grad_own,
    grad_near,
):
    feed_rows(
        side,
        relative_ref,
        (normed_own, normed_near),
        (cot_own, cot_near),
        up_ref,
        up_bias,
        down_ref,
        active,
        hidden,
        moved,
    )
    rows = grad_own.shape[0]
    grad_near[...] = mm_nt(hidden[rows:, :], up_ref[...]).astype(BF16)
    grad_own[...] = mm_nt(hidden[:rows, :], up_ref[...]).astype(BF16)


def halves(values, bit):
    half = values.shape[0] // 2
    low, high = values[:half], values[half:]
    return jnp.where(bit == 0, low, high), jnp.where(bit == 0, high, low)


def feed_far_kernel(
    side,
    level,
    ranks,
    relative_ref,
    normed_far,
    normed_last,
    cot_far,
    cot_last,
    up_ref,
    up_bias,
    down_ref,
    near_active,
    near_moved,
    active,
    hidden,
    moved,
    keep_ref,
    send_ref,
):
    feed_rows(
        side,
        relative_ref,
        (normed_far, normed_last),
        (cot_far, cot_last),
        up_ref,
        up_bias,
        down_ref,
        active,
        hidden,
        moved,
    )
    grad = mm_tn(near_active[...], near_moved[...]) + mm_tn(active[...], moved[...])
    keep, send = halves(grad.astype(BF16), (ranks[1] >> level) & 1)
    send_ref[...] = send
    keep_ref[...] = keep


def feed_grad_kernel(hidden, near_hidden, up_ref, grad_far, grad_last, bias_ref):
    rows = grad_far.shape[0]
    grad_last[...] = mm_nt(hidden[rows:, :], up_ref[...]).astype(BF16)
    grad_far[...] = mm_nt(hidden[:rows, :], up_ref[...]).astype(BF16)
    total = jnp.sum(hidden[...].astype(F32), axis=0, keepdims=True)
    total = total + jnp.sum(near_hidden[...].astype(F32), axis=0, keepdims=True)
    bias_ref[...] = jnp.broadcast_to(total, bias_ref.shape)


def up_grad_kernel(level, ranks, own, near, far, last, near_hidden, hidden, keep_ref, send_ref):
    rows = own.shape[0]
    grad = mm_tn(own[...], near_hidden[:rows, :]) + mm_tn(near[...], near_hidden[rows:, :])
    grad = grad + mm_tn(far[...], hidden[:rows, :]) + mm_tn(last[...], hidden[rows:, :])
    keep, send = halves(grad.astype(BF16), (ranks[1] >> level) & 1)
    send_ref[...] = send
    keep_ref[...] = keep


def out_kernel(near_active, active, down_ref, keep_ref, send_ref):
    rows = keep_ref.shape[1]
    keep_ref[0] = mm(near_active[:rows, :], down_ref[...]).astype(BF16)
    send_ref[0] = mm(near_active[rows:, :], down_ref[...]).astype(BF16)
    keep_ref[1] = mm(active[:rows, :], down_ref[...]).astype(BF16)
    send_ref[1] = mm(active[rows:, :], down_ref[...]).astype(BF16)


def add_kernel(left, right, out_ref):
    out_ref[...] = (left[...].astype(F32) + right[...].astype(F32)).astype(out_ref.dtype)


def middle_kernel(
    own_ref,
    near_ref,
    far_ref,
    middle_ref,
    moved_ref,
    gain,
    grad_ref,
    branch_ref,
    sums_ref,
):
    rows = own_ref.shape[0]
    grad_normed = own_ref[...].astype(F32) + near_ref[...].astype(F32) + far_ref[...].astype(F32)
    unit, inverse = unit_rows(middle_ref[...])
    cotangent = moved_ref[:rows, :].astype(F32)
    grad_middle = cotangent + norm_back(grad_normed, unit, inverse, gain[...])
    grad_ref[...] = grad_middle
    branch_ref[...] = grad_middle.astype(BF16)
    sums_ref[...] = jnp.zeros_like(sums_ref)
    sums_ref[0:1, :] = jnp.sum(grad_normed * unit, axis=0, keepdims=True)
    sums_ref[1:2, :] = jnp.sum(grad_normed, axis=0, keepdims=True)
    sums_ref[2:3, :] = jnp.sum(grad_middle, axis=0, keepdims=True)
    sums_ref[3:4, :] = jnp.sum(cotangent, axis=0, keepdims=True)


def attend_back_kernel(
    dims,
    picks,
    ranks,
    query_ref,
    key_ref,
    value_ref,
    probs_ref,
    *refs,
):
    groups, slots, head_width, side, scale = dims
    group_width = slots * head_width
    rank = ranks[0]
    length = side * side
    if len(refs) == 8:
        branch_ref, out_ref, grads, packed_ref, table_ref, grad_mixed, sheared, _ = refs
        fill = jnp.zeros((length, grad_mixed.shape[2] - group_width), BF16)
        product = mm_nt(branch_ref[...], out_ref[...]).astype(BF16)
        for group in range(groups):
            piece = product[:, group * group_width : (group + 1) * group_width]
            grad_mixed[group] = jnp.concatenate([piece, fill], axis=1)
    else:
        grad_mixed, grads, packed_ref, table_ref, sheared, _ = refs
    stride = 2 * side - 1
    span_lanes = sheared.shape[2]
    packed_lanes = packed_ref.shape[2]
    sheared[...] = jnp.zeros_like(sheared)

    def one_group(pick, carry):
        group = (picks[0] + pick) ^ rank
        wide = grad_mixed.shape[2] // LANES
        query_tiles, key_tiles, value_tiles = [None] * wide, [None] * wide, [None] * wide
        for slot in range(slots):
            head = group * slots + slot
            first, lanes, offset = head_window(slot, head_width)
            mask = head_mask(lanes, offset, head_width)
            span = slice(first, first + lanes)
            mixed_now = grad_mixed[group, :, span] * mask
            probs = probs_ref[head]
            grad_probs = mm_nt(value_ref[group, :, span], mixed_now)
            probs_wide = probs.astype(F32)
            weighted = probs_wide * grad_probs
            grad_scores = weighted - probs_wide * jnp.sum(weighted, axis=0, keepdims=True)
            rounded = grad_scores.astype(BF16)
            add_tiles(value_tiles, mm(probs, mixed_now), first)
            add_tiles(key_tiles, mm(rounded, query_ref[group, :, span] * mask), first)
            add_tiles(query_tiles, mm_tn(rounded, key_ref[group, :, span] * mask), first)
            steps = LANES // side
            shear = jnp.zeros((side, span_lanes), F32)
            for turn in range(steps):
                summed = None
                for jump in range(-(-side // steps)):
                    block = side - 1 - (jump * steps + turn)
                    if block >= 0:
                        piece = grad_scores[block * side : (block + 1) * side, :]
                        parts = []
                        if jump:
                            parts.append(jnp.zeros((side, jump * LANES), F32))
                        parts.append(piece)
                        rest = span_lanes - jump * LANES - length
                        if rest:
                            parts.append(jnp.zeros((side, rest), F32))
                        piece = jnp.concatenate(parts, axis=1)
                        summed = piece if summed is None else summed + piece
                shear = shear + (pltpu.roll(summed, turn * side, 1) if turn else summed)
            sheared[:, pl.ds(head, 1), :] = shear[:, None, :]
        query = (jnp.concatenate(query_tiles, axis=1) * scale).astype(BF16)
        key = (jnp.concatenate(key_tiles, axis=1) * scale).astype(BF16)
        value = jnp.concatenate(value_tiles, axis=1).astype(BF16)
        grads[0, pick] = query
        grads[1, pick] = key
        grads[2, pick] = value
        pieces = [query[:, :group_width], key[:, :group_width], value[:, :group_width]]
        if packed_lanes > 3 * group_width:
            pieces.append(jnp.zeros((length, packed_lanes - 3 * group_width), BF16))
        packed_ref[pick] = jnp.concatenate(pieces, axis=1)
        return carry

    lax.fori_loop(0, len(picks), one_group, 0)
    selections = [squeeze_part(part, side, stride) for part in range(span_lanes // LANES)]
    heads = groups * slots
    total = [jnp.zeros((heads, LANES), F32)] * (table_ref.shape[1] // LANES)
    for column in range(side):
        high, low = split_two(sheared[:, :, :][column])
        tiles = [None] * (table_ref.shape[1] // LANES)
        for part, (first, lanes, squeeze) in enumerate(selections):
            span = slice(part * LANES, (part + 1) * LANES)
            add_tiles(tiles, mm_nt(high[:, span], squeeze) + mm_nt(low[:, span], squeeze), first)
        spread = jnp.concatenate(
            [jnp.zeros((heads, LANES), F32) if tile is None else tile for tile in tiles], axis=1
        )
        turn = side - 1 - column
        turned = pltpu.roll(spread, turn, 1) if turn else spread
        total = [
            old + turned[:, place * LANES : (place + 1) * LANES] for place, old in enumerate(total)
        ]
    table_ref[...] = jnp.concatenate(total, axis=1)


def tokens_kernel(
    dims,
    ranks,
    steps_ref,
    near_grads,
    far_grads,
    near_table,
    far_table,
    query_ref,
    key_ref,
    value_ref,
    relative_ref,
    gain,
    middle_ref,
    middle_sums,
    embed_ref,
    tokens_hbm,
    grad_ref,
    image_ref,
    keep_ref,
    send_ref,
    flat,
    own_tokens,
    short,
    sem,
):
    groups, slots, head_width, side, scale = dims
    group_width = slots * head_width
    rank = ranks[0]
    length = side * side
    own_copy = pltpu.make_async_copy(
        tokens_hbm.at[pl.ds(pl.multiple_of(rank * length, length), length)], own_tokens, sem
    )
    own_copy.start()
    for group in range(groups):
        away = group ^ rank
        for item in range(3):
            piece = jnp.where(away >= 2, far_grads[item, away & 1], near_grads[item, away & 1])
            flat[item, :, group * group_width : (group + 1) * group_width] = piece[:, :group_width]
    grad_normed = (
        mm_nt(flat[0], query_ref[...])
        + mm_nt(flat[1], key_ref[...])
        + mm_nt(flat[2], value_ref[...])
    )
    place = place_matrix(relative_ref[0:1, :], side)
    own_copy.wait()
    unit, inverse = unit_rows(mm(place, own_tokens[...]))
    total = middle_ref[...] + norm_back(grad_normed, unit, inverse, gain[...])
    high, low = split_two(total)
    grad_ref[...] = mm_tn(place, high) + mm_tn(place, low)
    image_ref[...] = jnp.zeros_like(image_ref)
    image_ref[0:1, :] = jnp.sum(flat[0].astype(F32), axis=0, keepdims=True)
    image_ref[1:2, :] = jnp.sum(flat[2].astype(F32), axis=0, keepdims=True)
    image_ref[2:3, :] = embed_ref[0:1, :]
    image_ref[3:4, :] = jnp.full((1, image_ref.shape[1]), steps_ref[rank].astype(F32))
    sums = [middle_sums[j : j + 1, :] for j in range(4)]
    sums.append(jnp.sum(grad_normed * unit, axis=0, keepdims=True))
    sums.append(jnp.sum(grad_normed, axis=0, keepdims=True))
    short[...] = jnp.zeros_like(short)
    table = near_table[...] + far_table[...]
    for group in range(groups):
        away = group ^ rank
        short[away, 0:slots, :] = table[group * slots : (group + 1) * slots, :]
        for item, row in enumerate(sums):
            short[away, slots + item : slots + item + 1, :group_width] = row[
                :, group * group_width : (group + 1) * group_width
            ]
    for item in range(groups // 2):
        keep_ref[item] = short[2 * item]
        send_ref[item] = short[2 * item + 1]


def weights_kernel(
    dims, level, ranks, normed, pack0, pack1, pack2, pack3, branch0, branch1, branch2, branch3,
    mixed0, mixed1, mixed2, mixed3, keep_first, keep_second, send_first, send_second,
    packed, branch, mixed,
):
    groups, slots, head_width, side, scale = dims
    group_width = slots * head_width
    rows = side * side
    for chunk, refs in enumerate(
        ((pack0, branch0, mixed0), (pack1, branch1, mixed1), (pack2, branch2, mixed2), (pack3, branch3, mixed3))
    ):
        span = slice(chunk * rows, (chunk + 1) * rows)
        packed[span, :] = refs[0][...]
        branch[span, :] = refs[1][...]
        mixed[span, :] = refs[2][...]
    bit = (ranks[1] >> level) & 1
    left = mm_tn(packed[...], normed[...]).astype(BF16)
    right = mm_tn(mixed[...], branch[...]).astype(BF16)
    keep_first[...], send_first[...] = halves(left[: 2 * group_width], bit)
    value, out = left[2 * group_width : 3 * group_width], right[:group_width]
    keep_second[...] = jnp.where(bit == 0, value, out)
    send_second[...] = jnp.where(bit == 0, out, value)


def split_kernel(level, ranks, kept, got, keep_ref, send_ref):
    total = (kept[...].astype(F32) + got[...].astype(F32)).astype(BF16)
    keep, send = halves(total, (ranks[1] >> level) & 1)
    send_ref[...] = send
    keep_ref[...] = keep


def join_kernel(level, ranks, own, other, out_ref):
    half = own.shape[0]
    bit = (ranks[1] >> level) & 1
    out_ref[:half, :] = jnp.where(bit == 0, own[...], other[...])
    out_ref[half:, :] = jnp.where(bit == 0, other[...], own[...])


def widen_kernel(level, ranks, own, other, out_ref):
    bit = (ranks[1] >> level) & 1
    first = (pl.program_id(0) < pl.num_programs(0) // 2) == (bit == 0)

    @pl.when(first)
    def _():
        out_ref[...] = own[...].astype(F32)

    @pl.when(jnp.logical_not(first))
    def _():
        out_ref[...] = other[...].astype(F32)


def widen_pair_kernel(level, ranks, own, other, low_ref, high_ref):
    bit = (ranks[1] >> level) & 1
    low_ref[...] = jnp.where(bit == 0, own[...], other[...]).astype(F32)
    high_ref[...] = jnp.where(bit == 0, other[...], own[...]).astype(F32)


def block_kernel(side, relative_ref, own, near, far, middle_ref, bias, out_ref):
    total = own[0].astype(F32) + near[0].astype(F32) + far[...].astype(F32)
    total = (middle_ref[...] + total + bias[...]).astype(BF16)
    place = place_matrix(relative_ref[0:1, :], side)
    out_ref[...] = mm_tn(place, total).astype(BF16)


def shape_of(*sizes, dtype=BF16):
    return jax.ShapeDtypeStruct(sizes, dtype)


VMEM = pl.BlockSpec(memory_space=pltpu.VMEM)
HBM = pl.BlockSpec(memory_space=pl.ANY)
SMEM = pl.BlockSpec(memory_space=pltpu.SMEM)
MIB = 1024 * 1024


def run(kernel, outs, inputs, specs=None, scratch=(), deps=(), vmem=32):
    specs = [VMEM] * len(inputs) if specs is None else list(specs)
    count = len(inputs)

    def body(*refs):
        kernel(*refs[:count], *refs[count + len(deps) :])

    return pl.pallas_call(
        body,
        out_shape=outs,
        in_specs=specs + [HBM] * len(deps),
        out_specs=jax.tree.map(lambda _: VMEM, outs),
        scratch_shapes=list(scratch),
        compiler_params=pltpu.CompilerParams(vmem_limit_bytes=vmem * MIB),
        cost_estimate=pl.CostEstimate(flops=1000, bytes_accessed=1000, transcendentals=0),
    )(*inputs, *deps)


def widen(ranks, level, own, other):
    half, columns = own.shape
    parts = 2
    block = half // parts

    def own_map(i, me):
        bit = (me[1] >> level) & 1
        return (jnp.clip(i - parts * bit, 0, parts - 1), 0)

    def other_map(i, me):
        bit = (me[1] >> level) & 1
        return (jnp.clip(i - parts * (1 - bit), 0, parts - 1), 0)

    return pl.pallas_call(
        partial(widen_kernel, level),
        out_shape=shape_of(2 * half, columns, dtype=F32),
        grid_spec=pltpu.PrefetchScalarGridSpec(
            num_scalar_prefetch=1,
            grid=(2 * parts,),
            in_specs=[
                pl.BlockSpec((block, columns), own_map),
                pl.BlockSpec((block, columns), other_map),
            ],
            out_specs=pl.BlockSpec((block, columns), lambda i, me: (i, 0)),
        ),
        cost_estimate=pl.CostEstimate(flops=1000, bytes_accessed=1000, transcendentals=0),
    )(ranks, own, other)


def swap(array, axis, distance):
    size = lax.axis_size(axis)
    return lax.ppermute(array, axis, [(i, i ^ distance) for i in range(size)])


class Total:
    def __init__(self, ranks, order, keep, send):
        self.ranks, self.order = ranks, order
        self.keep = keep
        self.got = self.swap(0, send)

    def swap(self, place, array):
        return swap(array, "dp", 1 << self.order[place])

    def split(self, deps=()):
        half, columns = self.keep.shape
        part = shape_of(half // 2, columns)
        self.keep, send = run(
            partial(split_kernel, self.order[1]),
            [part, part],
            [self.ranks, self.keep, self.got],
            [SMEM, VMEM, VMEM],
            deps=deps,
            vmem=16,
        )
        self.got = self.swap(1, send)
        return self.keep

    def add(self, place, deps=()):
        self.keep = run(
            add_kernel,
            shape_of(*self.keep.shape),
            [self.keep, self.got],
            deps=deps,
            vmem=16,
        )
        self.got = self.swap(place, self.keep)
        return self.keep

    def join(self, deps=()):
        half, columns = self.keep.shape
        self.keep = run(
            partial(join_kernel, self.order[1]),
            shape_of(2 * half, columns),
            [self.ranks, self.keep, self.got],
            [SMEM, VMEM, VMEM],
            deps=deps,
            vmem=16,
        )
        self.got = self.swap(0, self.keep)
        return self.keep

    def advance(self, stage, deps=()):
        levels = len(self.order)
        if stage == 0:
            return self.split(deps)
        if stage < levels - 1:
            return self.add(stage + 1, deps)
        if stage == levels - 1:
            return self.add(1, deps)
        return self.join(deps)


def add_low(left, right):
    return (left.astype(F32) + right.astype(F32)).astype(BF16)


def on_device(
    tokens,
    timesteps,
    relative_index,
    time_table,
    query_weight,
    key_weight,
    value_weight,
    time_query_weight,
    time_value_weight,
    out_weight,
    out_bias,
    first_gain,
    first_shift,
    second_gain,
    second_shift,
    up_weight,
    up_bias,
    down_weight,
    down_bias,
    bias_table,
    cotangent,
):
    length = relative_index.shape[0]
    width = tokens.shape[1]
    heads = bias_table.shape[1]
    head_width = width // heads
    side = math.isqrt(length)
    stride = 2 * side - 1
    groups = lax.axis_size("mp")
    dp_size = lax.axis_size("dp")
    rank = lax.axis_index("mp")
    ranks = jnp.stack([rank, lax.axis_index("dp")]).astype(jnp.int32)
    slots = heads // groups
    group_width = slots * head_width
    group_lanes = round_up(group_width, LANES)
    packed_lanes = round_up(3 * group_width, LANES)
    table_lanes = round_up(stride * stride, LANES)
    span_lanes = round_up(stride * side, LANES)
    hidden_width = up_weight.shape[1]
    rows = groups * length
    dims = (groups, slots, head_width, side, head_width ** (-0.5))
    line = lambda vector: vector.reshape(1, -1)
    first_rows = VMEM
    levels = list(range(dp_size.bit_length() - 1))
    other_order = levels[1::-1] + levels[2:]

    def grouped(count=groups):
        return shape_of(count, length, group_lanes)

    cot_near = swap(cotangent, "mp", 1)
    cot_far = swap(cotangent, "mp", 2)
    steps = time_table.shape[0]
    outs = run(
        partial(attend_kernel, dims),
        [
            grouped(),
            grouped(),
            grouped(),
            shape_of(heads, length, length),
            grouped(),
            shape_of(length, width, dtype=F32),
            shape_of(length, width),
            shape_of(8, width, dtype=F32),
        ],
        [
            ranks,
            timesteps,
            relative_index,
            bias_table.T,
            line(first_gain),
            line(first_shift),
            line(second_gain),
            line(second_shift),
            line(out_bias),
            tokens,
            time_table.reshape(steps // 8, 8, width),
            query_weight,
            key_weight,
            value_weight,
            time_query_weight,
            time_value_weight,
            out_weight,
        ],
        [SMEM, SMEM, first_rows] + [VMEM] * 6 + [HBM] * 8,
        [
            pltpu.VMEM((6, width, width), BF16),
            pltpu.VMEM((length, width), BF16),
            pltpu.VMEM((8, width), BF16),
            pltpu.VMEM((heads, table_lanes), F32),
            pltpu.VMEM((heads * side, table_lanes), BF16),
            pltpu.VMEM((heads * side, table_lanes), BF16),
            pltpu.VMEM((heads, side, span_lanes), F32),
            pltpu.VMEM((length, width), BF16),
            pltpu.SemaphoreType.DMA((8,)),
        ],
        vmem=48,
    )
    query_rows, key_rows, value_rows, probs, mixed, middle, normed_own, embed = outs
    normed_near = swap(normed_own, "mp", 1)
    normed_far = swap(normed_own, "mp", 2)

    normed_first = pl.pallas_call(
        partial(normed_kernel, side),
        out_shape=shape_of(rows, width),
        grid_spec=pltpu.PrefetchScalarGridSpec(
            num_scalar_prefetch=1,
            grid=(groups,),
            in_specs=[
                pl.BlockSpec((8, length), lambda i, me: (0, 0)),
                pl.BlockSpec((length, width), lambda i, me: (i ^ me[0], 0)),
                pl.BlockSpec((1, width), lambda i, me: (0, 0)),
                pl.BlockSpec((1, width), lambda i, me: (0, 0)),
                HBM,
            ],
            out_specs=pl.BlockSpec((length, width), lambda i, me: (i, 0)),
        ),
        cost_estimate=pl.CostEstimate(flops=1000, bytes_accessed=1000, transcendentals=0),
    )(ranks, relative_index, tokens, line(first_gain), line(first_shift), normed_own)

    pair = shape_of(2 * length, width)
    hidden_pair = shape_of(2 * length, hidden_width)
    chunk = shape_of(length, width)
    near_active, near_hidden, near_moved, grad_own, grad_near = run(
        partial(feed_near_kernel, side),
        [hidden_pair, hidden_pair, pair, chunk, chunk],
        [
            relative_index,
            normed_own,
            normed_near,
            cotangent,
            cot_near,
            up_weight,
            line(up_bias),
            down_weight,
        ],
        [first_rows] + [VMEM] * 7,
        deps=[normed_first],
    )
    near_got = swap(grad_near, "mp", 1)
    normed_last = swap(normed_far, "mp", 1)
    cot_last = swap(cot_far, "mp", 1)
    half = shape_of(hidden_width // 2, width)
    active, hidden, moved, keep, send = run(
        partial(feed_far_kernel, side, levels[0]),
        [hidden_pair, hidden_pair, pair, half, half],
        [
            ranks,
            relative_index,
            normed_far,
            normed_last,
            cot_far,
            cot_last,
            up_weight,
            line(up_bias),
            down_weight,
            near_active,
            near_moved,
        ],
        [SMEM, first_rows] + [VMEM] * 9,
    )
    down = Total(ranks, levels, keep, send)
    grad_far, grad_last, up_bias_sum = run(
        feed_grad_kernel,
        [chunk, chunk, shape_of(8, hidden_width, dtype=F32)],
        [hidden, near_hidden, up_weight],
        deps=[keep],
    )
    last_got = swap(grad_last, "mp", 1)
    half = shape_of(width // 2, hidden_width)
    keep, send = run(
        partial(up_grad_kernel, other_order[0]),
        [half, half],
        [ranks, normed_own, normed_near, normed_far, normed_last, near_hidden, hidden],
        [SMEM] + [VMEM] * 6,
        deps=[up_bias_sum],
    )
    up = Total(ranks, other_order, keep, send)
    grad_sent = run(add_kernel, chunk, [grad_far, last_got], deps=[keep], vmem=16)
    far_got = swap(grad_sent, "mp", 2)
    chunks = shape_of(2, length, width)
    out_keep, out_send = run(
        out_kernel, [chunks, chunks], [near_active, active, down_weight], deps=[grad_sent]
    )
    grad_middle, grad_branch, middle_sums = run(
        middle_kernel,
        [shape_of(length, width, dtype=F32), chunk, shape_of(8, width, dtype=F32)],
        [grad_own, near_got, far_got, middle, near_moved, line(second_gain)],
        deps=[out_keep],
        vmem=16,
    )
    branch_near = swap(grad_branch, "mp", 1)
    branch_far = swap(grad_branch, "mp", 2)
    last = down.advance(0, deps=[middle_sums])

    table_shape = shape_of(heads, table_lanes, dtype=F32)
    back_scratch = [
        pltpu.VMEM((side, heads, span_lanes), F32),
        pltpu.SemaphoreType.DMA,
    ]
    grads_shape = shape_of(3, 2, length, group_lanes)
    packed_shape = shape_of(2, length, packed_lanes)
    heads_in = [ranks, query_rows, key_rows, value_rows, probs]
    far_grads, far_packed, far_table, grad_mixed = run(
        partial(attend_back_kernel, dims, (2, 3)),
        [grads_shape, packed_shape, table_shape, grouped()],
        heads_in + [grad_branch, out_weight],
        [SMEM] + [VMEM] * 6,
        back_scratch,
        deps=[last],
    )
    packed_2 = swap(far_packed[0], "mp", 2)
    packed_3 = swap(far_packed[1], "mp", 3)
    last = up.advance(0, deps=[far_table])
    near_grads, near_packed, near_table = run(
        partial(attend_back_kernel, dims, (0, 1)),
        [grads_shape, packed_shape, table_shape],
        heads_in + [grad_mixed],
        [SMEM] + [VMEM] * 5,
        back_scratch,
        deps=[last],
    )
    packed_1 = swap(near_packed[1], "mp", 1)
    last = down.advance(1, deps=[near_table])
    branch_last = swap(branch_far, "mp", 1)
    short_shape = shape_of(groups // 2, 16, table_lanes, dtype=F32)
    tokens_grad, image_rows, short_keep, short_send = run(
        partial(tokens_kernel, dims),
        [
            shape_of(length, width, dtype=F32),
            shape_of(8, width, dtype=F32),
            short_shape,
            short_shape,
        ],
        [
            ranks,
            timesteps,
            near_grads,
            far_grads,
            near_table,
            far_table,
            query_weight,
            key_weight,
            value_weight,
            relative_index,
            line(first_gain),
            grad_middle,
            middle_sums,
            embed,
            tokens,
        ],
        [SMEM, SMEM] + [VMEM] * 7 + [first_rows] + [VMEM] * 4 + [HBM],
        [
            pltpu.VMEM((3, length, width), BF16),
            pltpu.VMEM((length, width), BF16),
            pltpu.VMEM((groups, 16, table_lanes), F32),
            pltpu.SemaphoreType.DMA,
        ],
        deps=[last],
    )
    image_all = lax.all_gather(image_rows, ("dp", "mp"), axis=0, tiled=True)
    last = up.advance(1, deps=[image_rows])

    mixed_all = [lax.dynamic_index_in_dim(mixed, rank, 0, keepdims=False)]
    for away in range(1, groups):
        turned = lax.dynamic_index_in_dim(mixed, rank ^ away, 0, keepdims=False)
        mixed_all.append(swap(turned, "mp", away))
    half = shape_of(group_width, width)
    keep_first, keep_second, send_first, send_second = run(
        partial(weights_kernel, dims, levels[0]),
        [half] * 4,
        [ranks, normed_first, near_packed[0], packed_1, packed_2, packed_3]
        + [grad_branch, branch_near, branch_far, branch_last]
        + mixed_all,
        [SMEM] + [VMEM] * 13,
        [
            pltpu.VMEM((rows, packed_lanes), BF16),
            pltpu.VMEM((rows, width), BF16),
            pltpu.VMEM((rows, group_lanes), BF16),
        ],
        deps=[last],
    )
    first = Total(ranks, levels, keep_first, send_first)
    second = Total(ranks, levels, keep_second, send_second)
    last = keep_second

    short_got = swap(short_send, "mp", 1)
    out_got = swap(out_send, "mp", 1)
    short = short_keep + short_got
    out_far = swap(add_low(out_keep[1], out_got[1]), "mp", 2)
    short = short[0] + swap(short[1], "mp", 2)
    up_bias_rows = jnp.pad(up_bias_sum[0], (0, 2 * table_lanes - hidden_width))
    short = jnp.concatenate([short[:14], up_bias_rows.reshape(2, table_lanes)], axis=0)
    for level in levels:
        short = short + swap(short, "dp", 1 << level)

    stages = len(levels) + 1
    todo = [(down, 2), (first, 0), (second, 0), (up, 2)]
    for stage in range(3, stages):
        todo += [(down, stage)]
    todo += [(first, 1), (second, 1)]
    for stage in range(3, stages):
        todo += [(up, stage)]
    for stage in range(2, stages):
        todo += [(first, stage), (second, stage)]
    for total, stage in todo:
        last = total.advance(stage, deps=[last])
    down_grad = widen(ranks, levels[0], down.keep, down.got)
    up_grad = widen(ranks, other_order[0], up.keep, up.got)
    wide = shape_of(group_width, width, dtype=F32)
    query_grad, key_grad = run(
        partial(widen_pair_kernel, levels[0]),
        [wide, wide],
        [ranks, first.keep, first.got],
        [SMEM, VMEM, VMEM],
        vmem=16,
    )
    value_grad, out_grad = run(
        partial(widen_pair_kernel, levels[0]),
        [wide, wide],
        [ranks, second.keep, second.got],
        [SMEM, VMEM, VMEM],
        vmem=16,
    )

    image_all = image_all.reshape(-1, 8, width)
    query_sums, value_sums, embed_all = image_all[:, 0], image_all[:, 1], image_all[:, 2]
    steps_all = image_all[:, 3, 0].astype(jnp.int32)

    def own_block(array, axis_number):
        extent = array.shape[axis_number] // groups
        return lax.dynamic_slice_in_dim(array, rank * extent, extent, axis_number)

    contract_first = (((0,), (0,)), ((), ()))
    contract_last = (((1,), (1,)), ((), ()))
    time_query_grad = lax.dot_general(
        embed_all, own_block(query_sums, 1), contract_first, precision=HIGHEST
    )
    time_value_grad = lax.dot_general(
        embed_all, own_block(value_sums, 1), contract_first, precision=HIGHEST
    )
    grad_embed = lax.dot_general(
        query_sums, own_block(time_query_weight, 0).astype(F32), contract_last, precision=HIGHEST
    ) + lax.dot_general(
        value_sums, own_block(time_value_weight, 0).astype(F32), contract_last, precision=HIGHEST
    )
    onehot = jnp.arange(time_table.shape[0], dtype=jnp.int32)[:, None] == steps_all[None, :]
    time_table_grad = jnp.dot(onehot.astype(F32), grad_embed, precision=HIGHEST)

    parts = [short[slots + j, :group_width] for j in range(6)]
    second_gain_grad, second_shift_grad, out_bias_grad, down_bias_grad = parts[:4]
    first_gain_grad, first_shift_grad = parts[4:]
    bias_table_grad = short[:slots, : stride * stride].T
    up_bias_grad = short[14:].reshape(-1)[:hidden_width]

    block_out = run(
        partial(block_kernel, side),
        shape_of(length, width),
        [relative_index, out_keep, out_got, out_far, middle, line(down_bias)],
        [first_rows] + [VMEM] * 5,
        vmem=16,
    )
    return (
        block_out,
        tokens_grad,
        time_table_grad,
        query_grad.T,
        key_grad.T,
        value_grad.T,
        time_query_grad,
        time_value_grad,
        out_grad,
        out_bias_grad,
        first_gain_grad,
        first_shift_grad,
        second_gain_grad,
        second_shift_grad,
        up_grad,
        up_bias_grad,
        down_grad,
        down_bias_grad,
        bias_table_grad,
    )


def solution(mesh):
    whole = P()
    rows = P(("dp", "mp"), None)
    columns = P(None, "mp")
    split = P("mp")
    placed = (
        (P("dp", None), P("dp"))
        + (whole,) * 13
        + (columns, split, P("mp", None), whole, whole, rows)
    )
    return jax.shard_map(
        on_device,
        mesh=mesh,
        in_specs=placed,
        out_specs=(rows, rows)
        + (columns,) * 6
        + (P("mp", None),)
        + (split,) * 5
        + (columns, split, P("mp", None), split, columns),
        check_vma=False,
    )
```

```python
import math
from functools import partial

import jax
import jax.numpy as jnp
from jax import lax
from jax.experimental import pallas as pl
from jax.experimental.pallas import tpu as pltpu
from jax.sharding import PartitionSpec as P

EPSILON = 1e-06
HIGHEST = lax.Precision.HIGHEST
F32 = jnp.float32
BF16 = jnp.bfloat16
LANES = 128


def mm(left, right):
    return lax.dot_general(left, right, (((1,), (0,)), ((), ())), preferred_element_type=F32)


def mm_nt(left, right):
    return lax.dot_general(left, right, (((1,), (1,)), ((), ())), preferred_element_type=F32)


def mm_tn(left, right):
    return lax.dot_general(left, right, (((0,), (0,)), ((), ())), preferred_element_type=F32)


def round_up(value, step):
    return -(-value // step) * step


def head_window(slot, head_width):
    first = slot * head_width // LANES * LANES
    last = round_up((slot + 1) * head_width, LANES)
    return first, last - first, slot * head_width - first


def head_mask(lanes, offset, head_width):
    lane = lax.broadcasted_iota(jnp.int32, (1, lanes), 1)
    return jnp.where((lane >= offset) & (lane < offset + head_width), 1.0, 0.0).astype(BF16)


def unit_rows(values):
    centred = values - jnp.mean(values, axis=-1, keepdims=True)
    inverse = lax.rsqrt(jnp.mean(centred * centred, axis=-1, keepdims=True) + EPSILON)
    return centred * inverse, inverse


def norm_back(grad_out, unit, inverse, gain_row):
    grad_unit = grad_out * gain_row
    first_mean = jnp.mean(grad_unit, axis=-1, keepdims=True)
    second_mean = jnp.mean(grad_unit * unit, axis=-1, keepdims=True)
    return inverse * (grad_unit - first_mean - unit * second_mean)


def add_tiles(tiles, product, first):
    for part in range(product.shape[1] // LANES):
        place = first // LANES + part
        piece = product[:, part * LANES : (part + 1) * LANES]
        tiles[place] = piece if tiles[place] is None else tiles[place] + piece


def squeeze_part(part, side, stride):
    each = LANES // side
    first = part * each * stride // LANES * LANES
    last = round_up((part * each + each - 1) * stride + side, LANES)
    wide = lax.broadcasted_iota(jnp.int32, (last - first, LANES), 0) + first
    close = lax.broadcasted_iota(jnp.int32, (last - first, LANES), 1)
    same = wide == (part * each + close // side) * stride + close % side
    return first, last - first, jnp.where(same, 1.0, 0.0).astype(BF16)


def place_matrix(relative_row, side):
    stride = 2 * side - 1
    entry = relative_row.astype(F32)
    row_part = jnp.floor((entry + 0.5) * (1.0 / stride))
    column_part = entry - row_part * stride
    row_part = jnp.max(row_part, axis=1, keepdims=True) - row_part
    column_part = jnp.max(column_part, axis=1, keepdims=True) - column_part
    cells = (row_part * side + column_part).astype(jnp.int32)
    length = side * side
    cell = lax.broadcasted_iota(jnp.int32, (length, length), 0)
    return jnp.where(cell == cells, 1.0, 0.0).astype(BF16)


def split_two(values):
    high = values.astype(BF16)
    return high, (values - high.astype(F32)).astype(BF16)


def attend_kernel(
    dims,
    ranks,
    steps_ref,
    relative_ref,
    table_ref,
    params,
    tokens_hbm,
    times_hbm,
    query_hbm,
    key_hbm,
    value_hbm,
    time_query_hbm,
    time_value_hbm,
    out_hbm,
    query_ref,
    key_ref,
    value_ref,
    probs_ref,
    mixed_0,
    mixed_1,
    mixed_2,
    mixed_3,
    middle_ref,
    normed_ref,
    embed_ref,
    weights,
    own_tokens,
    times,
    table,
    wide_high,
    wide_low,
    windows,
    flat,
    mixed_ref,
    sems,
):
    groups, slots, head_width, side, scale = dims
    group_width = slots * head_width
    rank = ranks[0]
    length = side * side
    step = steps_ref[rank]
    own_copy = pltpu.make_async_copy(
        tokens_hbm.at[pl.ds(pl.multiple_of(rank * length, length), length)], own_tokens, sems.at[6]
    )
    own_copy.start()
    sources = (query_hbm, key_hbm, value_hbm, time_query_hbm, time_value_hbm, out_hbm)
    copies = {}
    for item in (0, 1, 3, 2, 4, 5):
        copies[item] = pltpu.make_async_copy(sources[item], weights.at[item], sems.at[item])
        copies[item].start()
    times_copy = pltpu.make_async_copy(times_hbm.at[step // 8], times, sems.at[7])
    times_copy.start()
    stride = 2 * side - 1
    heads = groups * slots
    row_lanes = table.shape[1]
    table[...] = jnp.zeros_like(table)
    table[:, : stride * stride] = table_ref[...]
    for head in range(heads):
        row = jnp.broadcast_to(table[head : head + 1, :], (side, row_lanes))
        shifted = pltpu.roll(row, row_lanes - (side - 1), 1, stride=1, stride_axis=0)
        high, low = split_two(shifted)
        wide_high[head * side : (head + 1) * side, :] = high
        wide_low[head * side : (head + 1) * side, :] = low
    span_lanes = windows.shape[2]
    for part in range(span_lanes // LANES):
        first, lanes, squeeze = squeeze_part(part, side, stride)
        span = slice(first, first + lanes)
        narrow = mm(wide_high[:, span], squeeze) + mm(wide_low[:, span], squeeze)
        windows[:, :, part * LANES : (part + 1) * LANES] = narrow.reshape(heads, side, LANES)
    place = place_matrix(relative_ref[0:1, :], side)
    own_copy.wait()
    own = mm(place, own_tokens[...])
    unit, _ = unit_rows(own)
    normed = (unit * params[0:1, :] + params[1:2, :]).astype(BF16)

    def into_groups(rows, target):
        fill = jnp.zeros((rows.shape[0], target.shape[2] - group_width), rows.dtype)
        for group in range(groups):
            piece = rows[:, group * group_width : (group + 1) * group_width]
            target[group] = jnp.concatenate([piece, fill], axis=1)

    copies[0].wait()
    query = mm(normed, weights[0])
    copies[1].wait()
    into_groups(mm(normed, weights[1]).astype(BF16), key_ref)
    key_ref.send()
    times_copy.wait()
    line = lax.broadcasted_iota(jnp.int32, times.shape, 0)
    chosen = jnp.where(line == step % 8, times[...].astype(F32), 0.0)
    embed = jnp.broadcast_to(jnp.sum(chosen, axis=0, keepdims=True), times.shape)
    embed_ref[...] = embed
    embed = embed.astype(BF16)
    copies[3].wait()
    into_groups((query + mm(embed, weights[3])[0:1]).astype(BF16), query_ref)
    query_ref.send()
    copies[2].wait()
    value = mm(normed, weights[2])
    copies[4].wait()
    into_groups((value + mm(embed, weights[4])[0:1]).astype(BF16), value_ref)
    value_ref.send()

    def one_group(group, carry):
        tiles = [None] * (query_ref.shape[2] // LANES)
        for slot in range(slots):
            head = group * slots + slot
            first, lanes, offset = head_window(slot, head_width)
            mask = head_mask(lanes, offset, head_width)
            window = windows[head]
            blocks = [None] * side
            steps = LANES // side
            for turn in range(steps):
                turned = window
                if turn:
                    turned = pltpu.roll(window, span_lanes - turn * side, 1)
                for jump in range(-(-side // steps)):
                    block = side - 1 - (jump * steps + turn)
                    if block >= 0:
                        blocks[block] = turned[:, jump * LANES : jump * LANES + length]
            bias = jnp.concatenate(blocks, axis=0)
            keys = key_ref[group, :, first : first + lanes]
            queries = query_ref[group, :, first : first + lanes] * mask
            scores = mm_nt(keys, queries) * scale + bias
            weights_now = jnp.exp(scores - jnp.max(scores, axis=0, keepdims=True))
            totals = jnp.sum(weights_now, axis=0, keepdims=True)
            probs = (weights_now * (1.0 / totals)).astype(BF16)
            probs_ref[head] = probs
            values = value_ref[group, :, first : first + lanes] * mask
            add_tiles(tiles, mm_tn(probs, values), first)
        mixed_ref[group] = jnp.concatenate(tiles, axis=1).astype(BF16)
        return carry

    lax.fori_loop(0, groups, one_group, 0)
    probs_ref.send()
    for group in range(groups):
        flat[:, group * group_width : (group + 1) * group_width] = mixed_ref[group][:, :group_width]
    for away, target in enumerate((mixed_0, mixed_1, mixed_2, mixed_3)):
        target[...] = mixed_ref[rank ^ away]
        target.send()
    copies[5].wait()
    middle = own + mm(flat[...], weights[5]) + params[4:5, :]
    middle_ref[...] = middle
    middle_ref.send()
    unit, _ = unit_rows(middle)
    normed_ref[...] = (unit * params[2:3, :] + params[3:4, :]).astype(BF16)


def normed_kernel(side, ranks, relative_ref, tokens_ref, params, dep, other, normed_ref):
    unit, _ = unit_rows(mm(place_matrix(relative_ref[0:1, :], side), tokens_ref[...]))
    normed_ref[...] = (unit * params[0:1, :] + params[1:2, :]).astype(BF16)


def gelu_pair(hidden):
    root = math.sqrt(2.0 / math.pi)
    square = hidden * hidden
    bend = jnp.tanh(hidden * (root + (root * 0.044715) * square))
    half = 0.5 + 0.5 * bend
    slope = half + (0.5 * hidden) * (1.0 - bend * bend) * (root + (3.0 * root * 0.044715) * square)
    return hidden * half, slope


def feed_rows(side, relative_ref, normed, cotangent, up_ref, up_bias, down_ref, active, hidden, moved):
    place = place_matrix(relative_ref[0:1, :], side)
    rows = place.shape[0]
    for chunk in range(len(normed)):
        span = slice(chunk * rows, (chunk + 1) * rows)
        turned = mm(place, cotangent[chunk][...]).astype(BF16)
        moved[span, :] = turned
        gelu_out, slope = gelu_pair(mm(normed[chunk][...], up_ref[...]) + up_bias[...])
        active[span, :] = gelu_out.astype(BF16)
        hidden[span, :] = (mm_nt(turned, down_ref[...]) * slope).astype(BF16)


def feed_near_kernel(
    side,
    relative_ref,
    normed_own,
    normed_near,
    cot_own,
    cot_near,
    up_ref,
    up_bias,
    down_ref,
    active,
    hidden,
    moved,
    grad_own,
    grad_near,
):
    feed_rows(
        side,
        relative_ref,
        (normed_own, normed_near),
        (cot_own, cot_near),
        up_ref,
        up_bias,
        down_ref,
        active,
        hidden,
        moved,
    )
    active.send()
    moved.send()
    hidden.send()
    rows = grad_own.shape[0]
    grad_near[...] = mm_nt(hidden[rows:, :], up_ref[...]).astype(BF16)
    grad_near.send()
    grad_own[...] = mm_nt(hidden[:rows, :], up_ref[...]).astype(BF16)


def halves(values, bit):
    half = values.shape[0] // 2
    low, high = values[:half], values[half:]
    return jnp.where(bit == 0, low, high), jnp.where(bit == 0, high, low)


def feed_far_kernel(
    side,
    relative_ref,
    normed_far,
    normed_last,
    cot_far,
    cot_last,
    up_ref,
    up_bias,
    down_ref,
    near_hidden,
    active,
    hidden,
    moved,
    grad_far,
    grad_last,
    bias_ref,
):
    feed_rows(
        side,
        relative_ref,
        (normed_far, normed_last),
        (cot_far, cot_last),
        up_ref,
        up_bias,
        down_ref,
        active,
        hidden,
        moved,
    )
    rows = grad_far.shape[0]
    grad_last[...] = mm_nt(hidden[rows:, :], up_ref[...]).astype(BF16)
    grad_far[...] = mm_nt(hidden[:rows, :], up_ref[...]).astype(BF16)
    total = jnp.sum(hidden[...].astype(F32), axis=0, keepdims=True)
    total = total + jnp.sum(near_hidden[...].astype(F32), axis=0, keepdims=True)
    bias_ref[...] = jnp.broadcast_to(total, bias_ref.shape)


def down_grad_kernel(level, ranks, near_active, near_moved, active, moved, keep_ref, send_ref):
    grad = mm_tn(near_active[...], near_moved[...]) + mm_tn(active[...], moved[...])
    keep, send = halves(grad.astype(BF16), (ranks[1] >> level) & 1)
    send_ref[...] = send
    keep_ref[...] = keep


def up_grad_kernel(
    level, ranks, own, near, far, last, near_hidden, hidden, keep_ref, send_ref, normed
):
    rows = own.shape[0]
    for chunk, ref in enumerate((own, near, far, last)):
        normed[chunk * rows : (chunk + 1) * rows, :] = ref[...]
    grad = mm_tn(normed[: 2 * rows, :], near_hidden[...]) + mm_tn(normed[2 * rows :, :], hidden[...])
    keep, send = halves(grad.astype(BF16), (ranks[1] >> level) & 1)
    send_ref[...] = send
    send_ref.send()
    keep_ref[...] = keep


def out_kernel(near_active, active, down_ref, keep_ref, send_ref):
    rows = keep_ref.shape[1]
    keep_ref[0] = mm(near_active[:rows, :], down_ref[...]).astype(BF16)
    send_ref[0] = mm(near_active[rows:, :], down_ref[...]).astype(BF16)
    keep_ref[1] = mm(active[:rows, :], down_ref[...]).astype(BF16)
    send_ref[1] = mm(active[rows:, :], down_ref[...]).astype(BF16)


def add_kernel(left, right, out_ref):
    out_ref[...] = (left[...].astype(F32) + right[...].astype(F32)).astype(out_ref.dtype)


def middle_kernel(
    own_ref,
    near_ref,
    far_ref,
    middle_ref,
    moved_ref,
    params,
    branch_ref,
    grad_ref,
    sums_ref,
):
    rows = own_ref.shape[0]
    grad_normed = own_ref[...].astype(F32) + near_ref[...].astype(F32) + far_ref[...].astype(F32)
    unit, inverse = unit_rows(middle_ref[...])
    cotangent = moved_ref[:rows, :].astype(F32)
    grad_middle = cotangent + norm_back(grad_normed, unit, inverse, params[2:3, :])
    branch_ref[...] = grad_middle.astype(BF16)
    branch_ref.send()
    grad_ref[...] = grad_middle
    grad_ref.send()
    sums_ref[...] = jnp.zeros(sums_ref.shape, F32)
    sums_ref[0:1, :] = jnp.sum(grad_normed * unit, axis=0, keepdims=True)
    sums_ref[1:2, :] = jnp.sum(grad_normed, axis=0, keepdims=True)
    sums_ref[2:3, :] = jnp.sum(grad_middle, axis=0, keepdims=True)
    sums_ref[3:4, :] = jnp.sum(cotangent, axis=0, keepdims=True)


def attend_back_kernel(
    dims,
    picks,
    ranks,
    *refs,
):
    groups, slots, head_width, side, scale = dims
    group_width = slots * head_width
    rank = ranks[0]
    length = side * side
    if len(refs) == 11:
        branch_ref, out_ref, query_ref, key_ref, value_ref, probs_ref = refs[:6]
        packed_a, packed_b, grads, grad_mixed, sheared = refs[6:]
        fill = jnp.zeros((length, grad_mixed.shape[2] - group_width), BF16)
        product = mm_nt(branch_ref[...], out_ref[...]).astype(BF16)
        for group in range(groups):
            piece = product[:, group * group_width : (group + 1) * group_width]
            grad_mixed[group] = jnp.concatenate([piece, fill], axis=1)
        grad_mixed.send()
    else:
        grad_mixed, query_ref, key_ref, value_ref, probs_ref = refs[:5]
        packed_a, packed_b, grads, sheared = refs[5:]
        grad_mixed.ready()
    for ref in (query_ref, key_ref, value_ref, probs_ref):
        ref.ready()
    stride = 2 * side - 1
    span_lanes = sheared.shape[2]
    packed_lanes = packed_a.shape[1]
    table_lanes = round_up(stride * stride, LANES)

    def one_group(pick, carry):
        group = (picks[0] + pick) ^ rank
        wide = grad_mixed.shape[2] // LANES
        query_tiles, key_tiles, value_tiles = [None] * wide, [None] * wide, [None] * wide
        for slot in range(slots):
            head = group * slots + slot
            first, lanes, offset = head_window(slot, head_width)
            mask = head_mask(lanes, offset, head_width)
            span = slice(first, first + lanes)
            mixed_now = grad_mixed[group, :, span] * mask
            probs = probs_ref[head]
            grad_probs = mm_nt(value_ref[group, :, span], mixed_now)
            probs_wide = probs.astype(F32)
            weighted = probs_wide * grad_probs
            grad_scores = weighted - probs_wide * jnp.sum(weighted, axis=0, keepdims=True)
            rounded = grad_scores.astype(BF16)
            add_tiles(value_tiles, mm(probs, mixed_now), first)
            add_tiles(key_tiles, mm(rounded, query_ref[group, :, span] * mask), first)
            add_tiles(query_tiles, mm_tn(rounded, key_ref[group, :, span] * mask), first)
            steps = LANES // side
            shear = jnp.zeros((side, span_lanes), F32)
            for turn in range(steps):
                summed = None
                for jump in range(-(-side // steps)):
                    block = side - 1 - (jump * steps + turn)
                    if block >= 0:
                        piece = grad_scores[block * side : (block + 1) * side, :]
                        parts = []
                        if jump:
                            parts.append(jnp.zeros((side, jump * LANES), F32))
                        parts.append(piece)
                        rest = span_lanes - jump * LANES - length
                        if rest:
                            parts.append(jnp.zeros((side, rest), F32))
                        piece = jnp.concatenate(parts, axis=1)
                        summed = piece if summed is None else summed + piece
                shear = shear + (pltpu.roll(summed, turn * side, 1) if turn else summed)
            sheared[:, pl.ds(pick * slots + slot, 1), :] = shear[:, None, :]
        query = (jnp.concatenate(query_tiles, axis=1) * scale).astype(BF16)
        key = (jnp.concatenate(key_tiles, axis=1) * scale).astype(BF16)
        value = jnp.concatenate(value_tiles, axis=1).astype(BF16)
        grads[0, pick] = query
        grads[1, pick] = key
        grads[2, pick] = value
        return carry

    lax.fori_loop(0, len(picks), one_group, 0)
    selections = [squeeze_part(part, side, stride) for part in range(span_lanes // LANES)]
    heads = 2 * slots
    tall = table_lanes // LANES
    total = [jnp.zeros((heads, LANES), F32)] * tall
    for column in range(side):
        high, low = split_two(sheared[column])
        tiles = [None] * tall
        for part, (first, lanes, squeeze) in enumerate(selections):
            span = slice(part * LANES, (part + 1) * LANES)
            add_tiles(tiles, mm_nt(high[:, span], squeeze) + mm_nt(low[:, span], squeeze), first)
        spread = jnp.concatenate(
            [jnp.zeros((heads, LANES), F32) if tile is None else tile for tile in tiles], axis=1
        )
        turn = side - 1 - column
        turned = pltpu.roll(spread, turn, 1) if turn else spread
        total = [
            old + turned[:, place * LANES : (place + 1) * LANES] for place, old in enumerate(total)
        ]
    for pick, packed_ref in enumerate((packed_a, packed_b)):
        for place in range(tall):
            packed_ref[length + place * slots : length + (place + 1) * slots, :LANES] = total[place][
                pick * slots : (pick + 1) * slots
            ].astype(BF16)
        pieces = [grads[item, pick][:, :group_width] for item in range(3)]
        if packed_lanes > 3 * group_width:
            pieces.append(jnp.zeros((length, packed_lanes - 3 * group_width), BF16))
        packed_ref[:length, :] = jnp.concatenate(pieces, axis=1)


def tokens_kernel(
    dims,
    ranks,
    steps_ref,
    near_grads,
    far_grads,
    query_ref,
    key_ref,
    value_ref,
    relative_ref,
    params,
    middle_ref,
    middle_sums,
    embed_ref,
    up_bias_ref,
    tokens_hbm,
    image_ref,
    grad_ref,
    flat,
    own_tokens,
    sem,
):
    groups, slots, head_width, side, scale = dims
    group_width = slots * head_width
    rank = ranks[0]
    length = side * side
    own_copy = pltpu.make_async_copy(
        tokens_hbm.at[pl.ds(pl.multiple_of(rank * length, length), length)], own_tokens, sem
    )
    own_copy.start()
    for group in range(groups):
        away = group ^ rank
        for item in range(3):
            piece = jnp.where(away >= 2, far_grads[item, away & 1], near_grads[item, away & 1])
            flat[item, :, group * group_width : (group + 1) * group_width] = piece[:, :group_width]
    grad_normed = (
        mm_nt(flat[0], query_ref[...])
        + mm_nt(flat[1], key_ref[...])
        + mm_nt(flat[2], value_ref[...])
    )
    place = place_matrix(relative_ref[0:1, :], side)
    own_copy.wait()
    unit, inverse = unit_rows(mm(place, own_tokens[...]))
    total = middle_ref[...] + norm_back(grad_normed, unit, inverse, params[0:1, :])
    high, low = split_two(total)
    grad_ref[...] = mm_tn(place, high) + mm_tn(place, low)
    grad_ref.send()
    step = steps_ref[rank]
    sums = [
        jnp.sum(flat[0].astype(F32), axis=0, keepdims=True),
        jnp.sum(flat[2].astype(F32), axis=0, keepdims=True),
        embed_ref[0:1, :],
        jnp.full((1, embed_ref.shape[1]), (step // 8).astype(F32)),
        jnp.full((1, embed_ref.shape[1]), (step % 8).astype(F32)),
        middle_sums[0:4, :],
        jnp.sum(grad_normed * unit, axis=0, keepdims=True),
        jnp.sum(grad_normed, axis=0, keepdims=True),
        up_bias_ref[0:1, :],
        jnp.zeros((4, embed_ref.shape[1]), F32),
    ]
    image_ref[...] = jnp.concatenate(sums, axis=0).astype(BF16)
    image_ref.send()


def weights_kernel(dims, level, ranks, normed, *refs):
    groups, slots, head_width, side, scale = dims
    group_width = slots * head_width
    rows = side * side
    keep_first, keep_second, send_first, send_second, packed, branch, mixed = refs[3 * groups :]
    table = None
    for chunk in range(groups):
        span = slice(chunk * rows, (chunk + 1) * rows)
        source = refs[chunk]
        packed[span, :] = source[:rows, :]
        branch[span, :] = refs[groups + chunk][...]
        mixed[span, :] = refs[2 * groups + chunk][...]
        part = source[rows:, :LANES].astype(F32)
        table = part if table is None else table + part
    bit = (ranks[1] >> level) & 1
    left = mm_tn(packed[...], normed[...]).astype(BF16)
    right = mm_tn(mixed[...], branch[...]).astype(BF16)
    keep_first[...], send_first[...] = halves(left[: 2 * group_width], bit)
    value, out = left[2 * group_width : 3 * group_width], right[:group_width]
    low, high = halves(table.astype(BF16), bit)
    fill = jnp.zeros((low.shape[0], value.shape[1] - LANES), BF16)
    keep_second[:group_width, :] = jnp.where(bit == 0, value, out)
    keep_second[group_width:, :] = jnp.concatenate([low, fill], axis=1)
    send_second[:group_width, :] = jnp.where(bit == 0, out, value)
    send_second[group_width:, :] = jnp.concatenate([high, fill], axis=1)


def split_kernel(level, tail, ranks, kept, got, keep_ref, send_ref):
    total = (kept[...].astype(F32) + got[...].astype(F32)).astype(BF16)
    bit = (ranks[1] >> level) & 1
    body = total.shape[0] - tail
    keep, send = halves(total[:body], bit)
    send_ref[: body // 2, :] = send
    keep_ref[: body // 2, :] = keep
    if tail:
        keep, send = halves(total[body:], bit)
        send_ref[body // 2 :, :] = send
        keep_ref[body // 2 :, :] = keep


def join_kernel(level, tail, ranks, own, other, out_ref):
    body = own.shape[0] - tail
    bit = (ranks[1] >> level) & 1
    low = jnp.where(bit == 0, own[...], other[...])
    high = jnp.where(bit == 0, other[...], own[...])
    out_ref[:body, :] = low[:body]
    out_ref[body : 2 * body, :] = high[:body]
    if tail:
        out_ref[2 * body : 2 * body + tail, :] = low[body:]
        out_ref[2 * body + tail :, :] = high[body:]


def widen_kernel(level, ranks, own, other, out_ref):
    bit = (ranks[1] >> level) & 1
    first = (pl.program_id(0) < pl.num_programs(0) // 2) == (bit == 0)

    @pl.when(first)
    def _():
        out_ref[...] = own[...].astype(F32)

    @pl.when(jnp.logical_not(first))
    def _():
        out_ref[...] = other[...].astype(F32)


def widen_pair_kernel(level, tail, ranks, own, other, low_ref, high_ref, *refs):
    bit = (ranks[1] >> level) & 1
    body = own.shape[0] - tail
    low_ref[...] = jnp.where(bit == 0, own[:body, :], other[:body, :]).astype(F32)
    low_ref.send()
    high_ref[...] = jnp.where(bit == 0, other[:body, :], own[:body, :]).astype(F32)
    high_ref.send()
    if tail:
        table = refs[0]
        slots = table.shape[0]
        low = jnp.where(bit == 0, own[body:, :LANES], other[body:, :LANES]).astype(F32)
        high = jnp.where(bit == 0, other[body:, :LANES], own[body:, :LANES]).astype(F32)
        for part in range(table.shape[1] // LANES):
            source, row = (low, part * slots) if part * slots < tail else (high, part * slots - tail)
            table[:, part * LANES : (part + 1) * LANES] = source[row : row + slots]


def finish_kernel(
    dims, images, ranks, all_ref, query_hbm, value_hbm, query_ref, value_ref, table_ref, sums_ref,
    weights, sems,
):
    groups, slots, head_width, side, scale = dims
    group_width = slots * head_width
    rank = ranks[0]
    start = pl.multiple_of(rank * group_width, 16)
    copies = []
    for item, source in enumerate((query_hbm, value_hbm)):
        copy = pltpu.make_async_copy(
            source.at[pl.ds(start, group_width)], weights.at[item], sems.at[item]
        )
        copy.start()
        copies.append(copy)

    def own_columns(rows):
        chosen = rows[:, :group_width]
        for group in range(1, groups):
            piece = rows[:, group * group_width : (group + 1) * group_width]
            chosen = jnp.where(rank == group, piece, chosen)
        return chosen

    sums_ref[...] = jnp.zeros(sums_ref.shape, F32)
    embed = all_ref[2]
    totals = None
    for item, target in enumerate((query_ref, value_ref)):
        rows = all_ref[item]
        target[...] = mm_tn(own_columns(rows), embed)
        target.send()
        copies[item].wait()
        part = mm_nt(rows, weights[item])
        totals = part if totals is None else totals + part
    steps = all_ref[3][:, 0:1].astype(F32) * 8.0 + all_ref[4][:, 0:1].astype(F32)
    step = lax.broadcasted_iota(jnp.int32, (images, table_ref.shape[1]), 1)
    chosen = jnp.where(step == steps.astype(jnp.int32), 1.0, 0.0).astype(BF16)
    high, low = split_two(totals)
    table_ref[...] = mm_tn(high, chosen) + mm_tn(low, chosen)
    table_ref.send()
    for item in range(6):
        total = jnp.sum(all_ref[5 + item].astype(F32), axis=0, keepdims=True)
        sums_ref[item : item + 1, :group_width] = own_columns(total)
    image = lax.broadcasted_iota(jnp.int32, (images, 1), 0)
    mine = jnp.where(image % groups == rank, all_ref[11].astype(F32), 0.0)
    sums_ref[6:7, :] = jnp.sum(mine, axis=0, keepdims=True)


def block_kernel(side, relative_ref, own, near, far, middle_ref, params, out_ref):
    total = own[0].astype(F32) + near[0].astype(F32) + far[...].astype(F32)
    total = (middle_ref[...] + total + params[5:6, :]).astype(BF16)
    place = place_matrix(relative_ref[0:1, :], side)
    out_ref[...] = mm_tn(place, total).astype(BF16)


def shape_of(*sizes, dtype=BF16):
    return jax.ShapeDtypeStruct(sizes, dtype)


VMEM = pl.BlockSpec(memory_space=pltpu.VMEM)
HBM = pl.BlockSpec(memory_space=pl.ANY)
SMEM = pl.BlockSpec(memory_space=pltpu.SMEM)
MIB = 1024 * 1024
FEED = 20


def cost(us):
    return pl.CostEstimate(flops=int(us * 1.15e9), bytes_accessed=1000, transcendentals=0)


class Staged:
    def __init__(self, source, target, sem):
        self.ref, self.waited = target, False
        self.copy = pltpu.make_async_copy(source, target, sem)
        self.copy.start()
        self.shape = target.shape

    def ready(self):
        if not self.waited:
            self.waited = True
            self.copy.wait()
        return self.ref

    def __getitem__(self, place):
        return self.ready()[place]


class Result:
    def __init__(self, ref, target=None, sem=None):
        self.ref, self.sent = ref, target is None
        self.copy = None if self.sent else pltpu.make_async_copy(ref, target, sem)
        self.shape, self.dtype = ref.shape, ref.dtype

    def __getitem__(self, place):
        return self.ref[place]

    def __setitem__(self, place, value):
        self.ref[place] = value

    def send(self):
        if not self.sent:
            self.sent = True
            self.copy.start()


class Held:
    def __init__(self, ref):
        self.ref, self.shape = ref, ref.shape

    def ready(self):
        return self.ref

    def __getitem__(self, place):
        return self.ref[place]


def run(kernel, outs, inputs, kinds=None, scratch=(), deps=(), us=0.2, away=(), vmem=40):
    kinds = "v" * len(inputs) if kinds is None else kinds
    assert len(kinds) == len(inputs)
    single = not isinstance(outs, (list, tuple))
    outs = [outs] if single else list(outs)
    staged = [place for place, kind in enumerate(kinds) if kind == "w"]
    count, extra, results = len(inputs), len(deps), len(outs)
    buffers = [pltpu.VMEM(inputs[place].shape, inputs[place].dtype) for place in staged]
    buffers += [pltpu.VMEM(outs[place].shape, outs[place].dtype) for place in away]
    if buffers:
        buffers.append(pltpu.SemaphoreType.DMA((len(buffers),)))

    def body(*refs):
        given = list(refs[:count])
        targets = refs[count + extra : count + extra + results]
        rest = refs[count + extra + results :]
        for place, kind in enumerate(kinds):
            if kind == "v":
                given[place] = Held(given[place])
        for order, place in enumerate(staged):
            sem = rest[len(buffers) - 1].at[order]
            given[place] = Staged(given[place], rest[order], sem)
        made = []
        for place, target in enumerate(targets):
            if place in away:
                order = len(staged) + away.index(place)
                made.append(Result(rest[order], target, rest[len(buffers) - 1].at[order]))
            else:
                made.append(Result(target))
        kernel(*given, *made, *rest[len(buffers) :])
        for result in made:
            result.send()
        for place in staged:
            given[place].ready()
        for result in made:
            if result.copy is not None:
                result.copy.wait()

    space = {"s": SMEM, "h": HBM, "v": VMEM, "w": HBM}
    found = pl.pallas_call(
        body,
        out_shape=outs,
        in_specs=[space[kind] for kind in kinds] + [HBM] * extra,
        out_specs=[HBM if place in away else VMEM for place in range(results)],
        scratch_shapes=buffers + list(scratch),
        compiler_params=pltpu.CompilerParams(vmem_limit_bytes=vmem * MIB),
        cost_estimate=cost(us),
    )(*inputs, *deps)
    return found[0] if single else found


def quick(kernel, outs, inputs, deps=()):
    count = len(inputs)

    def body(*refs):
        kernel(*refs[:count], *refs[count + len(deps) :])

    specs = [SMEM if given.shape == (2,) else VMEM for given in inputs]
    return pl.pallas_call(
        body,
        out_shape=outs,
        in_specs=specs + [HBM] * len(deps),
        out_specs=jax.tree.map(lambda _: VMEM, outs),
        compiler_params=pltpu.CompilerParams(vmem_limit_bytes=4 * MIB),
        cost_estimate=cost(0.1),
    )(*inputs, *deps)


def widen(ranks, level, own, other):
    half, columns = own.shape
    parts = 2
    block = half // parts

    def own_map(i, me):
        bit = (me[1] >> level) & 1
        return (jnp.clip(i - parts * bit, 0, parts - 1), 0)

    def other_map(i, me):
        bit = (me[1] >> level) & 1
        return (jnp.clip(i - parts * (1 - bit), 0, parts - 1), 0)

    return pl.pallas_call(
        partial(widen_kernel, level),
        out_shape=shape_of(2 * half, columns, dtype=F32),
        grid_spec=pltpu.PrefetchScalarGridSpec(
            num_scalar_prefetch=1,
            grid=(2 * parts,),
            in_specs=[
                pl.BlockSpec((block, columns), own_map),
                pl.BlockSpec((block, columns), other_map),
            ],
            out_specs=pl.BlockSpec((block, columns), lambda i, me: (i, 0)),
        ),
        compiler_params=pltpu.CompilerParams(vmem_limit_bytes=16 * MIB),
        cost_estimate=cost(5.0),
    )(ranks, own, other)


def swap(array, axis, distance):
    size = lax.axis_size(axis)
    return lax.ppermute(array, axis, [(i, i ^ distance) for i in range(size)])


def after(array, *others):
    return lax.optimization_barrier((array, *others))[0]


class Total:
    def __init__(self, ranks, order, keep, send, tail=0):
        self.ranks, self.order, self.tail = ranks, order, tail
        self.keep = keep
        self.got = self.swap(0, send)

    def swap(self, place, array):
        return swap(array, "dp", 1 << self.order[place])

    def split(self, deps=()):
        half, columns = self.keep.shape
        part = shape_of(half // 2, columns)
        self.keep, send = quick(
            partial(split_kernel, self.order[1], self.tail),
            [part, part],
            [self.ranks, self.keep, self.got],
            deps,
        )
        self.got = self.swap(1, send)
        return self.keep

    def add(self, place, deps=()):
        self.keep = quick(add_kernel, shape_of(*self.keep.shape), [self.keep, self.got], deps)
        self.got = self.swap(place, self.keep)
        return self.keep

    def join(self, deps=()):
        half, columns = self.keep.shape
        self.keep = quick(
            partial(join_kernel, self.order[1], self.tail // 2),
            shape_of(2 * half, columns),
            [self.ranks, self.keep, self.got],
            deps,
        )
        self.got = self.swap(0, self.keep)
        return self.keep

    def advance(self, stage, deps=()):
        levels = len(self.order)
        if stage == 0:
            return self.split(deps)
        if stage < levels - 1:
            return self.add(stage + 1, deps)
        if stage == levels - 1:
            return self.add(1, deps)
        return self.join(deps)


def add_low(left, right):
    return (left.astype(F32) + right.astype(F32)).astype(BF16)


def on_device(
    tokens,
    timesteps,
    relative_index,
    time_table,
    query_weight,
    key_weight,
    value_weight,
    time_query_weight,
    time_value_weight,
    out_weight,
    out_bias,
    first_gain,
    first_shift,
    second_gain,
    second_shift,
    up_weight,
    up_bias,
    down_weight,
    down_bias,
    bias_table,
    cotangent,
):
    length = relative_index.shape[0]
    width = tokens.shape[1]
    heads = bias_table.shape[1]
    head_width = width // heads
    side = math.isqrt(length)
    stride = 2 * side - 1
    groups = lax.axis_size("mp")
    dp_size = lax.axis_size("dp")
    rank = lax.axis_index("mp")
    ranks = jnp.stack([rank, lax.axis_index("dp")]).astype(jnp.int32)
    slots = heads // groups
    group_width = slots * head_width
    group_lanes = round_up(group_width, LANES)
    packed_lanes = round_up(3 * group_width, LANES)
    table_lanes = round_up(stride * stride, LANES)
    span_lanes = round_up(stride * side, LANES)
    hidden_width = up_weight.shape[1]
    rows = groups * length
    dims = (groups, slots, head_width, side, head_width ** (-0.5))
    line = lambda vector: vector.reshape(1, -1)
    params = jnp.stack(
        [first_gain, first_shift, second_gain, second_shift, out_bias, down_bias]
        + [jnp.zeros_like(down_bias)] * 2
    )
    levels = list(range(dp_size.bit_length() - 1))
    other_order = levels[1::-1] + levels[2:]

    def grouped():
        return shape_of(groups, length, group_lanes)

    one_group = shape_of(length, group_lanes)

    cot_near = swap(cotangent, "mp", 1)
    cot_far = swap(cotangent, "mp", 2)
    steps = time_table.shape[0]
    outs = run(
        partial(attend_kernel, dims),
        [
            grouped(),
            grouped(),
            grouped(),
            shape_of(heads, length, length),
            one_group,
            one_group,
            one_group,
            one_group,
            shape_of(length, width, dtype=F32),
            shape_of(length, width),
            shape_of(8, width, dtype=F32),
        ],
        [
            ranks,
            timesteps,
            relative_index,
            bias_table.T,
            params,
            tokens,
            time_table.reshape(steps // 8, 8, width),
            query_weight,
            key_weight,
            value_weight,
            time_query_weight,
            time_value_weight,
            out_weight,
        ],
        "ssvvv" + "h" * 8,
        [
            pltpu.VMEM((6, width, width), BF16),
            pltpu.VMEM((length, width), BF16),
            pltpu.VMEM((8, width), BF16),
            pltpu.VMEM((heads, table_lanes), F32),
            pltpu.VMEM((heads * side, table_lanes), BF16),
            pltpu.VMEM((heads * side, table_lanes), BF16),
            pltpu.VMEM((heads, side, span_lanes), F32),
            pltpu.VMEM((length, width), BF16),
            pltpu.VMEM((groups, length, group_lanes), BF16),
            pltpu.SemaphoreType.DMA((8,)),
        ],
        us=16.0,
        vmem=54,
    )
    query_rows, key_rows, value_rows, probs = outs[:4]
    mixed = outs[4:8]
    middle, normed_own, embed = outs[8:]
    normed_near = swap(normed_own, "mp", 1)
    normed_far = swap(normed_own, "mp", 2)

    normed_first = pl.pallas_call(
        partial(normed_kernel, side),
        out_shape=shape_of(rows, width),
        grid_spec=pltpu.PrefetchScalarGridSpec(
            num_scalar_prefetch=1,
            grid=(groups,),
            in_specs=[
                pl.BlockSpec((8, length), lambda i, me: (0, 0)),
                pl.BlockSpec((length, width), lambda i, me: (i ^ me[0], 0)),
                pl.BlockSpec((8, width), lambda i, me: (0, 0)),
                HBM,
                HBM,
            ],
            out_specs=pl.BlockSpec((length, width), lambda i, me: (i, 0)),
        ),
        compiler_params=pltpu.CompilerParams(vmem_limit_bytes=40 * MIB),
        cost_estimate=cost(0.3),
    )(ranks, relative_index, tokens, params, normed_own, cot_far)

    cot_last = swap(cot_far, "mp", 1)
    pair = shape_of(2 * length, width)
    hidden_pair = shape_of(2 * length, hidden_width)
    chunk = shape_of(length, width)
    near_active, near_hidden, near_moved, grad_own, grad_near = run(
        partial(feed_near_kernel, side),
        [hidden_pair, hidden_pair, pair, chunk, chunk],
        [
            relative_index,
            normed_own,
            normed_near,
            cotangent,
            cot_near,
            up_weight,
            line(up_bias),
            down_weight,
        ],
        "vvvvvwvw",
        deps=[normed_first, cot_last],
        us=7.0,
        vmem=FEED,
    )
    near_got = swap(grad_near, "mp", 1)
    normed_last = swap(after(normed_far, grad_near), "mp", 1)
    mixed_got = [swap(mixed[away], "mp", away) for away in range(1, groups)]
    active, hidden, moved, grad_far, grad_last, up_bias_sum = run(
        partial(feed_far_kernel, side),
        [hidden_pair, hidden_pair, pair, chunk, chunk, shape_of(8, hidden_width, dtype=F32)],
        [
            relative_index,
            normed_far,
            normed_last,
            cot_far,
            cot_last,
            up_weight,
            line(up_bias),
            down_weight,
            near_hidden,
        ],
        "vvvvvwvwv",
        us=9.0,
        deps=[near_got],
        vmem=FEED,
    )
    last_got = swap(grad_last, "mp", 1)
    half = shape_of(hidden_width // 2, width)
    keep, send = run(
        partial(down_grad_kernel, levels[0]),
        [half, half],
        [ranks, near_active, near_moved, active, moved],
        "svvvv",
        deps=[up_bias_sum] + mixed_got,
        vmem=FEED,
    )
    down = Total(ranks, levels, keep, send)
    grad_sent = run(add_kernel, chunk, [grad_far, last_got], deps=[keep], vmem=4)
    far_got = swap(grad_sent, "mp", 2)
    half = shape_of(width // 2, hidden_width)
    keep, send = run(
        partial(up_grad_kernel, other_order[0]),
        [half, half],
        [ranks, normed_own, normed_near, normed_far, normed_last, near_hidden, hidden],
        "s" + "v" * 6,
        [pltpu.VMEM((rows, width), BF16)],
        deps=[grad_sent],
        us=0.4,
        vmem=FEED,
    )
    up = Total(ranks, other_order, keep, send)
    chunks = shape_of(2, length, width)
    out_keep, out_send = run(
        out_kernel, [chunks, chunks], [near_active, active, down_weight], "vvw", deps=[keep], us=0.4, vmem=FEED
    )
    out_got = swap(out_send, "mp", 1)
    grad_branch, grad_middle, middle_sums = run(
        middle_kernel,
        [chunk, shape_of(length, width, dtype=F32), shape_of(8, width, dtype=F32)],
        [grad_own, near_got, far_got, middle, near_moved, params],
        deps=[out_keep],
        vmem=8,
    )
    branch_near = swap(grad_branch, "mp", 1)
    branch_far = swap(grad_branch, "mp", 2)
    last = down.advance(0, deps=[middle_sums])

    tail = slots * table_lanes // LANES
    back_scratch = [pltpu.VMEM((side, 2 * slots, span_lanes), F32)]
    grads_shape = shape_of(3, 2, length, group_lanes)
    packed_shape = shape_of(length + tail, packed_lanes)
    heads_in = [query_rows, key_rows, value_rows, probs]
    packed_2, packed_3, far_grads, grad_mixed = run(
        partial(attend_back_kernel, dims, (2, 3)),
        [packed_shape, packed_shape, grads_shape, grouped()],
        [ranks, grad_branch, out_weight] + heads_in,
        "svwvvvv",
        back_scratch,
        deps=[last, branch_near],
        us=0.8,
    )
    packed_2 = swap(packed_2, "mp", 2)
    packed_3 = swap(packed_3, "mp", 3)
    last = up.advance(0, deps=[grad_mixed])
    last = down.advance(1, deps=[last])
    packed_0, packed_1, near_grads = run(
        partial(attend_back_kernel, dims, (0, 1)),
        [packed_shape, packed_shape, grads_shape],
        [ranks, grad_mixed] + heads_in,
        "svvvvv",
        back_scratch,
        deps=[last],
        us=0.8,
    )
    last = up.advance(1, deps=[packed_0, branch_far, packed_2])
    packed_1 = swap(packed_1, "mp", 1)
    branch_last = swap(branch_far, "mp", 1)
    half = shape_of(group_width, width)
    more = shape_of(group_width + tail // 2, width)
    keep_first, keep_second, send_first, send_second = run(
        partial(weights_kernel, dims, levels[0]),
        [half, more, half, more],
        [ranks, normed_first, packed_0, packed_1, packed_2, packed_3]
        + [grad_branch, branch_near, branch_far, branch_last]
        + [mixed[0]]
        + mixed_got,
        "s" + "v" * 13,
        [
            pltpu.VMEM((rows, packed_lanes), BF16),
            pltpu.VMEM((rows, width), BF16),
            pltpu.VMEM((rows, group_lanes), BF16),
        ],
        deps=[last],
        us=0.5,
    )
    first = Total(ranks, levels, keep_first, send_first)
    second = Total(ranks, levels, keep_second, send_second, tail // 2)
    last = keep_second
    image_rows, tokens_grad = run(
        partial(tokens_kernel, dims),
        [shape_of(16, width), shape_of(length, width, dtype=F32)],
        [
            ranks,
            timesteps,
            near_grads,
            far_grads,
            query_weight,
            key_weight,
            value_weight,
            relative_index,
            params,
            grad_middle,
            middle_sums,
            embed,
            jnp.pad(up_bias_sum, ((0, 0), (0, width - hidden_width))),
            tokens,
        ],
        "ssvvwwwvvvvvvh",
        [
            pltpu.VMEM((3, length, width), BF16),
            pltpu.VMEM((length, width), BF16),
            pltpu.SemaphoreType.DMA,
        ],
        deps=[last],
        us=0.7,
        away=(1,),
        vmem=24,
    )
    image_all = lax.all_gather(image_rows, ("dp", "mp"), axis=0, tiled=True)
    last = image_rows

    out_far = swap(add_low(out_keep[1], out_got[1]), "mp", 2)

    stages = len(levels) + 1
    todo = [(down, 2), (first, 0), (second, 0), (down, 3), (first, 1), (second, 1), (up, 2)]
    todo += [(up, 3), (first, 2), (second, 2), (first, 3), (second, 3)]
    for stage in range(4, stages):
        todo += [(total, stage) for total in (down, up, first, second)]
    for total, stage in todo:
        last = total.advance(stage, deps=[last])
    down_grad = widen(ranks, levels[0], down.keep, down.got)
    up_grad = widen(ranks, other_order[0], up.keep, up.got)
    wide = shape_of(group_width, width, dtype=F32)
    query_grad, key_grad = run(
        partial(widen_pair_kernel, levels[0], 0),
        [wide, wide],
        [ranks, first.keep, first.got],
        "svv",
        away=(0, 1),
    )
    value_grad, out_grad, table_grad = run(
        partial(widen_pair_kernel, levels[0], tail // 2),
        [wide, wide, shape_of(slots, table_lanes, dtype=F32)],
        [ranks, second.keep, second.got],
        "svv",
        away=(0, 1),
    )

    images = dp_size * groups
    image_all = image_all.reshape(images, 16, width)[:, :12].transpose(1, 0, 2)
    time_query_grad, time_value_grad, time_table_grad, sums = run(
        partial(finish_kernel, dims, images),
        [
            shape_of(group_width, width, dtype=F32),
            shape_of(group_width, width, dtype=F32),
            shape_of(group_width, steps, dtype=F32),
            shape_of(8, width, dtype=F32),
        ],
        [ranks, image_all, time_query_weight, time_value_weight],
        "svhh",
        [pltpu.VMEM((2, group_width, width), BF16), pltpu.SemaphoreType.DMA((2,))],
        away=(0, 1, 2),
        vmem=24,
    )
    parts = [sums[j, :group_width] for j in range(6)]
    second_gain_grad, second_shift_grad, out_bias_grad, down_bias_grad = parts[:4]
    first_gain_grad, first_shift_grad = parts[4:]
    bias_table_grad = table_grad[:, : stride * stride].T
    up_bias_grad = sums[6, :hidden_width]

    block_out = run(
        partial(block_kernel, side),
        shape_of(length, width),
        [relative_index, out_keep, out_got, out_far, middle, params],
    )
    return (
        block_out,
        tokens_grad,
        time_table_grad.T,
        query_grad.T,
        key_grad.T,
        value_grad.T,
        time_query_grad.T,
        time_value_grad.T,
        out_grad,
        out_bias_grad,
        first_gain_grad,
        first_shift_grad,
        second_gain_grad,
        second_shift_grad,
        up_grad,
        up_bias_grad,
        down_grad,
        down_bias_grad,
        bias_table_grad,
    )


def solution(mesh):
    whole = P()
    rows = P(("dp", "mp"), None)
    columns = P(None, "mp")
    split = P("mp")
    placed = (
        (P("dp", None), P("dp"))
        + (whole,) * 13
        + (columns, split, P("mp", None), whole, whole, rows)
    )
    return jax.shard_map(
        on_device,
        mesh=mesh,
        in_specs=placed,
        out_specs=(rows, rows)
        + (columns,) * 6
        + (P("mp", None),)
        + (split,) * 5
        + (columns, split, P("mp", None), split, columns),
        check_vma=False,
    )
```

```python
import math
from functools import partial

import jax
import jax.numpy as jnp
from jax import lax
from jax.experimental import pallas as pl
from jax.experimental.pallas import tpu as pltpu
from jax.sharding import PartitionSpec as P

EPSILON = 1e-06
HIGHEST = lax.Precision.HIGHEST
F32 = jnp.float32
BF16 = jnp.bfloat16
LANES = 128
PACE = 0.3


def mm(left, right):
    return lax.dot_general(left, right, (((1,), (0,)), ((), ())), preferred_element_type=F32)


def mm_nt(left, right):
    return lax.dot_general(left, right, (((1,), (1,)), ((), ())), preferred_element_type=F32)


def mm_tn(left, right):
    return lax.dot_general(left, right, (((0,), (0,)), ((), ())), preferred_element_type=F32)


def round_up(value, step):
    return -(-value // step) * step


def head_window(slot, head_width):
    first = slot * head_width // LANES * LANES
    last = round_up((slot + 1) * head_width, LANES)
    return first, last - first, slot * head_width - first


def head_mask(lanes, offset, head_width):
    lane = lax.broadcasted_iota(jnp.int32, (1, lanes), 1)
    return jnp.where((lane >= offset) & (lane < offset + head_width), 1.0, 0.0).astype(BF16)


def row_of(ref):
    return ref[...].reshape(1, ref.shape[0])


def unit_rows(values):
    centred = values - jnp.mean(values, axis=-1, keepdims=True)
    inverse = lax.rsqrt(jnp.mean(centred * centred, axis=-1, keepdims=True) + EPSILON)
    return centred * inverse, inverse


def norm_back(grad_out, unit, inverse, gain_row):
    grad_unit = grad_out * gain_row
    first_mean = jnp.mean(grad_unit, axis=-1, keepdims=True)
    second_mean = jnp.mean(grad_unit * unit, axis=-1, keepdims=True)
    return inverse * (grad_unit - first_mean - unit * second_mean)


def add_tiles(tiles, product, first):
    for part in range(product.shape[1] // LANES):
        place = first // LANES + part
        piece = product[:, part * LANES : (part + 1) * LANES]
        tiles[place] = piece if tiles[place] is None else tiles[place] + piece


def squeeze_part(part, side, stride):
    each = LANES // side
    first = part * each * stride // LANES * LANES
    last = round_up((part * each + each - 1) * stride + side, LANES)
    wide = lax.broadcasted_iota(jnp.int32, (last - first, LANES), 0) + first
    close = lax.broadcasted_iota(jnp.int32, (last - first, LANES), 1)
    same = wide == (part * each + close // side) * stride + close % side
    return first, last - first, jnp.where(same, 1.0, 0.0).astype(BF16)


def place_matrix(relative_row, side):
    stride = 2 * side - 1
    entry = relative_row.astype(F32)
    row_part = jnp.floor((entry + 0.5) * (1.0 / stride))
    column_part = entry - row_part * stride
    row_part = jnp.max(row_part, axis=1, keepdims=True) - row_part
    column_part = jnp.max(column_part, axis=1, keepdims=True) - column_part
    cells = (row_part * side + column_part).astype(jnp.int32)
    length = side * side
    cell = lax.broadcasted_iota(jnp.int32, (length, length), 0)
    return jnp.where(cell == cells, 1.0, 0.0).astype(BF16)


def split_two(values):
    high = values.astype(BF16)
    return high, (values - high.astype(F32)).astype(BF16)


def attend_kernel(
    dims,
    ranks,
    steps_ref,
    relative_ref,
    table_ref,
    first_gain,
    first_shift,
    second_gain,
    second_shift,
    out_bias,
    tokens_hbm,
    times_hbm,
    query_hbm,
    key_hbm,
    value_hbm,
    time_query_hbm,
    time_value_hbm,
    out_hbm,
    query_ref,
    key_ref,
    value_ref,
    probs_ref,
    mixed_0,
    mixed_1,
    mixed_far,
    middle_ref,
    normed_ref,
    embed_ref,
    weights,
    own_tokens,
    times,
    table,
    wide_high,
    wide_low,
    windows,
    flat,
    mixed_ref,
    sems,
):
    groups, slots, head_width, side, scale = dims
    group_width = slots * head_width
    rank = ranks[0]
    length = side * side
    step = steps_ref[rank]
    own_copy = pltpu.make_async_copy(
        tokens_hbm.at[pl.ds(pl.multiple_of(rank * length, length), length)], own_tokens, sems.at[6]
    )
    own_copy.start()
    sources = (query_hbm, key_hbm, value_hbm, time_query_hbm, time_value_hbm, out_hbm)
    copies = {}
    for item in (0, 1, 3, 2, 4, 5):
        copies[item] = pltpu.make_async_copy(sources[item], weights.at[item], sems.at[item])
        copies[item].start()
    times_copy = pltpu.make_async_copy(times_hbm.at[step // 8], times, sems.at[7])
    times_copy.start()
    stride = 2 * side - 1
    heads = groups * slots
    row_lanes = table.shape[1]
    table[...] = jnp.zeros_like(table)
    table[:, : stride * stride] = table_ref[...]
    for head in range(heads):
        row = jnp.broadcast_to(table[head : head + 1, :], (side, row_lanes))
        shifted = pltpu.roll(row, row_lanes - (side - 1), 1, stride=1, stride_axis=0)
        high, low = split_two(shifted)
        wide_high[head * side : (head + 1) * side, :] = high
        wide_low[head * side : (head + 1) * side, :] = low
    span_lanes = windows.shape[2]
    for part in range(span_lanes // LANES):
        first, lanes, squeeze = squeeze_part(part, side, stride)
        span = slice(first, first + lanes)
        narrow = mm(wide_high[:, span], squeeze) + mm(wide_low[:, span], squeeze)
        windows[:, :, part * LANES : (part + 1) * LANES] = narrow.reshape(heads, side, LANES)
    place = place_matrix(relative_ref[0:1, :], side)
    own_copy.wait()
    own = mm(place, own_tokens[...])
    unit, _ = unit_rows(own)
    normed = (unit * row_of(first_gain) + row_of(first_shift)).astype(BF16)

    def into_groups(rows, target):
        fill = jnp.zeros((rows.shape[0], target.shape[2] - group_width), rows.dtype)
        for group in range(groups):
            piece = rows[:, group * group_width : (group + 1) * group_width]
            target[group] = jnp.concatenate([piece, fill], axis=1)

    copies[0].wait()
    query = mm(normed, weights[0])
    copies[1].wait()
    into_groups(mm(normed, weights[1]).astype(BF16), key_ref)
    key_ref.send()
    times_copy.wait()
    line = lax.broadcasted_iota(jnp.int32, times.shape, 0)
    chosen = jnp.where(line == step % 8, times[...].astype(F32), 0.0)
    embed = jnp.broadcast_to(jnp.sum(chosen, axis=0, keepdims=True), times.shape)
    embed_ref[...] = embed
    embed = embed.astype(BF16)
    copies[3].wait()
    into_groups((query + mm(embed, weights[3])[0:1]).astype(BF16), query_ref)
    query_ref.send()
    copies[2].wait()
    value = mm(normed, weights[2])
    copies[4].wait()
    into_groups((value + mm(embed, weights[4])[0:1]).astype(BF16), value_ref)
    value_ref.send()

    def one_group(group, carry):
        tiles = [None] * (query_ref.shape[2] // LANES)
        for slot in range(slots):
            head = group * slots + slot
            first, lanes, offset = head_window(slot, head_width)
            mask = head_mask(lanes, offset, head_width)
            window = windows[head]
            blocks = [None] * side
            steps = LANES // side
            for turn in range(steps):
                turned = window
                if turn:
                    turned = pltpu.roll(window, span_lanes - turn * side, 1)
                for jump in range(-(-side // steps)):
                    block = side - 1 - (jump * steps + turn)
                    if block >= 0:
                        blocks[block] = turned[:, jump * LANES : jump * LANES + length]
            bias = jnp.concatenate(blocks, axis=0)
            keys = key_ref[group, :, first : first + lanes]
            queries = query_ref[group, :, first : first + lanes] * mask
            scores = mm_nt(keys, queries) * scale + bias
            weights_now = jnp.exp(scores - jnp.max(scores, axis=0, keepdims=True))
            totals = jnp.sum(weights_now, axis=0, keepdims=True)
            probs = (weights_now * (1.0 / totals)).astype(BF16)
            probs_ref[head] = probs
            values = value_ref[group, :, first : first + lanes] * mask
            add_tiles(tiles, mm_tn(probs, values), first)
        mixed_ref[group] = jnp.concatenate(tiles, axis=1).astype(BF16)
        probs_ref.send_rows(group * slots, slots)
        return carry

    lax.fori_loop(0, groups, one_group, 0)
    for group in range(groups):
        flat[:, group * group_width : (group + 1) * group_width] = mixed_ref[group][:, :group_width]
    for away in (2, 3):
        mixed_far[away - 2] = mixed_ref[rank ^ away]
    mixed_far.send()
    mixed_1[...] = mixed_ref[rank ^ 1]
    mixed_1.send()
    mixed_0[...] = mixed_ref[rank]
    mixed_0.send()
    copies[5].wait()
    middle = own + mm(flat[...], weights[5]) + row_of(out_bias)
    middle_ref[...] = middle
    middle_ref.send()
    unit, _ = unit_rows(middle)
    normed_ref[...] = (unit * row_of(second_gain) + row_of(second_shift)).astype(BF16)


def normed_kernel(side, ranks, relative_ref, tokens_ref, gain, shift, normed_ref):
    unit, _ = unit_rows(mm(place_matrix(relative_ref[0:1, :], side), tokens_ref[...]))
    normed_ref[...] = (unit * row_of(gain) + row_of(shift)).astype(BF16)


def gelu_pair(hidden):
    root = math.sqrt(2.0 / math.pi)
    square = hidden * hidden
    bend = jnp.tanh(hidden * (root + (root * 0.044715) * square))
    half = 0.5 + 0.5 * bend
    slope = half + (0.5 * hidden) * (1.0 - bend * bend) * (root + (3.0 * root * 0.044715) * square)
    return hidden * half, slope


def feed_rows(side, relative_ref, normed, cotangent, up_ref, up_bias, down_ref, active, hidden, moved):
    place = place_matrix(relative_ref[0:1, :], side)
    rows = place.shape[0]
    for chunk in range(len(normed)):
        span = slice(chunk * rows, (chunk + 1) * rows)
        turned = mm(place, cotangent[chunk][...]).astype(BF16)
        moved[span, :] = turned
        gelu_out, slope = gelu_pair(mm(normed[chunk][...], up_ref[...]) + row_of(up_bias))
        active[span, :] = gelu_out.astype(BF16)
        hidden[span, :] = (mm_nt(turned, down_ref[...]) * slope).astype(BF16)


def feed_near_kernel(
    side,
    relative_ref,
    normed_own,
    normed_near,
    cot_own,
    cot_near,
    up_ref,
    up_bias,
    down_ref,
    active,
    hidden,
    moved,
    grad_own,
    grad_near,
):
    feed_rows(
        side,
        relative_ref,
        (normed_own, normed_near),
        (cot_own, cot_near),
        up_ref,
        up_bias,
        down_ref,
        active,
        hidden,
        moved,
    )
    active.send()
    moved.send()
    hidden.send()
    rows = grad_own.shape[0]
    grad_near[...] = mm_nt(hidden[rows:, :], up_ref[...]).astype(BF16)
    grad_near.send()
    grad_own[...] = mm_nt(hidden[:rows, :], up_ref[...]).astype(BF16)


def halves(values, bit):
    half = values.shape[0] // 2
    low, high = values[:half], values[half:]
    return jnp.where(bit == 0, low, high), jnp.where(bit == 0, high, low)


def feed_far_kernel(
    side,
    relative_ref,
    normed_far,
    normed_last,
    cot_far,
    cot_last,
    up_ref,
    up_bias,
    down_ref,
    near_hidden,
    active,
    hidden,
    moved,
    grad_far,
    grad_last,
    bias_ref,
):
    feed_rows(
        side,
        relative_ref,
        (normed_far, normed_last),
        (cot_far, cot_last),
        up_ref,
        up_bias,
        down_ref,
        active,
        hidden,
        moved,
    )
    rows = grad_far.shape[0]
    grad_last[...] = mm_nt(hidden[rows:, :], up_ref[...]).astype(BF16)
    grad_far[...] = mm_nt(hidden[:rows, :], up_ref[...]).astype(BF16)
    total = jnp.sum(hidden[...].astype(F32), axis=0, keepdims=True)
    total = total + jnp.sum(near_hidden[...].astype(F32), axis=0, keepdims=True)
    bias_ref[...] = jnp.broadcast_to(total, bias_ref.shape)


def down_grad_kernel(level, ranks, near_active, near_moved, active, moved, keep_ref, send_ref):
    grad = mm_tn(near_active[...], near_moved[...]) + mm_tn(active[...], moved[...])
    keep, send = halves(grad.astype(BF16), (ranks[1] >> level) & 1)
    send_ref[...] = send
    keep_ref[...] = keep


def up_grad_kernel(
    level, ranks, own, near, far, last, near_hidden, hidden, keep_ref, send_ref, normed
):
    rows = own.shape[0]
    for chunk, ref in enumerate((own, near, far, last)):
        normed[chunk * rows : (chunk + 1) * rows, :] = ref[...]
    grad = mm_tn(normed[: 2 * rows, :], near_hidden[...]) + mm_tn(normed[2 * rows :, :], hidden[...])
    keep, send = halves(grad.astype(BF16), (ranks[1] >> level) & 1)
    send_ref[...] = send
    send_ref.send()
    keep_ref[...] = keep


def out_kernel(near_active, active, down_ref, keep_ref, send_ref):
    rows = keep_ref.shape[1]
    keep_ref[0] = mm(near_active[:rows, :], down_ref[...]).astype(BF16)
    send_ref[0] = mm(near_active[rows:, :], down_ref[...]).astype(BF16)
    keep_ref[1] = mm(active[:rows, :], down_ref[...]).astype(BF16)
    send_ref[1] = mm(active[rows:, :], down_ref[...]).astype(BF16)


def add_kernel(left, right, out_ref):
    out_ref[...] = (left[...].astype(F32) + right[...].astype(F32)).astype(out_ref.dtype)


def middle_kernel(
    own_ref,
    near_ref,
    far_ref,
    middle_ref,
    moved_ref,
    gain,
    branch_ref,
    grad_ref,
    sums_ref,
):
    rows = own_ref.shape[0]
    grad_normed = own_ref[...].astype(F32) + near_ref[...].astype(F32) + far_ref[...].astype(F32)
    unit, inverse = unit_rows(middle_ref[...])
    cotangent = moved_ref[:rows, :].astype(F32)
    grad_middle = cotangent + norm_back(grad_normed, unit, inverse, row_of(gain))
    branch_ref[...] = grad_middle.astype(BF16)
    branch_ref.send()
    grad_ref[...] = grad_middle
    grad_ref.send()
    sums_ref[...] = jnp.zeros(sums_ref.shape, F32)
    sums_ref[0:1, :] = jnp.sum(grad_normed * unit, axis=0, keepdims=True)
    sums_ref[1:2, :] = jnp.sum(grad_normed, axis=0, keepdims=True)
    sums_ref[2:3, :] = jnp.sum(grad_middle, axis=0, keepdims=True)
    sums_ref[3:4, :] = jnp.sum(cotangent, axis=0, keepdims=True)


def attend_back_kernel(
    dims,
    picks,
    ranks,
    *refs,
):
    groups, slots, head_width, side, scale = dims
    group_width = slots * head_width
    rank = ranks[0]
    length = side * side
    hbm = refs[1:5] if len(refs) == 14 else refs[2:6]
    nows = refs[-5:-1]

    def fetch(pick, item):
        group = (picks[0] + pick) ^ rank
        source = hbm[item].at[pl.ds(group * slots, slots)] if item == 3 else hbm[item].at[group]
        return pltpu.make_async_copy(source, nows[item].at[pick], refs[-1].at[pick, item])

    for pick in range(2):
        for item in (3, 2, 0, 1):
            fetch(pick, item).start()
    if len(refs) == 15:
        branch_ref, out_ref = refs[:2]
        packed_far, grads, grad_mixed, sheared, query_now, key_now, value_now, probs_now, _ = refs[6:]
        packed_all = [packed_far.ref.at[0], packed_far.ref.at[1]]
        fill = jnp.zeros((length, grad_mixed.shape[2] - group_width), BF16)
        product = mm_nt(branch_ref[...], out_ref[...]).astype(BF16)
        for group in range(groups):
            piece = product[:, group * group_width : (group + 1) * group_width]
            grad_mixed[group] = jnp.concatenate([piece, fill], axis=1)
        grad_mixed.send()
    else:
        grad_mixed = refs[0]
        packed_a, packed_b, grads, sheared, query_now, key_now, value_now, probs_now, _ = refs[5:]
        packed_all = [packed_a.ref, packed_b.ref]
        grad_mixed.ready()
    stride = 2 * side - 1
    span_lanes = sheared.shape[2]
    packed_lanes = packed_all[0].shape[1]
    table_lanes = round_up(stride * stride, LANES)

    def one_group(pick, carry):
        group = (picks[0] + pick) ^ rank
        for item in range(4):
            fetch(pick, item).wait()
        wide = grad_mixed.shape[2] // LANES
        query_tiles, key_tiles, value_tiles = [None] * wide, [None] * wide, [None] * wide
        for slot in range(slots):
            first, lanes, offset = head_window(slot, head_width)
            mask = head_mask(lanes, offset, head_width)
            span = slice(first, first + lanes)
            mixed_now = grad_mixed[group, :, span] * mask
            probs = probs_now[pick, slot]
            grad_probs = mm_nt(value_now[pick, :, span], mixed_now)
            probs_wide = probs.astype(F32)
            weighted = probs_wide * grad_probs
            grad_scores = weighted - probs_wide * jnp.sum(weighted, axis=0, keepdims=True)
            rounded = grad_scores.astype(BF16)
            add_tiles(value_tiles, mm(probs, mixed_now), first)
            add_tiles(key_tiles, mm(rounded, query_now[pick, :, span] * mask), first)
            add_tiles(query_tiles, mm_tn(rounded, key_now[pick, :, span] * mask), first)
            steps = LANES // side
            shear = jnp.zeros((side, span_lanes), F32)
            for turn in range(steps):
                summed = None
                for jump in range(-(-side // steps)):
                    block = side - 1 - (jump * steps + turn)
                    if block >= 0:
                        piece = grad_scores[block * side : (block + 1) * side, :]
                        parts = []
                        if jump:
                            parts.append(jnp.zeros((side, jump * LANES), F32))
                        parts.append(piece)
                        rest = span_lanes - jump * LANES - length
                        if rest:
                            parts.append(jnp.zeros((side, rest), F32))
                        piece = jnp.concatenate(parts, axis=1)
                        summed = piece if summed is None else summed + piece
                shear = shear + (pltpu.roll(summed, turn * side, 1) if turn else summed)
            sheared[:, pl.ds(pick * slots + slot, 1), :] = shear[:, None, :]
        query = (jnp.concatenate(query_tiles, axis=1) * scale).astype(BF16)
        key = (jnp.concatenate(key_tiles, axis=1) * scale).astype(BF16)
        value = jnp.concatenate(value_tiles, axis=1).astype(BF16)
        grads[0, pick] = query
        grads[1, pick] = key
        grads[2, pick] = value
        return carry

    lax.fori_loop(0, len(picks), one_group, 0)
    selections = [squeeze_part(part, side, stride) for part in range(span_lanes // LANES)]
    heads = 2 * slots
    tall = table_lanes // LANES
    total = [jnp.zeros((heads, LANES), F32)] * tall
    for column in range(side):
        high, low = split_two(sheared[column])
        tiles = [None] * tall
        for part, (first, lanes, squeeze) in enumerate(selections):
            span = slice(part * LANES, (part + 1) * LANES)
            add_tiles(tiles, mm_nt(high[:, span], squeeze) + mm_nt(low[:, span], squeeze), first)
        spread = jnp.concatenate(
            [jnp.zeros((heads, LANES), F32) if tile is None else tile for tile in tiles], axis=1
        )
        turn = side - 1 - column
        turned = pltpu.roll(spread, turn, 1) if turn else spread
        total = [
            old + turned[:, place * LANES : (place + 1) * LANES] for place, old in enumerate(total)
        ]
    for pick, packed_ref in enumerate(packed_all):
        for place in range(tall):
            packed_ref[length + place * slots : length + (place + 1) * slots, :LANES] = total[place][
                pick * slots : (pick + 1) * slots
            ].astype(BF16)
        pieces = [grads[item, pick][:, :group_width] for item in range(3)]
        if packed_lanes > 3 * group_width:
            pieces.append(jnp.zeros((length, packed_lanes - 3 * group_width), BF16))
        packed_ref[:length, :] = jnp.concatenate(pieces, axis=1)


def tokens_kernel(
    dims,
    ranks,
    near_grads,
    far_grads,
    query_ref,
    key_ref,
    value_ref,
    relative_ref,
    gain,
    middle_ref,
    middle_sums,
    tokens_hbm,
    image_ref,
    grad_ref,
    flat,
    own_tokens,
    sem,
):
    groups, slots, head_width, side, scale = dims
    group_width = slots * head_width
    rank = ranks[0]
    length = side * side
    own_copy = pltpu.make_async_copy(
        tokens_hbm.at[pl.ds(pl.multiple_of(rank * length, length), length)], own_tokens, sem
    )
    own_copy.start()
    for group in range(groups):
        away = group ^ rank
        for item in range(3):
            piece = jnp.where(away >= 2, far_grads[item, away & 1], near_grads[item, away & 1])
            flat[item, :, group * group_width : (group + 1) * group_width] = piece[:, :group_width]
    grad_normed = (
        mm_nt(flat[0], query_ref[...])
        + mm_nt(flat[1], key_ref[...])
        + mm_nt(flat[2], value_ref[...])
    )
    place = place_matrix(relative_ref[0:1, :], side)
    own_copy.wait()
    unit, inverse = unit_rows(mm(place, own_tokens[...]))
    total = middle_ref[...] + norm_back(grad_normed, unit, inverse, row_of(gain))
    high, low = split_two(total)
    grad_ref[...] = mm_tn(place, high) + mm_tn(place, low)
    grad_ref.send()
    sums = [
        jnp.sum(flat[0].astype(F32), axis=0, keepdims=True),
        jnp.sum(flat[2].astype(F32), axis=0, keepdims=True),
        jnp.sum(grad_normed * unit, axis=0, keepdims=True),
        jnp.sum(grad_normed, axis=0, keepdims=True),
        middle_sums[0:4, :],
    ]
    image_ref[...] = jnp.concatenate(sums, axis=0)
    image_ref.send()


def own_columns(rows, rank, groups):
    columns = rows.shape[1] // groups
    chosen = rows[:, :columns]
    for group in range(1, groups):
        chosen = jnp.where(rank == group, rows[:, group * columns : (group + 1) * columns], chosen)
    return chosen


def weights_kernel(dims, level, ranks, steps_ref, normed, *refs):
    groups, slots, head_width, side, scale = dims
    group_width = slots * head_width
    rows = side * side
    rank = ranks[0]
    lines_own, lines_far, lines_near, up_bias_ref, query_hbm, value_hbm = refs[
        3 * groups : 3 * groups + 6
    ]
    keep_first, keep_second, send_first, send_second = refs[3 * groups + 6 : 3 * groups + 10]
    packed, branch, mixed, tail, times, sems = refs[3 * groups + 10 :]
    start = pl.multiple_of(rank * group_width, 16)
    copies = []
    for item, source in enumerate((query_hbm, value_hbm)):
        copies.append(
            pltpu.make_async_copy(
                source.at[pl.ds(start, group_width)], times.at[item], sems.at[item]
            )
        )
        copies[item].start()
    table = None
    for chunk in range(groups):
        span = slice(chunk * rows, (chunk + 1) * rows)
        source, other = refs[chunk].ref, refs[2 * groups + chunk].ref
        if chunk >= 2:
            source, other = source.at[chunk - 2], other.at[chunk - 2]
        packed[span, :] = source[:rows, :]
        branch[span, :] = refs[groups + chunk][...]
        mixed[span, :] = other[...]
        part = source[rows:, :LANES].astype(F32)
        table = part if table is None else table + part
    bit = (ranks[1] >> level) & 1
    left = mm_tn(packed[...], normed[...]).astype(BF16)
    right = mm_tn(mixed[...], branch[...]).astype(BF16)
    value, out = left[2 * group_width : 3 * group_width], right[:group_width]
    keep_second[...] = jnp.where(bit == 0, value, out)
    send_second[...] = jnp.where(bit == 0, out, value)

    lines = [lines_own[...], lines_near[:8, :], lines_far[...], lines_near[8:, :]]
    embed = None
    for item in range(2):
        both = jnp.concatenate([line[item : item + 1, :] for line in lines] * 2, axis=0)
        high = both.astype(BF16).astype(F32)
        place = lax.broadcasted_iota(jnp.int32, both.shape, 0)
        both = jnp.where(place < groups, high, both - high).astype(BF16)
        copies[item].wait()
        product = mm_nt(both, times[item])
        product = product[:groups] + product[groups:]
        embed = product if embed is None else embed + product
    tail[...] = jnp.zeros_like(tail)
    tail[: table.shape[0], :LANES] = table
    each = group_width // 2
    for chunk in range(groups):
        total = jnp.sum(packed[chunk * rows : (chunk + 1) * rows, :].astype(F32), axis=0, keepdims=True)
        step = steps_ref[rank ^ chunk]
        fill = tail.shape[1] - LANES - 3 * group_width - 16
        line = [
            total[:, :group_width],
            total[:, 2 * group_width : 3 * group_width],
            embed[chunk : chunk + 1, :],
            jnp.zeros((1, fill), F32),
            jnp.full((1, 8), (step // 8).astype(F32)),
            jnp.full((1, 8), (step % 8).astype(F32)),
        ]
        image = ranks[1] * groups + (rank ^ chunk)
        tail[pl.ds(image, 1), LANES:] = jnp.concatenate(line, axis=1)
    vectors = lines[0] + lines[1] + lines[2] + lines[3]
    vectors = [own_columns(vectors[item : item + 1, :], rank, groups) for item in range(2, 8)]
    vectors += [
        up_bias_ref[0:1, part * group_width : (part + 1) * group_width]
        for part in range(up_bias_ref.shape[1] // group_width)
    ]
    first = LANES + 3 * group_width
    for item, vector in enumerate(vectors):
        tail[2 * item : 2 * item + 1, first : first + each] = vector[:, :each]
        tail[2 * item + 1 : 2 * item + 2, first : first + each] = vector[:, each:]
    keep, send = halves(left[: 2 * group_width], bit)
    keep_first[:group_width, :] = keep
    send_first[:group_width, :] = send
    keep, send = halves(tail[...].astype(BF16), bit)
    keep_first[group_width:, :] = keep
    send_first[group_width:, :] = send


def split_kernel(level, tail, ranks, kept, got, keep_ref, send_ref):
    total = (kept[...].astype(F32) + got[...].astype(F32)).astype(BF16)
    bit = (ranks[1] >> level) & 1
    body = total.shape[0] - tail
    keep, send = halves(total[:body], bit)
    send_ref[: body // 2, :] = send
    keep_ref[: body // 2, :] = keep
    if tail:
        keep, send = halves(total[body:], bit)
        send_ref[body // 2 :, :] = send
        keep_ref[body // 2 :, :] = keep


def join_kernel(level, tail, ranks, own, other, out_ref):
    body = own.shape[0] - tail
    bit = (ranks[1] >> level) & 1
    low = jnp.where(bit == 0, own[...], other[...])
    high = jnp.where(bit == 0, other[...], own[...])
    out_ref[:body, :] = low[:body]
    out_ref[body : 2 * body, :] = high[:body]
    if tail:
        out_ref[2 * body : 2 * body + tail, :] = low[body:]
        out_ref[2 * body + tail :, :] = high[body:]


def widen_kernel(level, cross, each, ranks, own, other, out_ref):
    bit = (ranks[1] >> level) & 1
    block = pl.program_id(0) // each
    first = (block % 2 if cross else block // 2) == bit

    @pl.when(first)
    def _():
        out_ref[...] = own[...].astype(F32)

    @pl.when(jnp.logical_not(first))
    def _():
        out_ref[...] = other[...].astype(F32)


def widen_pair_kernel(level, ranks, own, other, low_ref, high_ref, tail_ref):
    bit = (ranks[1] >> level) & 1
    low = jnp.where(bit == 0, own[...], other[...]).astype(F32)
    high = jnp.where(bit == 0, other[...], own[...]).astype(F32)
    body, half = low_ref.shape[0], tail_ref.shape[0] // 2
    tail_ref[:half, :] = low[body:]
    tail_ref[half:, :] = high[body:]
    low_ref[...] = low[:body]
    low_ref.send()
    high_ref[...] = high[:body]


def widen_cross_kernel(level, ranks, own, other, low_ref, high_ref):
    bit = (ranks[1] >> level) & 1
    body = own.shape[0] // 2
    even = jnp.where(bit == 0, own[...], other[...]).astype(F32)
    odd = jnp.where(bit == 0, other[...], own[...]).astype(F32)
    low_ref[:body, :] = even[:body]
    low_ref[body:, :] = odd[:body]
    low_ref.send()
    high_ref[:body, :] = even[body:]
    high_ref[body:, :] = odd[body:]


def finish_kernel(
    dims, images, tail, times, query_ref, value_ref, table_ref, bias_ref, sums_ref
):
    groups, slots, head_width, side, scale = dims
    group_width = slots * head_width
    for part in range(bias_ref.shape[1] // LANES):
        bias_ref[:, part * LANES : (part + 1) * LANES] = tail[
            part * slots : (part + 1) * slots, :LANES
        ]
    each = group_width // 2
    first = LANES + 3 * group_width
    sums_ref[...] = jnp.zeros(sums_ref.shape, F32)
    for item in range(10):
        for part in range(2):
            row = 2 * item + part
            sums_ref[item : item + 1, part * each : (part + 1) * each] = tail[
                row : row + 1, first : first + each
            ]
    last = tail.shape[1]
    steps = tail[:images, last - 16 : last - 15] * 8.0 + tail[:images, last - 8 : last - 7]
    step = lax.broadcasted_iota(jnp.int32, (images, table_ref.shape[1]), 1)
    chosen = jnp.where(step == steps.astype(jnp.int32), 1.0, 0.0).astype(BF16)
    total = tail[:images, LANES + 2 * group_width : LANES + 3 * group_width].astype(BF16)
    table_ref[...] = mm_tn(total, chosen)
    table_ref.send()
    embed = mm(chosen, times[...]).astype(BF16)
    for item, target in enumerate((query_ref, value_ref)):
        rows = tail[:images, LANES + item * group_width : LANES + (item + 1) * group_width]
        target[...] = mm_tn(rows.astype(BF16), embed)
        target.send()


def block_kernel(side, relative_ref, own, near, far, middle_ref, bias, out_ref):
    total = own[0].astype(F32) + near[0].astype(F32) + far[...].astype(F32)
    total = (middle_ref[...] + total + row_of(bias)).astype(BF16)
    place = place_matrix(relative_ref[0:1, :], side)
    out_ref[...] = mm_tn(place, total).astype(BF16)


def shape_of(*sizes, dtype=BF16):
    return jax.ShapeDtypeStruct(sizes, dtype)


VMEM = pl.BlockSpec(memory_space=pltpu.VMEM)
HBM = pl.BlockSpec(memory_space=pl.ANY)
SMEM = pl.BlockSpec(memory_space=pltpu.SMEM)
MIB = 1024 * 1024
FEED = 16


def cost(us):
    return pl.CostEstimate(flops=int(us * PACE * 1.15e9), bytes_accessed=1000, transcendentals=0)


class Staged:
    def __init__(self, source, target, sem):
        self.ref, self.waited = target, False
        self.copy = pltpu.make_async_copy(source, target, sem)
        self.copy.start()
        self.shape = target.shape

    def ready(self):
        if not self.waited:
            self.waited = True
            self.copy.wait()
        return self.ref

    def __getitem__(self, place):
        return self.ready()[place]


class Result:
    def __init__(self, ref, target=None, sem=None):
        self.ref, self.sent = ref, target is None
        self.copy = None if self.sent else pltpu.make_async_copy(ref, target, sem)
        self.shape, self.dtype = ref.shape, ref.dtype
        self.target, self.sem = target, sem

    def send_rows(self, start, count):
        self.sent = True
        rows = pl.ds(start, count)
        pltpu.make_async_copy(self.ref.at[rows], self.target.at[rows], self.sem).start()

    def __getitem__(self, place):
        return self.ref[place]

    def __setitem__(self, place, value):
        self.ref[place] = value

    def send(self):
        if not self.sent:
            self.sent = True
            self.copy.start()


class Held:
    def __init__(self, ref):
        self.ref, self.shape = ref, ref.shape

    def ready(self):
        return self.ref

    def __getitem__(self, place):
        return self.ref[place]


def run(kernel, outs, inputs, kinds=None, scratch=(), deps=(), us=2.5, away=(), vmem=16):
    kinds = "v" * len(inputs) if kinds is None else kinds
    assert len(kinds) == len(inputs)
    single = not isinstance(outs, (list, tuple))
    outs = [outs] if single else list(outs)
    staged = [place for place, kind in enumerate(kinds) if kind == "w"]
    count, results = len(inputs), len(outs)
    if deps:
        inputs = [after(inputs[0], *deps), *inputs[1:]]
    buffers = [pltpu.VMEM(inputs[place].shape, inputs[place].dtype) for place in staged]
    buffers += [pltpu.VMEM(outs[place].shape, outs[place].dtype) for place in away]
    if buffers:
        buffers.append(pltpu.SemaphoreType.DMA((len(buffers),)))

    def body(*refs):
        given = list(refs[:count])
        targets = refs[count : count + results]
        rest = refs[count + results :]
        for place, kind in enumerate(kinds):
            if kind == "v":
                given[place] = Held(given[place])
        for order, place in enumerate(staged):
            sem = rest[len(buffers) - 1].at[order]
            given[place] = Staged(given[place], rest[order], sem)
        made = []
        for place, target in enumerate(targets):
            if place in away:
                order = len(staged) + away.index(place)
                made.append(Result(rest[order], target, rest[len(buffers) - 1].at[order]))
            else:
                made.append(Result(target))
        kernel(*given, *made, *rest[len(buffers) :])
        for result in made:
            result.send()
        for place in staged:
            given[place].ready()
        for result in made:
            if result.copy is not None:
                result.copy.wait()

    space = {"s": SMEM, "h": HBM, "v": VMEM, "w": HBM}
    found = pl.pallas_call(
        body,
        out_shape=outs,
        in_specs=[space[kind] for kind in kinds],
        out_specs=[HBM if place in away else VMEM for place in range(results)],
        scratch_shapes=buffers + list(scratch),
        compiler_params=pltpu.CompilerParams(vmem_limit_bytes=vmem * MIB),
        cost_estimate=cost(us),
    )(*inputs)
    return found[0] if single else found


def quick(kernel, outs, inputs, deps=()):
    if deps:
        inputs = [after(inputs[0], *deps), *inputs[1:]]
    return pl.pallas_call(
        kernel,
        out_shape=outs,
        in_specs=[SMEM if given.shape == (2,) else VMEM for given in inputs],
        out_specs=jax.tree.map(lambda _: VMEM, outs),
        compiler_params=pltpu.CompilerParams(vmem_limit_bytes=4 * MIB),
        cost_estimate=cost(1.2),
    )(*inputs)


def widen(ranks, level, own, other, last, cross=False):
    half, columns = own.shape
    each = 2
    block = half // (2 * each)
    parts = 4 * each

    def place_of(i, bit):
        quarter, inner = i // each, i % each
        if cross:
            return ((quarter // 2) * each + inner, 0)
        return (jnp.clip(i - 2 * each * bit, 0, 2 * each - 1), 0)

    def own_map(i, me):
        return place_of(i, (me[1] >> level) & 1)

    def other_map(i, me):
        return place_of(i, 1 - ((me[1] >> level) & 1))

    return pl.pallas_call(
        partial(widen_kernel, level, cross, each),
        out_shape=shape_of(2 * half, columns, dtype=F32),
        grid_spec=pltpu.PrefetchScalarGridSpec(
            num_scalar_prefetch=1,
            grid=(parts,),
            in_specs=[
                pl.BlockSpec((block, columns), own_map),
                pl.BlockSpec((block, columns), other_map),
            ],
            out_specs=pl.BlockSpec((block, columns), lambda i, me: (i, 0)),
        ),
        compiler_params=pltpu.CompilerParams(vmem_limit_bytes=16 * MIB),
        cost_estimate=cost(3.5),
    )(after(ranks, last), own, other)


def swap(array, axis, distance):
    size = lax.axis_size(axis)
    return lax.ppermute(array, axis, [(i, i ^ distance) for i in range(size)])


def after(array, *others):
    return lax.optimization_barrier((array, *others))[0]


class Total:
    def __init__(self, ranks, order, keep, send, tail=0, cross=False):
        self.ranks, self.order, self.tail = ranks, order, tail
        self.back = (0, 1) if cross else (1, 0)
        self.keep = keep
        self.got = self.swap(0, send)

    def swap(self, place, array):
        return swap(array, "dp", 1 << self.order[place])

    def split(self, deps=()):
        half, columns = self.keep.shape
        part = shape_of(half // 2, columns)
        self.keep, send = quick(
            partial(split_kernel, self.order[1], self.tail),
            [part, part],
            [self.ranks, self.keep, self.got],
            deps,
        )
        self.got = self.swap(1, send)
        return self.keep

    def add(self, place, deps=()):
        self.keep = quick(add_kernel, shape_of(*self.keep.shape), [self.keep, self.got], deps)
        self.got = self.swap(place, self.keep)
        return self.keep

    def join(self, deps=()):
        half, columns = self.keep.shape
        self.keep = quick(
            partial(join_kernel, self.order[self.back[0]], self.tail // 2),
            shape_of(2 * half, columns),
            [self.ranks, self.keep, self.got],
            deps,
        )
        self.got = self.swap(self.back[1], self.keep)
        return self.keep

    def exchange(self, deps=()):
        for place in range(2, len(self.order)):
            self.add(place, deps)
        return self.keep

    def finish(self, deps=()):
        return self.add(self.back[0], deps)


def add_low(left, right):
    return (left.astype(F32) + right.astype(F32)).astype(BF16)


def on_device(
    tokens,
    timesteps,
    relative_index,
    time_table,
    query_weight,
    key_weight,
    value_weight,
    time_query_weight,
    time_value_weight,
    out_weight,
    out_bias,
    first_gain,
    first_shift,
    second_gain,
    second_shift,
    up_weight,
    up_bias,
    down_weight,
    down_bias,
    bias_table,
    cotangent,
):
    length = relative_index.shape[0]
    width = tokens.shape[1]
    heads = bias_table.shape[1]
    head_width = width // heads
    side = math.isqrt(length)
    stride = 2 * side - 1
    groups = lax.axis_size("mp")
    dp_size = lax.axis_size("dp")
    rank = lax.axis_index("mp")
    ranks = jnp.stack([rank, lax.axis_index("dp")]).astype(jnp.int32)
    slots = heads // groups
    group_width = slots * head_width
    group_lanes = round_up(group_width, LANES)
    packed_lanes = round_up(3 * group_width, LANES)
    table_lanes = round_up(stride * stride, LANES)
    span_lanes = round_up(stride * side, LANES)
    hidden_width = up_weight.shape[1]
    rows = groups * length
    dims = (groups, slots, head_width, side, head_width ** (-0.5))
    levels = list(range(dp_size.bit_length() - 1))
    other_order = levels[1::-1] + levels[2:]

    def grouped():
        return shape_of(groups, length, group_lanes)

    one_group = shape_of(length, group_lanes)

    cot_near = swap(cotangent, "mp", 1)
    cot_far = swap(cotangent, "mp", 2)
    steps = time_table.shape[0]
    outs = run(
        partial(attend_kernel, dims),
        [
            grouped(),
            grouped(),
            grouped(),
            shape_of(heads, length, length),
            one_group,
            one_group,
            shape_of(2, length, group_lanes),
            shape_of(length, width, dtype=F32),
            shape_of(length, width),
            shape_of(8, width, dtype=F32),
        ],
        [
            ranks,
            timesteps,
            relative_index,
            bias_table.T,
            first_gain,
            first_shift,
            second_gain,
            second_shift,
            out_bias,
            tokens,
            time_table.reshape(steps // 8, 8, width),
            query_weight,
            key_weight,
            value_weight,
            time_query_weight,
            time_value_weight,
            out_weight,
        ],
        "sswwwwwww" + "h" * 8,
        [
            pltpu.VMEM((6, width, width), BF16),
            pltpu.VMEM((length, width), BF16),
            pltpu.VMEM((8, width), BF16),
            pltpu.VMEM((heads, table_lanes), F32),
            pltpu.VMEM((heads * side, table_lanes), BF16),
            pltpu.VMEM((heads * side, table_lanes), BF16),
            pltpu.VMEM((heads, side, span_lanes), F32),
            pltpu.VMEM((length, width), BF16),
            pltpu.VMEM((groups, length, group_lanes), BF16),
            pltpu.SemaphoreType.DMA((8,)),
        ],
        us=60.0,
        away=(0, 1, 2, 3, 4, 5, 6, 7),
        vmem=56,
    )
    query_rows, key_rows, value_rows, probs = outs[:4]
    mixed_own, mixed_near, mixed_far, middle, normed_own, embed = outs[4:]
    normed_near = swap(normed_own, "mp", 1)
    normed_far = swap(normed_own, "mp", 2)

    normed_first = pl.pallas_call(
        partial(normed_kernel, side),
        out_shape=shape_of(rows, width),
        grid_spec=pltpu.PrefetchScalarGridSpec(
            num_scalar_prefetch=1,
            grid=(groups,),
            in_specs=[
                pl.BlockSpec((8, length), lambda i, me: (0, 0)),
                pl.BlockSpec((length, width), lambda i, me: (i ^ me[0], 0)),
                VMEM,
                VMEM,
            ],
            out_specs=pl.BlockSpec((length, width), lambda i, me: (i, 0)),
        ),
        compiler_params=pltpu.CompilerParams(vmem_limit_bytes=40 * MIB),
        cost_estimate=cost(4.0),
    )(after(ranks, normed_own, cot_far), relative_index, tokens, first_gain, first_shift)

    cot_last = swap(after(cot_far, normed_own), "mp", 1)
    pair = shape_of(2 * length, width)
    hidden_pair = shape_of(2 * length, hidden_width)
    chunk = shape_of(length, width)
    near_active, near_hidden, near_moved, grad_own, grad_near = run(
        partial(feed_near_kernel, side),
        [hidden_pair, hidden_pair, pair, chunk, chunk],
        [
            relative_index,
            normed_own,
            normed_near,
            cotangent,
            cot_near,
            up_weight,
            up_bias,
            down_weight,
        ],
        "vvvvvwvw",
        deps=[normed_first, cot_last],
        us=7.2,
        vmem=FEED,
    )
    near_got = swap(grad_near, "mp", 1)
    normed_last = swap(after(normed_far, grad_near), "mp", 1)
    mixed_far = swap(mixed_far, "mp", 2)
    active, hidden, moved, grad_far, grad_last, up_bias_sum = run(
        partial(feed_far_kernel, side),
        [hidden_pair, hidden_pair, pair, chunk, chunk, shape_of(8, hidden_width, dtype=F32)],
        [
            relative_index,
            normed_far,
            normed_last,
            cot_far,
            cot_last,
            up_weight,
            up_bias,
            down_weight,
            near_hidden,
        ],
        "vvvvvwvwv",
        us=7.5,
        deps=[near_got],
        vmem=FEED,
    )
    last_got = swap(grad_last, "mp", 1)
    half = shape_of(hidden_width // 2, width)
    keep, send = run(
        partial(down_grad_kernel, levels[0]),
        [half, half],
        [ranks, near_active, near_moved, active, moved],
        "svvvv",
        deps=[up_bias_sum, mixed_far],
        us=14.0,
        vmem=FEED,
    )
    down = Total(ranks, levels, keep, send)
    grad_sent = run(add_kernel, chunk, [grad_far, last_got], deps=[keep], vmem=4)
    far_got = swap(grad_sent, "mp", 2)
    mixed_last = swap(after(mixed_far, grad_sent), "mp", 1)
    mixed_near = swap(after(mixed_near, grad_sent), "mp", 1)
    half = shape_of(width // 2, hidden_width)
    keep, send = run(
        partial(up_grad_kernel, other_order[0]),
        [half, half],
        [ranks, normed_own, normed_near, normed_far, normed_last, near_hidden, hidden],
        "s" + "v" * 6,
        [pltpu.VMEM((rows, width), BF16)],
        deps=[grad_sent],
        us=4.9,
        vmem=FEED,
    )
    up = Total(ranks, other_order, keep, send, cross=True)
    chunks = shape_of(2, length, width)
    out_keep, out_send = run(
        out_kernel, [chunks, chunks], [near_active, active, down_weight], "vvw", deps=[keep], us=5.0, vmem=FEED
    )
    out_got = swap(out_send, "mp", 1)
    grad_branch, grad_middle, middle_sums = run(
        middle_kernel,
        [chunk, shape_of(length, width, dtype=F32), shape_of(8, width, dtype=F32)],
        [grad_own, near_got, far_got, middle, near_moved, second_gain],
        "vvvvvw",
        deps=[out_keep],
        vmem=8,
    )
    branch_near = swap(grad_branch, "mp", 1)
    branch_far = swap(grad_branch, "mp", 2)
    last = middle_sums

    tail = slots * table_lanes // LANES
    two_groups = pltpu.VMEM((2, length, group_lanes), BF16)
    back_scratch = [
        pltpu.VMEM((side, 2 * slots, span_lanes), F32),
        two_groups,
        two_groups,
        two_groups,
        pltpu.VMEM((2, slots, length, length), BF16),
        pltpu.SemaphoreType.DMA((2, 4)),
    ]
    grads_shape = shape_of(3, 2, length, group_lanes)
    packed_shape = shape_of(length + tail, packed_lanes)
    packed_pair = shape_of(2, length + tail, packed_lanes)
    heads_in = [query_rows, key_rows, value_rows, probs]
    packed_far, far_grads, grad_mixed = run(
        partial(attend_back_kernel, dims, (2, 3)),
        [packed_pair, grads_shape, grouped()],
        [ranks, grad_branch, out_weight] + heads_in,
        "svwhhhh",
        back_scratch,
        deps=[last, mixed_last, mixed_near],
        us=8.3,
    )
    packed_far = swap(packed_far, "mp", 2)
    last = grad_mixed
    packed_0, packed_1, near_grads = run(
        partial(attend_back_kernel, dims, (0, 1)),
        [packed_shape, packed_shape, grads_shape],
        [ranks, grad_mixed] + heads_in,
        "svhhhh",
        back_scratch,
        deps=[last],
        us=8.3,
    )
    last = down.split([packed_0, branch_far])
    branch_last = swap(after(branch_far, last), "mp", 1)
    last = up.split([last])
    image_rows, tokens_grad = run(
        partial(tokens_kernel, dims),
        [shape_of(8, width, dtype=F32), shape_of(length, width, dtype=F32)],
        [
            ranks,
            near_grads,
            far_grads,
            query_weight,
            key_weight,
            value_weight,
            relative_index,
            first_gain,
            grad_middle,
            middle_sums,
            tokens,
        ],
        "svvwwwwwvvh",
        [
            pltpu.VMEM((3, length, width), BF16),
            pltpu.VMEM((length, width), BF16),
            pltpu.SemaphoreType.DMA,
        ],
        deps=[last, branch_last],
        us=8.6,
        away=(1,),
        vmem=24,
    )
    lines_far = swap(image_rows, "mp", 2)
    last = down.exchange([image_rows, packed_far, lines_far])
    lines_near = swap(jnp.concatenate([image_rows, lines_far], axis=0), "mp", 1)
    packed_last = swap(after(packed_far, last), "mp", 1)
    packed_1 = swap(after(packed_1, last), "mp", 1)
    half = shape_of(group_width, width)
    images = dp_size * groups
    tail_rows = max(tail, images)
    more = shape_of(group_width + tail_rows // 2, width)
    keep_first, keep_second, send_first, send_second = run(
        partial(weights_kernel, dims, levels[0]),
        [more, half, more, half],
        [ranks, timesteps, normed_first, packed_0, packed_1, packed_far, packed_last]
        + [grad_branch, branch_near, branch_far, branch_last]
        + [mixed_own, mixed_near, mixed_far, mixed_last]
        + [image_rows, lines_far, lines_near, up_bias_sum, time_query_weight, time_value_weight],
        "ss" + "v" * 17 + "hh",
        [
            pltpu.VMEM((rows, packed_lanes), BF16),
            pltpu.VMEM((rows, width), BF16),
            pltpu.VMEM((rows, group_lanes), BF16),
            pltpu.VMEM((tail_rows, width), F32),
            pltpu.VMEM((2, group_width, width), BF16),
            pltpu.SemaphoreType.DMA((2,)),
        ],
        deps=[last],
        us=5.2,
    )
    first = Total(ranks, levels, keep_first, send_first, tail_rows // 2)
    last = first.split([keep_second])
    second = Total(ranks, levels, keep_second, after(send_second, last), cross=True)
    last = down.finish([last])
    last = up.exchange([last])
    out_far = swap(add_low(out_keep[1], out_got[1]), "mp", 2)
    last = second.split([last])
    last = down.join([last])
    last = up.finish([last])
    last = first.exchange([last])
    last = up.join([last])
    last = first.finish([last])
    last = second.exchange([last])
    last = first.join([last])
    down_grad = widen(ranks, levels[0], down.keep, down.got, last)
    last = second.finish([down_grad])
    last = second.join([last])
    up_grad = widen(ranks, other_order[1], up.keep, up.got, last, cross=True)
    wide = shape_of(group_width, width, dtype=F32)
    query_grad, key_grad, tail_sums = run(
        partial(widen_pair_kernel, levels[0]),
        [wide, wide, shape_of(tail_rows, width, dtype=F32)],
        [ranks, first.keep, first.got],
        "svv",
        away=(0, 1),
        deps=[up_grad],
    )
    value_grad, out_grad = run(
        partial(widen_cross_kernel, levels[1]),
        [wide, wide],
        [ranks, second.keep, second.got],
        "svv",
        away=(0, 1),
        deps=[query_grad],
    )

    time_query_grad, time_value_grad, time_table_grad, table_grad, sums = run(
        partial(finish_kernel, dims, images),
        [
            shape_of(group_width, width, dtype=F32),
            shape_of(group_width, width, dtype=F32),
            shape_of(group_width, steps, dtype=F32),
            shape_of(slots, table_lanes, dtype=F32),
            shape_of(16, group_width, dtype=F32),
        ],
        [tail_sums, time_table],
        "vw",
        away=(0, 1, 2),
        vmem=52,
    )
    first_gain_grad, first_shift_grad, second_gain_grad, second_shift_grad = sums[:4]
    out_bias_grad, down_bias_grad = sums[4], sums[5]
    up_bias_grad = sums[6 : 6 + hidden_width // group_width].reshape(-1)
    bias_table_grad = table_grad[:, : stride * stride].T

    block_out = run(
        partial(block_kernel, side),
        shape_of(length, width),
        [relative_index, out_keep, out_got, out_far, middle, down_bias],
        "wvvvvw",
    )
    return (
        block_out,
        tokens_grad,
        time_table_grad.T,
        query_grad.T,
        key_grad.T,
        value_grad.T,
        time_query_grad.T,
        time_value_grad.T,
        out_grad,
        out_bias_grad,
        first_gain_grad,
        first_shift_grad,
        second_gain_grad,
        second_shift_grad,
        up_grad,
        up_bias_grad,
        down_grad,
        down_bias_grad,
        bias_table_grad,
    )


def solution(mesh):
    whole = P()
    rows = P(("dp", "mp"), None)
    columns = P(None, "mp")
    split = P("mp")
    placed = (
        (P("dp", None), P("dp"))
        + (whole,) * 13
        + (columns, split, P("mp", None), whole, whole, rows)
    )
    return jax.shard_map(
        on_device,
        mesh=mesh,
        in_specs=placed,
        out_specs=(rows, rows)
        + (columns,) * 6
        + (P("mp", None),)
        + (split,) * 5
        + (columns, split, P("mp", None), split, columns),
        check_vma=False,
    )
```

```python
import math
from functools import partial

import jax
import jax.numpy as jnp
from jax import lax
from jax.experimental import pallas as pl
from jax.experimental.pallas import tpu as pltpu
from jax.sharding import PartitionSpec as P

EPSILON = 1e-06
HIGHEST = lax.Precision.HIGHEST
F32 = jnp.float32
BF16 = jnp.bfloat16
LANES = 128
PACE = 0.3


def mm(left, right):
    return lax.dot_general(left, right, (((1,), (0,)), ((), ())), preferred_element_type=F32)


def mm_nt(left, right):
    return lax.dot_general(left, right, (((1,), (1,)), ((), ())), preferred_element_type=F32)


def mm_tn(left, right):
    return lax.dot_general(left, right, (((0,), (0,)), ((), ())), preferred_element_type=F32)


def round_up(value, step):
    return -(-value // step) * step


def head_window(slot, head_width):
    first = slot * head_width // LANES * LANES
    last = round_up((slot + 1) * head_width, LANES)
    return first, last - first, slot * head_width - first


def head_mask(lanes, offset, head_width):
    lane = lax.broadcasted_iota(jnp.int32, (1, lanes), 1)
    return jnp.where((lane >= offset) & (lane < offset + head_width), 1.0, 0.0).astype(BF16)


def row_of(ref):
    return ref[...].reshape(1, ref.shape[0])


def unit_rows(values):
    centred = values - jnp.mean(values, axis=-1, keepdims=True)
    inverse = lax.rsqrt(jnp.mean(centred * centred, axis=-1, keepdims=True) + EPSILON)
    return centred * inverse, inverse


def norm_back(grad_out, unit, inverse, gain_row):
    grad_unit = grad_out * gain_row
    first_mean = jnp.mean(grad_unit, axis=-1, keepdims=True)
    second_mean = jnp.mean(grad_unit * unit, axis=-1, keepdims=True)
    return inverse * (grad_unit - first_mean - unit * second_mean)


def add_tiles(tiles, product, first):
    for part in range(product.shape[1] // LANES):
        place = first // LANES + part
        piece = product[:, part * LANES : (part + 1) * LANES]
        tiles[place] = piece if tiles[place] is None else tiles[place] + piece


def squeeze_part(part, side, stride):
    each = LANES // side
    first = part * each * stride // LANES * LANES
    last = round_up((part * each + each - 1) * stride + side, LANES)
    wide = lax.broadcasted_iota(jnp.int32, (last - first, LANES), 0) + first
    close = lax.broadcasted_iota(jnp.int32, (last - first, LANES), 1)
    same = wide == (part * each + close // side) * stride + close % side
    return first, last - first, jnp.where(same, 1.0, 0.0).astype(BF16)


def place_matrix(relative_row, side):
    stride = 2 * side - 1
    entry = relative_row.astype(F32)
    row_part = jnp.floor((entry + 0.5) * (1.0 / stride))
    column_part = entry - row_part * stride
    row_part = jnp.max(row_part, axis=1, keepdims=True) - row_part
    column_part = jnp.max(column_part, axis=1, keepdims=True) - column_part
    cells = (row_part * side + column_part).astype(jnp.int32)
    length = side * side
    cell = lax.broadcasted_iota(jnp.int32, (length, length), 0)
    return jnp.where(cell == cells, 1.0, 0.0).astype(BF16)


def split_two(values):
    high = values.astype(BF16)
    return high, (values - high.astype(F32)).astype(BF16)


def attend_kernel(
    dims,
    ranks,
    steps_ref,
    relative_ref,
    table_ref,
    first_gain,
    first_shift,
    second_gain,
    second_shift,
    out_bias,
    tokens_hbm,
    times_hbm,
    query_hbm,
    key_hbm,
    value_hbm,
    time_query_hbm,
    time_value_hbm,
    out_hbm,
    query_ref,
    key_ref,
    value_ref,
    probs_ref,
    mixed_0,
    mixed_1,
    mixed_far,
    middle_ref,
    normed_ref,
    embed_ref,
    weights,
    own_tokens,
    times,
    table,
    wide_high,
    wide_low,
    windows,
    flat,
    mixed_ref,
    sems,
):
    groups, slots, head_width, side, scale = dims
    group_width = slots * head_width
    rank = ranks[0]
    length = side * side
    step = steps_ref[rank]
    own_copy = pltpu.make_async_copy(
        tokens_hbm.at[pl.ds(pl.multiple_of(rank * length, length), length)], own_tokens, sems.at[6]
    )
    own_copy.start()
    sources = (query_hbm, key_hbm, value_hbm, time_query_hbm, time_value_hbm, out_hbm)
    copies = {}
    for item in (0, 1, 3, 2, 4, 5):
        copies[item] = pltpu.make_async_copy(sources[item], weights.at[item], sems.at[item])
        copies[item].start()
    times_copy = pltpu.make_async_copy(times_hbm.at[step // 8], times, sems.at[7])
    times_copy.start()
    stride = 2 * side - 1
    heads = groups * slots
    row_lanes = table.shape[1]
    table[...] = jnp.zeros_like(table)
    table[:, : stride * stride] = table_ref[...]
    for head in range(heads):
        row = jnp.broadcast_to(table[head : head + 1, :], (side, row_lanes))
        shifted = pltpu.roll(row, row_lanes - (side - 1), 1, stride=1, stride_axis=0)
        high, low = split_two(shifted)
        wide_high[head * side : (head + 1) * side, :] = high
        wide_low[head * side : (head + 1) * side, :] = low
    span_lanes = windows.shape[2]
    for part in range(span_lanes // LANES):
        first, lanes, squeeze = squeeze_part(part, side, stride)
        span = slice(first, first + lanes)
        narrow = mm(wide_high[:, span], squeeze) + mm(wide_low[:, span], squeeze)
        windows[:, :, part * LANES : (part + 1) * LANES] = narrow.reshape(heads, side, LANES)
    place = place_matrix(relative_ref[0:1, :], side)
    own_copy.wait()
    own = mm(place, own_tokens[...])
    unit, _ = unit_rows(own)
    normed = (unit * row_of(first_gain) + row_of(first_shift)).astype(BF16)

    def into_groups(rows, target):
        fill = jnp.zeros((rows.shape[0], target.shape[2] - group_width), rows.dtype)
        for group in range(groups):
            piece = rows[:, group * group_width : (group + 1) * group_width]
            target[group] = jnp.concatenate([piece, fill], axis=1)

    copies[0].wait()
    query = mm(normed, weights[0])
    copies[1].wait()
    into_groups(mm(normed, weights[1]).astype(BF16), key_ref)
    key_ref.send()
    times_copy.wait()
    line = lax.broadcasted_iota(jnp.int32, times.shape, 0)
    chosen = jnp.where(line == step % 8, times[...].astype(F32), 0.0)
    embed = jnp.broadcast_to(jnp.sum(chosen, axis=0, keepdims=True), times.shape)
    embed_ref[...] = embed
    embed = embed.astype(BF16)
    copies[3].wait()
    into_groups((query + mm(embed, weights[3])[0:1]).astype(BF16), query_ref)
    query_ref.send()
    copies[2].wait()
    value = mm(normed, weights[2])
    copies[4].wait()
    into_groups((value + mm(embed, weights[4])[0:1]).astype(BF16), value_ref)
    value_ref.send()

    def one_group(group, carry):
        tiles = [None] * (query_ref.shape[2] // LANES)
        for slot in range(slots):
            head = group * slots + slot
            first, lanes, offset = head_window(slot, head_width)
            mask = head_mask(lanes, offset, head_width)
            window = windows[head]
            blocks = [None] * side
            steps = LANES // side
            for turn in range(steps):
                turned = window
                if turn:
                    turned = pltpu.roll(window, span_lanes - turn * side, 1)
                for jump in range(-(-side // steps)):
                    block = side - 1 - (jump * steps + turn)
                    if block >= 0:
                        blocks[block] = turned[:, jump * LANES : jump * LANES + length]
            bias = jnp.concatenate(blocks, axis=0)
            keys = key_ref[group, :, first : first + lanes]
            queries = query_ref[group, :, first : first + lanes] * mask
            scores = mm_nt(keys, queries) * scale + bias
            weights_now = jnp.exp(scores - jnp.max(scores, axis=0, keepdims=True))
            totals = jnp.sum(weights_now, axis=0, keepdims=True)
            probs = (weights_now * (1.0 / totals)).astype(BF16)
            probs_ref[head] = probs
            values = value_ref[group, :, first : first + lanes] * mask
            add_tiles(tiles, mm_tn(probs, values), first)
        mixed_ref[group] = jnp.concatenate(tiles, axis=1).astype(BF16)
        probs_ref.send_rows(group * slots, slots)
        return carry

    lax.fori_loop(0, groups, one_group, 0)
    for group in range(groups):
        flat[:, group * group_width : (group + 1) * group_width] = mixed_ref[group][:, :group_width]
    for away in (2, 3):
        mixed_far[away - 2] = mixed_ref[rank ^ away]
    mixed_far.send()
    mixed_1[...] = mixed_ref[rank ^ 1]
    mixed_1.send()
    mixed_0[...] = mixed_ref[rank]
    mixed_0.send()
    copies[5].wait()
    middle = own + mm(flat[...], weights[5]) + row_of(out_bias)
    middle_ref[...] = middle
    middle_ref.send()
    unit, _ = unit_rows(middle)
    normed_ref[...] = (unit * row_of(second_gain) + row_of(second_shift)).astype(BF16)


def normed_kernel(side, ranks, relative_ref, tokens_ref, gain, shift, normed_ref):
    unit, _ = unit_rows(mm(place_matrix(relative_ref[0:1, :], side), tokens_ref[...]))
    normed_ref[...] = (unit * row_of(gain) + row_of(shift)).astype(BF16)


def gelu_pair(hidden):
    root = math.sqrt(2.0 / math.pi)
    square = hidden * hidden
    bend = jnp.tanh(hidden * (root + (root * 0.044715) * square))
    half = 0.5 + 0.5 * bend
    slope = half + (0.5 * hidden) * (1.0 - bend * bend) * (root + (3.0 * root * 0.044715) * square)
    return hidden * half, slope


def feed_rows(side, relative_ref, normed, cotangent, up_ref, up_bias, down_ref, active, hidden, moved):
    place = place_matrix(relative_ref[0:1, :], side)
    rows = place.shape[0]
    for chunk in range(len(normed)):
        span = slice(chunk * rows, (chunk + 1) * rows)
        turned = mm(place, cotangent[chunk][...]).astype(BF16)
        moved[span, :] = turned
        gelu_out, slope = gelu_pair(mm(normed[chunk][...], up_ref[...]) + row_of(up_bias))
        active[span, :] = gelu_out.astype(BF16)
        hidden[span, :] = (mm_nt(turned, down_ref[...]) * slope).astype(BF16)


def feed_near_kernel(
    side,
    relative_ref,
    normed_own,
    normed_near,
    cot_own,
    cot_near,
    up_ref,
    up_bias,
    down_ref,
    active,
    hidden,
    moved,
    grad_own,
    grad_near,
):
    feed_rows(
        side,
        relative_ref,
        (normed_own, normed_near),
        (cot_own, cot_near),
        up_ref,
        up_bias,
        down_ref,
        active,
        hidden,
        moved,
    )
    active.send()
    moved.send()
    hidden.send()
    rows = grad_own.shape[0]
    grad_near[...] = mm_nt(hidden[rows:, :], up_ref[...]).astype(BF16)
    grad_near.send()
    grad_own[...] = mm_nt(hidden[:rows, :], up_ref[...]).astype(BF16)


def halves(values, bit):
    half = values.shape[0] // 2
    low, high = values[:half], values[half:]
    return jnp.where(bit == 0, low, high), jnp.where(bit == 0, high, low)


def feed_far_kernel(
    side,
    relative_ref,
    normed_far,
    normed_last,
    cot_far,
    cot_last,
    up_ref,
    up_bias,
    down_ref,
    near_hidden,
    active,
    hidden,
    moved,
    grad_far,
    grad_last,
    bias_ref,
):
    feed_rows(
        side,
        relative_ref,
        (normed_far, normed_last),
        (cot_far, cot_last),
        up_ref,
        up_bias,
        down_ref,
        active,
        hidden,
        moved,
    )
    rows = grad_far.shape[0]
    grad_last[...] = mm_nt(hidden[rows:, :], up_ref[...]).astype(BF16)
    grad_far[...] = mm_nt(hidden[:rows, :], up_ref[...]).astype(BF16)
    total = jnp.sum(hidden[...].astype(F32), axis=0, keepdims=True)
    total = total + jnp.sum(near_hidden[...].astype(F32), axis=0, keepdims=True)
    bias_ref[...] = jnp.broadcast_to(total, bias_ref.shape)


def down_grad_kernel(level, ranks, near_active, near_moved, active, moved, keep_ref, send_ref):
    grad = mm_tn(near_active[...], near_moved[...]) + mm_tn(active[...], moved[...])
    keep, send = halves(grad.astype(BF16), (ranks[1] >> level) & 1)
    send_ref[...] = send
    keep_ref[...] = keep


def up_grad_kernel(
    level, ranks, own, near, far, last, near_hidden, hidden, keep_ref, send_ref, normed
):
    rows = own.shape[0]
    for chunk, ref in enumerate((own, near, far, last)):
        normed[chunk * rows : (chunk + 1) * rows, :] = ref[...]
    grad = mm_tn(normed[: 2 * rows, :], near_hidden[...]) + mm_tn(normed[2 * rows :, :], hidden[...])
    keep, send = halves(grad.astype(BF16), (ranks[1] >> level) & 1)
    send_ref[...] = send
    send_ref.send()
    keep_ref[...] = keep


def out_kernel(near_active, active, down_ref, keep_ref, send_ref):
    rows = keep_ref.shape[1]
    keep_ref[0] = mm(near_active[:rows, :], down_ref[...]).astype(BF16)
    send_ref[0] = mm(near_active[rows:, :], down_ref[...]).astype(BF16)
    keep_ref[1] = mm(active[:rows, :], down_ref[...]).astype(BF16)
    send_ref[1] = mm(active[rows:, :], down_ref[...]).astype(BF16)


def add_kernel(left, right, out_ref):
    out_ref[...] = (left[...].astype(F32) + right[...].astype(F32)).astype(out_ref.dtype)


def middle_kernel(
    own_ref,
    near_ref,
    far_ref,
    middle_ref,
    moved_ref,
    gain,
    branch_ref,
    grad_ref,
    sums_ref,
):
    rows = own_ref.shape[0]
    grad_normed = own_ref[...].astype(F32) + near_ref[...].astype(F32) + far_ref[...].astype(F32)
    unit, inverse = unit_rows(middle_ref[...])
    cotangent = moved_ref[:rows, :].astype(F32)
    grad_middle = cotangent + norm_back(grad_normed, unit, inverse, row_of(gain))
    branch_ref[...] = grad_middle.astype(BF16)
    branch_ref.send()
    grad_ref[...] = grad_middle
    grad_ref.send()
    sums_ref[...] = jnp.zeros(sums_ref.shape, F32)
    sums_ref[0:1, :] = jnp.sum(grad_normed * unit, axis=0, keepdims=True)
    sums_ref[1:2, :] = jnp.sum(grad_normed, axis=0, keepdims=True)
    sums_ref[2:3, :] = jnp.sum(grad_middle, axis=0, keepdims=True)
    sums_ref[3:4, :] = jnp.sum(cotangent, axis=0, keepdims=True)


def attend_back_kernel(
    dims,
    picks,
    ranks,
    *refs,
):
    groups, slots, head_width, side, scale = dims
    group_width = slots * head_width
    rank = ranks[0]
    length = side * side
    hbm = refs[1:5] if len(refs) == 14 else refs[2:6]
    nows = refs[-5:-1]

    def fetch(pick, item):
        group = (picks[0] + pick) ^ rank
        source = hbm[item].at[pl.ds(group * slots, slots)] if item == 3 else hbm[item].at[group]
        return pltpu.make_async_copy(source, nows[item].at[pick], refs[-1].at[pick, item])

    for pick in range(2):
        for item in (3, 2, 0, 1):
            fetch(pick, item).start()
    if len(refs) == 15:
        branch_ref, out_ref = refs[:2]
        packed_far, grads, grad_mixed, sheared, query_now, key_now, value_now, probs_now, _ = refs[6:]
        packed_all = [packed_far.ref.at[0], packed_far.ref.at[1]]
        fill = jnp.zeros((length, grad_mixed.shape[2] - group_width), BF16)
        product = mm_nt(branch_ref[...], out_ref[...]).astype(BF16)
        for group in range(groups):
            piece = product[:, group * group_width : (group + 1) * group_width]
            grad_mixed[group] = jnp.concatenate([piece, fill], axis=1)
        grad_mixed.send()
    else:
        grad_mixed = refs[0]
        packed_a, packed_b, grads, sheared, query_now, key_now, value_now, probs_now, _ = refs[5:]
        packed_all = [packed_a.ref, packed_b.ref]
        grad_mixed.ready()
    stride = 2 * side - 1
    span_lanes = sheared.shape[2]
    packed_lanes = packed_all[0].shape[1]
    table_lanes = round_up(stride * stride, LANES)

    def one_group(pick, carry):
        group = (picks[0] + pick) ^ rank
        for item in range(4):
            fetch(pick, item).wait()
        wide = grad_mixed.shape[2] // LANES
        query_tiles, key_tiles, value_tiles = [None] * wide, [None] * wide, [None] * wide
        for slot in range(slots):
            first, lanes, offset = head_window(slot, head_width)
            mask = head_mask(lanes, offset, head_width)
            span = slice(first, first + lanes)
            mixed_now = grad_mixed[group, :, span] * mask
            probs = probs_now[pick, slot]
            grad_probs = mm_nt(value_now[pick, :, span], mixed_now)
            probs_wide = probs.astype(F32)
            weighted = probs_wide * grad_probs
            grad_scores = weighted - probs_wide * jnp.sum(weighted, axis=0, keepdims=True)
            rounded = grad_scores.astype(BF16)
            add_tiles(value_tiles, mm(probs, mixed_now), first)
            add_tiles(key_tiles, mm(rounded, query_now[pick, :, span] * mask), first)
            add_tiles(query_tiles, mm_tn(rounded, key_now[pick, :, span] * mask), first)
            steps = LANES // side
            shear = jnp.zeros((side, span_lanes), F32)
            for turn in range(steps):
                summed = None
                for jump in range(-(-side // steps)):
                    block = side - 1 - (jump * steps + turn)
                    if block >= 0:
                        piece = grad_scores[block * side : (block + 1) * side, :]
                        parts = []
                        if jump:
                            parts.append(jnp.zeros((side, jump * LANES), F32))
                        parts.append(piece)
                        rest = span_lanes - jump * LANES - length
                        if rest:
                            parts.append(jnp.zeros((side, rest), F32))
                        piece = jnp.concatenate(parts, axis=1)
                        summed = piece if summed is None else summed + piece
                shear = shear + (pltpu.roll(summed, turn * side, 1) if turn else summed)
            sheared[:, pl.ds(pick * slots + slot, 1), :] = shear[:, None, :]
        query = (jnp.concatenate(query_tiles, axis=1) * scale).astype(BF16)
        key = (jnp.concatenate(key_tiles, axis=1) * scale).astype(BF16)
        value = jnp.concatenate(value_tiles, axis=1).astype(BF16)
        grads[0, pick] = query
        grads[1, pick] = key
        grads[2, pick] = value
        return carry

    lax.fori_loop(0, len(picks), one_group, 0)
    selections = [squeeze_part(part, side, stride) for part in range(span_lanes // LANES)]
    heads = 2 * slots
    tall = table_lanes // LANES
    total = [jnp.zeros((heads, LANES), F32)] * tall
    for column in range(side):
        high, low = split_two(sheared[column])
        tiles = [None] * tall
        for part, (first, lanes, squeeze) in enumerate(selections):
            span = slice(part * LANES, (part + 1) * LANES)
            add_tiles(tiles, mm_nt(high[:, span], squeeze) + mm_nt(low[:, span], squeeze), first)
        spread = jnp.concatenate(
            [jnp.zeros((heads, LANES), F32) if tile is None else tile for tile in tiles], axis=1
        )
        turn = side - 1 - column
        turned = pltpu.roll(spread, turn, 1) if turn else spread
        total = [
            old + turned[:, place * LANES : (place + 1) * LANES] for place, old in enumerate(total)
        ]
    for pick, packed_ref in enumerate(packed_all):
        for place in range(tall):
            packed_ref[length + place * slots : length + (place + 1) * slots, :LANES] = total[place][
                pick * slots : (pick + 1) * slots
            ].astype(BF16)
        pieces = [grads[item, pick][:, :group_width] for item in range(3)]
        if packed_lanes > 3 * group_width:
            pieces.append(jnp.zeros((length, packed_lanes - 3 * group_width), BF16))
        packed_ref[:length, :] = jnp.concatenate(pieces, axis=1)


def tokens_kernel(
    dims,
    ranks,
    near_grads,
    far_grads,
    query_ref,
    key_ref,
    value_ref,
    relative_ref,
    gain,
    middle_ref,
    middle_sums,
    tokens_hbm,
    image_ref,
    grad_ref,
    flat,
    own_tokens,
    sem,
):
    groups, slots, head_width, side, scale = dims
    group_width = slots * head_width
    rank = ranks[0]
    length = side * side
    own_copy = pltpu.make_async_copy(
        tokens_hbm.at[pl.ds(pl.multiple_of(rank * length, length), length)], own_tokens, sem
    )
    own_copy.start()
    for group in range(groups):
        away = group ^ rank
        for item in range(3):
            piece = jnp.where(away >= 2, far_grads[item, away & 1], near_grads[item, away & 1])
            flat[item, :, group * group_width : (group + 1) * group_width] = piece[:, :group_width]
    grad_normed = (
        mm_nt(flat[0], query_ref[...])
        + mm_nt(flat[1], key_ref[...])
        + mm_nt(flat[2], value_ref[...])
    )
    place = place_matrix(relative_ref[0:1, :], side)
    own_copy.wait()
    unit, inverse = unit_rows(mm(place, own_tokens[...]))
    total = middle_ref[...] + norm_back(grad_normed, unit, inverse, row_of(gain))
    high, low = split_two(total)
    grad_ref[...] = mm_tn(place, high) + mm_tn(place, low)
    grad_ref.send()
    sums = [
        jnp.sum(flat[0].astype(F32), axis=0, keepdims=True),
        jnp.sum(flat[2].astype(F32), axis=0, keepdims=True),
        jnp.sum(grad_normed * unit, axis=0, keepdims=True),
        jnp.sum(grad_normed, axis=0, keepdims=True),
        middle_sums[0:4, :],
    ]
    image_ref[...] = jnp.concatenate(sums, axis=0)
    image_ref.send()


def own_columns(rows, rank, groups):
    columns = rows.shape[1] // groups
    chosen = rows[:, :columns]
    for group in range(1, groups):
        chosen = jnp.where(rank == group, rows[:, group * columns : (group + 1) * columns], chosen)
    return chosen


def weights_kernel(dims, level, ranks, steps_ref, normed, *refs):
    groups, slots, head_width, side, scale = dims
    group_width = slots * head_width
    rows = side * side
    rank = ranks[0]
    lines_own, lines_far, lines_near, up_bias_ref, query_hbm, value_hbm = refs[
        3 * groups : 3 * groups + 6
    ]
    keep_first, keep_second, send_first, send_second = refs[3 * groups + 6 : 3 * groups + 10]
    packed, branch, mixed, tail, times, sems = refs[3 * groups + 10 :]
    start = pl.multiple_of(rank * group_width, 16)
    copies = []
    for item, source in enumerate((query_hbm, value_hbm)):
        copies.append(
            pltpu.make_async_copy(
                source.at[pl.ds(start, group_width)], times.at[item], sems.at[item]
            )
        )
        copies[item].start()
    table = None
    for chunk in range(groups):
        span = slice(chunk * rows, (chunk + 1) * rows)
        source, other = refs[chunk].ref, refs[2 * groups + chunk].ref
        if chunk >= 2:
            source, other = source.at[chunk - 2], other.at[chunk - 2]
        packed[span, :] = source[:rows, :]
        branch[span, :] = refs[groups + chunk][...]
        mixed[span, :] = other[...]
        part = source[rows:, :LANES].astype(F32)
        table = part if table is None else table + part
    bit = (ranks[1] >> level) & 1
    left = mm_tn(packed[...], normed[...]).astype(BF16)
    right = mm_tn(mixed[...], branch[...]).astype(BF16)
    value, out = left[2 * group_width : 3 * group_width], right[:group_width]
    keep_second[...] = jnp.where(bit == 0, value, out)
    send_second[...] = jnp.where(bit == 0, out, value)

    lines = [lines_own[...], lines_near[:8, :], lines_far[...], lines_near[8:, :]]
    embed = None
    for item in range(2):
        both = jnp.concatenate([line[item : item + 1, :] for line in lines] * 2, axis=0)
        high = both.astype(BF16).astype(F32)
        place = lax.broadcasted_iota(jnp.int32, both.shape, 0)
        both = jnp.where(place < groups, high, both - high).astype(BF16)
        copies[item].wait()
        product = mm_nt(both, times[item])
        product = product[:groups] + product[groups:]
        embed = product if embed is None else embed + product
    tail[...] = jnp.zeros_like(tail)
    tail[: table.shape[0], :LANES] = table
    each = group_width // 2
    for chunk in range(groups):
        total = jnp.sum(packed[chunk * rows : (chunk + 1) * rows, :].astype(F32), axis=0, keepdims=True)
        step = steps_ref[rank ^ chunk]
        fill = tail.shape[1] - LANES - 3 * group_width - 16
        line = [
            total[:, :group_width],
            total[:, 2 * group_width : 3 * group_width],
            embed[chunk : chunk + 1, :],
            jnp.zeros((1, fill), F32),
            jnp.full((1, 8), (step // 8).astype(F32)),
            jnp.full((1, 8), (step % 8).astype(F32)),
        ]
        image = ranks[1] * groups + (rank ^ chunk)
        tail[pl.ds(image, 1), LANES:] = jnp.concatenate(line, axis=1)
    vectors = lines[0] + lines[1] + lines[2] + lines[3]
    vectors = [own_columns(vectors[item : item + 1, :], rank, groups) for item in range(2, 8)]
    vectors += [
        up_bias_ref[0:1, part * group_width : (part + 1) * group_width]
        for part in range(up_bias_ref.shape[1] // group_width)
    ]
    first = LANES + 3 * group_width
    for item, vector in enumerate(vectors):
        tail[2 * item : 2 * item + 1, first : first + each] = vector[:, :each]
        tail[2 * item + 1 : 2 * item + 2, first : first + each] = vector[:, each:]
    keep, send = halves(left[: 2 * group_width], bit)
    keep_first[:group_width, :] = keep
    send_first[:group_width, :] = send
    keep, send = halves(tail[...].astype(BF16), bit)
    keep_first[group_width:, :] = keep
    send_first[group_width:, :] = send


def split_kernel(level, tail, ranks, kept, got, keep_ref, send_ref):
    total = (kept[...].astype(F32) + got[...].astype(F32)).astype(BF16)
    bit = (ranks[1] >> level) & 1
    body = total.shape[0] - tail
    keep, send = halves(total[:body], bit)
    send_ref[: body // 2, :] = send
    keep_ref[: body // 2, :] = keep
    if tail:
        keep, send = halves(total[body:], bit)
        send_ref[body // 2 :, :] = send
        keep_ref[body // 2 :, :] = keep


def join_kernel(level, tail, ranks, own, other, out_ref):
    body = own.shape[0] - tail
    bit = (ranks[1] >> level) & 1
    low = jnp.where(bit == 0, own[...], other[...])
    high = jnp.where(bit == 0, other[...], own[...])
    out_ref[:body, :] = low[:body]
    out_ref[body : 2 * body, :] = high[:body]
    if tail:
        out_ref[2 * body : 2 * body + tail, :] = low[body:]
        out_ref[2 * body + tail :, :] = high[body:]


def widen_kernel(level, cross, each, ranks, own, other, out_ref):
    bit = (ranks[1] >> level) & 1
    block = pl.program_id(0) // each
    first = (block % 2 if cross else block // 2) == bit

    @pl.when(first)
    def _():
        out_ref[...] = own[...].astype(F32)

    @pl.when(jnp.logical_not(first))
    def _():
        out_ref[...] = other[...].astype(F32)


def widen_pair_kernel(level, ranks, own, other, low_ref, high_ref, tail_ref):
    bit = (ranks[1] >> level) & 1
    low = jnp.where(bit == 0, own[...], other[...]).astype(F32)
    high = jnp.where(bit == 0, other[...], own[...]).astype(F32)
    body, half = low_ref.shape[0], tail_ref.shape[0] // 2
    tail_ref[:half, :] = low[body:]
    tail_ref[half:, :] = high[body:]
    low_ref[...] = low[:body]
    low_ref.send()
    high_ref[...] = high[:body]


def widen_cross_kernel(level, ranks, own, other, low_ref, high_ref):
    bit = (ranks[1] >> level) & 1
    body = own.shape[0] // 2
    even = jnp.where(bit == 0, own[...], other[...]).astype(F32)
    odd = jnp.where(bit == 0, other[...], own[...]).astype(F32)
    low_ref[:body, :] = even[:body]
    low_ref[body:, :] = odd[:body]
    low_ref.send()
    high_ref[:body, :] = even[body:]
    high_ref[body:, :] = odd[body:]


def finish_kernel(
    dims, images, tail, times, query_ref, value_ref, table_ref, bias_ref, sums_ref
):
    groups, slots, head_width, side, scale = dims
    group_width = slots * head_width
    for part in range(bias_ref.shape[1] // LANES):
        bias_ref[:, part * LANES : (part + 1) * LANES] = tail[
            part * slots : (part + 1) * slots, :LANES
        ]
    each = group_width // 2
    first = LANES + 3 * group_width
    sums_ref[...] = jnp.zeros(sums_ref.shape, F32)
    for item in range(10):
        for part in range(2):
            row = 2 * item + part
            sums_ref[item : item + 1, part * each : (part + 1) * each] = tail[
                row : row + 1, first : first + each
            ]
    last = tail.shape[1]
    steps = tail[:images, last - 16 : last - 15] * 8.0 + tail[:images, last - 8 : last - 7]
    step = lax.broadcasted_iota(jnp.int32, (images, table_ref.shape[1]), 1)
    chosen = jnp.where(step == steps.astype(jnp.int32), 1.0, 0.0).astype(BF16)
    total = tail[:images, LANES + 2 * group_width : LANES + 3 * group_width].astype(BF16)
    table_ref[...] = mm_tn(total, chosen)
    table_ref.send()
    embed = mm(chosen, times[...]).astype(BF16)
    for item, target in enumerate((query_ref, value_ref)):
        rows = tail[:images, LANES + item * group_width : LANES + (item + 1) * group_width]
        target[...] = mm_tn(rows.astype(BF16), embed)
        target.send()


def block_kernel(side, relative_ref, own, near, far, middle_ref, bias, out_ref):
    total = own[0].astype(F32) + near[0].astype(F32) + far[...].astype(F32)
    total = (middle_ref[...] + total + row_of(bias)).astype(BF16)
    place = place_matrix(relative_ref[0:1, :], side)
    out_ref[...] = mm_tn(place, total).astype(BF16)


def shape_of(*sizes, dtype=BF16):
    return jax.ShapeDtypeStruct(sizes, dtype)


VMEM = pl.BlockSpec(memory_space=pltpu.VMEM)
HBM = pl.BlockSpec(memory_space=pl.ANY)
SMEM = pl.BlockSpec(memory_space=pltpu.SMEM)
MIB = 1024 * 1024
FEED = 16


def cost(us):
    return pl.CostEstimate(flops=int(us * PACE * 1.15e9), bytes_accessed=1000, transcendentals=0)


class Staged:
    def __init__(self, source, target, sem):
        self.ref, self.waited = target, False
        self.copy = pltpu.make_async_copy(source, target, sem)
        self.copy.start()
        self.shape = target.shape

    def ready(self):
        if not self.waited:
            self.waited = True
            self.copy.wait()
        return self.ref

    def __getitem__(self, place):
        return self.ready()[place]


class Result:
    def __init__(self, ref, target=None, sem=None):
        self.ref, self.sent = ref, target is None
        self.copy = None if self.sent else pltpu.make_async_copy(ref, target, sem)
        self.shape, self.dtype = ref.shape, ref.dtype
        self.target, self.sem = target, sem

    def send_rows(self, start, count):
        self.sent = True
        rows = pl.ds(start, count)
        pltpu.make_async_copy(self.ref.at[rows], self.target.at[rows], self.sem).start()

    def __getitem__(self, place):
        return self.ref[place]

    def __setitem__(self, place, value):
        self.ref[place] = value

    def send(self):
        if not self.sent:
            self.sent = True
            self.copy.start()


class Held:
    def __init__(self, ref):
        self.ref, self.shape = ref, ref.shape

    def ready(self):
        return self.ref

    def __getitem__(self, place):
        return self.ref[place]


def run(kernel, outs, inputs, kinds=None, scratch=(), deps=(), us=2.5, away=(), vmem=16):
    kinds = "v" * len(inputs) if kinds is None else kinds
    assert len(kinds) == len(inputs)
    single = not isinstance(outs, (list, tuple))
    outs = [outs] if single else list(outs)
    staged = [place for place, kind in enumerate(kinds) if kind == "w"]
    count, results = len(inputs), len(outs)
    if deps:
        inputs = [after(inputs[0], *deps), *inputs[1:]]
    buffers = [pltpu.VMEM(inputs[place].shape, inputs[place].dtype) for place in staged]
    buffers += [pltpu.VMEM(outs[place].shape, outs[place].dtype) for place in away]
    if buffers:
        buffers.append(pltpu.SemaphoreType.DMA((len(buffers),)))

    def body(*refs):
        given = list(refs[:count])
        targets = refs[count : count + results]
        rest = refs[count + results :]
        for place, kind in enumerate(kinds):
            if kind == "v":
                given[place] = Held(given[place])
        for order, place in enumerate(staged):
            sem = rest[len(buffers) - 1].at[order]
            given[place] = Staged(given[place], rest[order], sem)
        made = []
        for place, target in enumerate(targets):
            if place in away:
                order = len(staged) + away.index(place)
                made.append(Result(rest[order], target, rest[len(buffers) - 1].at[order]))
            else:
                made.append(Result(target))
        kernel(*given, *made, *rest[len(buffers) :])
        for result in made:
            result.send()
        for place in staged:
            given[place].ready()
        for result in made:
            if result.copy is not None:
                result.copy.wait()

    space = {"s": SMEM, "h": HBM, "v": VMEM, "w": HBM}
    found = pl.pallas_call(
        body,
        out_shape=outs,
        in_specs=[space[kind] for kind in kinds],
        out_specs=[HBM if place in away else VMEM for place in range(results)],
        scratch_shapes=buffers + list(scratch),
        compiler_params=pltpu.CompilerParams(vmem_limit_bytes=vmem * MIB),
        cost_estimate=cost(us),
    )(*inputs)
    return found[0] if single else found


def quick(kernel, outs, inputs, deps=(), us=1.2):
    if deps:
        inputs = [after(inputs[0], *deps), *inputs[1:]]
    return pl.pallas_call(
        kernel,
        out_shape=outs,
        in_specs=[SMEM if given.shape == (2,) else VMEM for given in inputs],
        out_specs=jax.tree.map(lambda _: VMEM, outs),
        compiler_params=pltpu.CompilerParams(vmem_limit_bytes=4 * MIB),
        cost_estimate=cost(us),
    )(*inputs)


def widen(ranks, level, own, other, last, cross=False):
    half, columns = own.shape
    each = 2
    block = half // (2 * each)
    parts = 4 * each

    def place_of(i, bit):
        quarter, inner = i // each, i % each
        if cross:
            return ((quarter // 2) * each + inner, 0)
        return (jnp.clip(i - 2 * each * bit, 0, 2 * each - 1), 0)

    def own_map(i, me):
        return place_of(i, (me[1] >> level) & 1)

    def other_map(i, me):
        return place_of(i, 1 - ((me[1] >> level) & 1))

    return pl.pallas_call(
        partial(widen_kernel, level, cross, each),
        out_shape=shape_of(2 * half, columns, dtype=F32),
        grid_spec=pltpu.PrefetchScalarGridSpec(
            num_scalar_prefetch=1,
            grid=(parts,),
            in_specs=[
                pl.BlockSpec((block, columns), own_map),
                pl.BlockSpec((block, columns), other_map),
            ],
            out_specs=pl.BlockSpec((block, columns), lambda i, me: (i, 0)),
        ),
        compiler_params=pltpu.CompilerParams(vmem_limit_bytes=16 * MIB),
        cost_estimate=cost(3.5),
    )(after(ranks, last), own, other)


def swap(array, axis, distance):
    size = lax.axis_size(axis)
    return lax.ppermute(array, axis, [(i, i ^ distance) for i in range(size)])


def after(array, *others):
    return lax.optimization_barrier((array, *others))[0]


class Total:
    def __init__(self, ranks, order, keep, send, tail=0, cross=False):
        self.ranks, self.order, self.tail = ranks, order, tail
        self.back = (0, 1) if cross else (1, 0)
        self.keep = keep
        self.got = self.swap(0, send)

    def swap(self, place, array):
        return swap(array, "dp", 1 << self.order[place])

    def split(self, deps=(), us=1.2):
        half, columns = self.keep.shape
        part = shape_of(half // 2, columns)
        self.keep, send = quick(
            partial(split_kernel, self.order[1], self.tail),
            [part, part],
            [self.ranks, self.keep, self.got],
            deps,
            us,
        )
        self.got = self.swap(1, send)
        return self.keep

    def add(self, place, deps=()):
        self.keep = quick(add_kernel, shape_of(*self.keep.shape), [self.keep, self.got], deps)
        self.got = self.swap(place, self.keep)
        return self.keep

    def join(self, deps=()):
        half, columns = self.keep.shape
        self.keep = quick(
            partial(join_kernel, self.order[self.back[0]], self.tail // 2),
            shape_of(2 * half, columns),
            [self.ranks, self.keep, self.got],
            deps,
        )
        self.got = self.swap(self.back[1], self.keep)
        return self.keep

    def exchange(self, deps=()):
        for place in range(2, len(self.order)):
            self.add(place, deps)
        return self.keep

    def finish(self, deps=()):
        return self.add(self.back[0], deps)


def add_low(left, right):
    return (left.astype(F32) + right.astype(F32)).astype(BF16)


def on_device(
    tokens,
    timesteps,
    relative_index,
    time_table,
    query_weight,
    key_weight,
    value_weight,
    time_query_weight,
    time_value_weight,
    out_weight,
    out_bias,
    first_gain,
    first_shift,
    second_gain,
    second_shift,
    up_weight,
    up_bias,
    down_weight,
    down_bias,
    bias_table,
    cotangent,
):
    length = relative_index.shape[0]
    width = tokens.shape[1]
    heads = bias_table.shape[1]
    head_width = width // heads
    side = math.isqrt(length)
    stride = 2 * side - 1
    groups = lax.axis_size("mp")
    dp_size = lax.axis_size("dp")
    rank = lax.axis_index("mp")
    ranks = jnp.stack([rank, lax.axis_index("dp")]).astype(jnp.int32)
    slots = heads // groups
    group_width = slots * head_width
    group_lanes = round_up(group_width, LANES)
    packed_lanes = round_up(3 * group_width, LANES)
    table_lanes = round_up(stride * stride, LANES)
    span_lanes = round_up(stride * side, LANES)
    hidden_width = up_weight.shape[1]
    rows = groups * length
    dims = (groups, slots, head_width, side, head_width ** (-0.5))
    levels = list(range(dp_size.bit_length() - 1))
    other_order = levels[1::-1] + levels[2:]

    def grouped():
        return shape_of(groups, length, group_lanes)

    one_group = shape_of(length, group_lanes)

    cot_near = swap(cotangent, "mp", 1)
    cot_far = swap(cotangent, "mp", 2)
    steps = time_table.shape[0]
    outs = run(
        partial(attend_kernel, dims),
        [
            grouped(),
            grouped(),
            grouped(),
            shape_of(heads, length, length),
            one_group,
            one_group,
            shape_of(2, length, group_lanes),
            shape_of(length, width, dtype=F32),
            shape_of(length, width),
            shape_of(8, width, dtype=F32),
        ],
        [
            ranks,
            timesteps,
            relative_index,
            bias_table.T,
            first_gain,
            first_shift,
            second_gain,
            second_shift,
            out_bias,
            tokens,
            time_table.reshape(steps // 8, 8, width),
            query_weight,
            key_weight,
            value_weight,
            time_query_weight,
            time_value_weight,
            out_weight,
        ],
        "sswwwwwww" + "h" * 8,
        [
            pltpu.VMEM((6, width, width), BF16),
            pltpu.VMEM((length, width), BF16),
            pltpu.VMEM((8, width), BF16),
            pltpu.VMEM((heads, table_lanes), F32),
            pltpu.VMEM((heads * side, table_lanes), BF16),
            pltpu.VMEM((heads * side, table_lanes), BF16),
            pltpu.VMEM((heads, side, span_lanes), F32),
            pltpu.VMEM((length, width), BF16),
            pltpu.VMEM((groups, length, group_lanes), BF16),
            pltpu.SemaphoreType.DMA((8,)),
        ],
        us=60.0,
        away=(0, 1, 2, 3, 4, 5, 6, 7),
        vmem=56,
    )
    query_rows, key_rows, value_rows, probs = outs[:4]
    mixed_own, mixed_near, mixed_far, middle, normed_own, embed = outs[4:]
    normed_near = swap(normed_own, "mp", 1)
    normed_far = swap(normed_own, "mp", 2)

    normed_first = pl.pallas_call(
        partial(normed_kernel, side),
        out_shape=shape_of(rows, width),
        grid_spec=pltpu.PrefetchScalarGridSpec(
            num_scalar_prefetch=1,
            grid=(groups,),
            in_specs=[
                pl.BlockSpec((8, length), lambda i, me: (0, 0)),
                pl.BlockSpec((length, width), lambda i, me: (i ^ me[0], 0)),
                VMEM,
                VMEM,
            ],
            out_specs=pl.BlockSpec((length, width), lambda i, me: (i, 0)),
        ),
        compiler_params=pltpu.CompilerParams(vmem_limit_bytes=40 * MIB),
        cost_estimate=cost(4.0),
    )(after(ranks, normed_own, cot_far), relative_index, tokens, first_gain, first_shift)

    cot_last = swap(after(cot_far, normed_own), "mp", 1)
    pair = shape_of(2 * length, width)
    hidden_pair = shape_of(2 * length, hidden_width)
    chunk = shape_of(length, width)
    near_active, near_hidden, near_moved, grad_own, grad_near = run(
        partial(feed_near_kernel, side),
        [hidden_pair, hidden_pair, pair, chunk, chunk],
        [
            relative_index,
            normed_own,
            normed_near,
            cotangent,
            cot_near,
            up_weight,
            up_bias,
            down_weight,
        ],
        "vvvvvwvw",
        deps=[normed_first, cot_last],
        us=7.2,
        vmem=FEED,
    )
    near_got = swap(grad_near, "mp", 1)
    normed_last = swap(after(normed_far, grad_near), "mp", 1)
    mixed_far = swap(mixed_far, "mp", 2)
    active, hidden, moved, grad_far, grad_last, up_bias_sum = run(
        partial(feed_far_kernel, side),
        [hidden_pair, hidden_pair, pair, chunk, chunk, shape_of(8, hidden_width, dtype=F32)],
        [
            relative_index,
            normed_far,
            normed_last,
            cot_far,
            cot_last,
            up_weight,
            up_bias,
            down_weight,
            near_hidden,
        ],
        "vvvvvwvwv",
        us=7.5,
        deps=[near_got],
        vmem=FEED,
    )
    last_got = swap(grad_last, "mp", 1)
    half = shape_of(hidden_width // 2, width)
    keep, send = run(
        partial(down_grad_kernel, levels[0]),
        [half, half],
        [ranks, near_active, near_moved, active, moved],
        "svvvv",
        deps=[up_bias_sum, mixed_far],
        us=14.0,
        vmem=FEED,
    )
    down = Total(ranks, levels, keep, send)
    grad_sent = run(add_kernel, chunk, [grad_far, last_got], deps=[keep], vmem=4)
    far_got = swap(grad_sent, "mp", 2)
    mixed_last = swap(after(mixed_far, grad_sent), "mp", 1)
    mixed_near = swap(after(mixed_near, grad_sent), "mp", 1)
    half = shape_of(width // 2, hidden_width)
    keep, send = run(
        partial(up_grad_kernel, other_order[0]),
        [half, half],
        [ranks, normed_own, normed_near, normed_far, normed_last, near_hidden, hidden],
        "s" + "v" * 6,
        [pltpu.VMEM((rows, width), BF16)],
        deps=[grad_sent],
        us=4.9,
        vmem=FEED,
    )
    up = Total(ranks, other_order, keep, send, cross=True)
    chunks = shape_of(2, length, width)
    out_keep, out_send = run(
        out_kernel, [chunks, chunks], [near_active, active, down_weight], "vvw", deps=[keep], us=5.0, vmem=FEED
    )
    out_got = swap(out_send, "mp", 1)
    grad_branch, grad_middle, middle_sums = run(
        middle_kernel,
        [chunk, shape_of(length, width, dtype=F32), shape_of(8, width, dtype=F32)],
        [grad_own, near_got, far_got, middle, near_moved, second_gain],
        "vvvvvw",
        deps=[out_keep],
        vmem=8,
    )
    branch_near = swap(grad_branch, "mp", 1)
    branch_far = swap(grad_branch, "mp", 2)
    last = middle_sums

    tail = slots * table_lanes // LANES
    two_groups = pltpu.VMEM((2, length, group_lanes), BF16)
    back_scratch = [
        pltpu.VMEM((side, 2 * slots, span_lanes), F32),
        two_groups,
        two_groups,
        two_groups,
        pltpu.VMEM((2, slots, length, length), BF16),
        pltpu.SemaphoreType.DMA((2, 4)),
    ]
    grads_shape = shape_of(3, 2, length, group_lanes)
    packed_shape = shape_of(length + tail, packed_lanes)
    packed_pair = shape_of(2, length + tail, packed_lanes)
    heads_in = [query_rows, key_rows, value_rows, probs]
    packed_far, far_grads, grad_mixed = run(
        partial(attend_back_kernel, dims, (2, 3)),
        [packed_pair, grads_shape, grouped()],
        [ranks, grad_branch, out_weight] + heads_in,
        "svwhhhh",
        back_scratch,
        deps=[last, mixed_last, mixed_near],
        us=8.3,
    )
    packed_far = swap(packed_far, "mp", 2)
    last = grad_mixed
    packed_0, packed_1, near_grads = run(
        partial(attend_back_kernel, dims, (0, 1)),
        [packed_shape, packed_shape, grads_shape],
        [ranks, grad_mixed] + heads_in,
        "svhhhh",
        back_scratch,
        deps=[last],
        us=8.3,
    )
    last = down.split([packed_0, branch_far])
    branch_last = swap(after(branch_far, last), "mp", 1)
    last = up.split([last])
    image_rows, tokens_grad = run(
        partial(tokens_kernel, dims),
        [shape_of(8, width, dtype=F32), shape_of(length, width, dtype=F32)],
        [
            ranks,
            near_grads,
            far_grads,
            query_weight,
            key_weight,
            value_weight,
            relative_index,
            first_gain,
            grad_middle,
            middle_sums,
            tokens,
        ],
        "svvwwwwwvvh",
        [
            pltpu.VMEM((3, length, width), BF16),
            pltpu.VMEM((length, width), BF16),
            pltpu.SemaphoreType.DMA,
        ],
        deps=[last, branch_last],
        us=8.6,
        away=(1,),
        vmem=24,
    )
    lines_far = swap(image_rows, "mp", 2)
    last = down.exchange([image_rows, packed_far, lines_far, up.got])
    lines_near = swap(after(jnp.concatenate([image_rows, lines_far], axis=0), last), "mp", 1)
    packed_last = swap(after(packed_far, last), "mp", 1)
    packed_1 = swap(after(packed_1, last), "mp", 1)
    half = shape_of(group_width, width)
    images = dp_size * groups
    tail_rows = max(tail, images)
    more = shape_of(group_width + tail_rows // 2, width)
    keep_first, keep_second, send_first, send_second = run(
        partial(weights_kernel, dims, levels[0]),
        [more, half, more, half],
        [ranks, timesteps, normed_first, packed_0, packed_1, packed_far, packed_last]
        + [grad_branch, branch_near, branch_far, branch_last]
        + [mixed_own, mixed_near, mixed_far, mixed_last]
        + [image_rows, lines_far, lines_near, up_bias_sum, time_query_weight, time_value_weight],
        "ss" + "v" * 17 + "hh",
        [
            pltpu.VMEM((rows, packed_lanes), BF16),
            pltpu.VMEM((rows, width), BF16),
            pltpu.VMEM((rows, group_lanes), BF16),
            pltpu.VMEM((tail_rows, width), F32),
            pltpu.VMEM((2, group_width, width), BF16),
            pltpu.SemaphoreType.DMA((2,)),
        ],
        deps=[last],
        us=5.2,
    )
    first = Total(ranks, levels, keep_first, send_first, tail_rows // 2)
    last = down.finish([keep_second])
    last = first.split([last], 8.0)
    second = Total(ranks, levels, keep_second, send_second, cross=True)
    last = up.exchange([last])
    out_far = swap(add_low(out_keep[1], out_got[1]), "mp", 2)
    last = second.split([last], 8.0)
    last = down.join([last])
    last = up.finish([last])
    last = first.exchange([last])
    last = up.join([last])
    last = first.finish([last])
    last = second.exchange([last])
    last = first.join([last])
    down_grad = widen(ranks, levels[0], down.keep, down.got, last)
    last = second.finish([down_grad])
    last = second.join([last])
    up_grad = widen(ranks, other_order[1], up.keep, up.got, last, cross=True)
    wide = shape_of(group_width, width, dtype=F32)
    query_grad, key_grad, tail_sums = run(
        partial(widen_pair_kernel, levels[0]),
        [wide, wide, shape_of(tail_rows, width, dtype=F32)],
        [ranks, first.keep, first.got],
        "svv",
        away=(0, 1),
        deps=[up_grad],
    )
    value_grad, out_grad = run(
        partial(widen_cross_kernel, levels[1]),
        [wide, wide],
        [ranks, second.keep, second.got],
        "svv",
        away=(0, 1),
        deps=[query_grad],
    )

    time_query_grad, time_value_grad, time_table_grad, table_grad, sums = run(
        partial(finish_kernel, dims, images),
        [
            shape_of(group_width, width, dtype=F32),
            shape_of(group_width, width, dtype=F32),
            shape_of(group_width, steps, dtype=F32),
            shape_of(slots, table_lanes, dtype=F32),
            shape_of(16, group_width, dtype=F32),
        ],
        [tail_sums, time_table],
        "vw",
        away=(0, 1, 2),
        vmem=52,
    )
    first_gain_grad, first_shift_grad, second_gain_grad, second_shift_grad = sums[:4]
    out_bias_grad, down_bias_grad = sums[4], sums[5]
    up_bias_grad = sums[6 : 6 + hidden_width // group_width].reshape(-1)
    bias_table_grad = table_grad[:, : stride * stride].T

    block_out = run(
        partial(block_kernel, side),
        shape_of(length, width),
        [relative_index, out_keep, out_got, out_far, middle, down_bias],
        "wvvvvw",
    )
    return (
        block_out,
        tokens_grad,
        time_table_grad.T,
        query_grad.T,
        key_grad.T,
        value_grad.T,
        time_query_grad.T,
        time_value_grad.T,
        out_grad,
        out_bias_grad,
        first_gain_grad,
        first_shift_grad,
        second_gain_grad,
        second_shift_grad,
        up_grad,
        up_bias_grad,
        down_grad,
        down_bias_grad,
        bias_table_grad,
    )


def solution(mesh):
    whole = P()
    rows = P(("dp", "mp"), None)
    columns = P(None, "mp")
    split = P("mp")
    placed = (
        (P("dp", None), P("dp"))
        + (whole,) * 13
        + (columns, split, P("mp", None), whole, whole, rows)
    )
    return jax.shard_map(
        on_device,
        mesh=mesh,
        in_specs=placed,
        out_specs=(rows, rows)
        + (columns,) * 6
        + (P("mp", None),)
        + (split,) * 5
        + (columns, split, P("mp", None), split, columns),
        check_vma=False,
    )
```

```python
import math
from functools import partial

import jax
import jax.numpy as jnp
from jax import lax
from jax.experimental import pallas as pl
from jax.experimental.pallas import tpu as pltpu
from jax.sharding import PartitionSpec as P

EPSILON = 1e-06
HIGHEST = lax.Precision.HIGHEST
F32 = jnp.float32
BF16 = jnp.bfloat16
LANES = 128
PACE = 0.3


def mm(left, right):
    return lax.dot_general(left, right, (((1,), (0,)), ((), ())), preferred_element_type=F32)


def mm_nt(left, right):
    return lax.dot_general(left, right, (((1,), (1,)), ((), ())), preferred_element_type=F32)


def mm_tn(left, right):
    return lax.dot_general(left, right, (((0,), (0,)), ((), ())), preferred_element_type=F32)


def round_up(value, step):
    return -(-value // step) * step


def head_window(slot, head_width):
    first = slot * head_width // LANES * LANES
    last = round_up((slot + 1) * head_width, LANES)
    return first, last - first, slot * head_width - first


def head_mask(lanes, offset, head_width):
    lane = lax.broadcasted_iota(jnp.int32, (1, lanes), 1)
    return jnp.where((lane >= offset) & (lane < offset + head_width), 1.0, 0.0).astype(BF16)


def row_of(ref):
    return ref[...].reshape(1, ref.shape[0])


def unit_rows(values):
    centred = values - jnp.mean(values, axis=-1, keepdims=True)
    inverse = lax.rsqrt(jnp.mean(centred * centred, axis=-1, keepdims=True) + EPSILON)
    return centred * inverse, inverse


def norm_back(grad_out, unit, inverse, gain_row):
    grad_unit = grad_out * gain_row
    first_mean = jnp.mean(grad_unit, axis=-1, keepdims=True)
    second_mean = jnp.mean(grad_unit * unit, axis=-1, keepdims=True)
    return inverse * (grad_unit - first_mean - unit * second_mean)


def add_tiles(tiles, product, first):
    for part in range(product.shape[1] // LANES):
        place = first // LANES + part
        piece = product[:, part * LANES : (part + 1) * LANES]
        tiles[place] = piece if tiles[place] is None else tiles[place] + piece


def squeeze_part(part, side, stride):
    each = LANES // side
    first = part * each * stride // LANES * LANES
    last = round_up((part * each + each - 1) * stride + side, LANES)
    wide = lax.broadcasted_iota(jnp.int32, (last - first, LANES), 0) + first
    close = lax.broadcasted_iota(jnp.int32, (last - first, LANES), 1)
    same = wide == (part * each + close // side) * stride + close % side
    return first, last - first, jnp.where(same, 1.0, 0.0).astype(BF16)


def place_matrix(relative_row, side):
    stride = 2 * side - 1
    entry = relative_row.astype(F32)
    row_part = jnp.floor((entry + 0.5) * (1.0 / stride))
    column_part = entry - row_part * stride
    row_part = jnp.max(row_part, axis=1, keepdims=True) - row_part
    column_part = jnp.max(column_part, axis=1, keepdims=True) - column_part
    cells = (row_part * side + column_part).astype(jnp.int32)
    length = side * side
    cell = lax.broadcasted_iota(jnp.int32, (length, length), 0)
    return jnp.where(cell == cells, 1.0, 0.0).astype(BF16)


def split_two(values):
    high = values.astype(BF16)
    return high, (values - high.astype(F32)).astype(BF16)


def attend_kernel(
    dims,
    ranks,
    steps_ref,
    relative_ref,
    table_ref,
    first_gain,
    first_shift,
    second_gain,
    second_shift,
    out_bias,
    tokens_hbm,
    times_hbm,
    query_hbm,
    key_hbm,
    value_hbm,
    time_query_hbm,
    time_value_hbm,
    out_hbm,
    query_ref,
    key_ref,
    value_ref,
    probs_ref,
    mixed_0,
    mixed_1,
    mixed_far,
    middle_ref,
    normed_ref,
    embed_ref,
    weights,
    own_tokens,
    times,
    table,
    wide_high,
    wide_low,
    windows,
    flat,
    mixed_ref,
    sems,
):
    groups, slots, head_width, side, scale = dims
    group_width = slots * head_width
    rank = ranks[0]
    length = side * side
    step = steps_ref[rank]
    own_copy = pltpu.make_async_copy(
        tokens_hbm.at[pl.ds(pl.multiple_of(rank * length, length), length)], own_tokens, sems.at[6]
    )
    own_copy.start()
    sources = (query_hbm, key_hbm, value_hbm, time_query_hbm, time_value_hbm, out_hbm)
    copies = {}
    for item in (0, 1, 3, 2, 4, 5):
        copies[item] = pltpu.make_async_copy(sources[item], weights.at[item], sems.at[item])
        copies[item].start()
    times_copy = pltpu.make_async_copy(times_hbm.at[step // 8], times, sems.at[7])
    times_copy.start()
    stride = 2 * side - 1
    heads = groups * slots
    row_lanes = table.shape[1]
    table[...] = jnp.zeros_like(table)
    table[:, : stride * stride] = table_ref[...]
    for head in range(heads):
        row = jnp.broadcast_to(table[head : head + 1, :], (side, row_lanes))
        shifted = pltpu.roll(row, row_lanes - (side - 1), 1, stride=1, stride_axis=0)
        high, low = split_two(shifted)
        wide_high[head * side : (head + 1) * side, :] = high
        wide_low[head * side : (head + 1) * side, :] = low
    span_lanes = windows.shape[2]
    for part in range(span_lanes // LANES):
        first, lanes, squeeze = squeeze_part(part, side, stride)
        span = slice(first, first + lanes)
        narrow = mm(wide_high[:, span], squeeze) + mm(wide_low[:, span], squeeze)
        windows[:, :, part * LANES : (part + 1) * LANES] = narrow.reshape(heads, side, LANES)
    place = place_matrix(relative_ref[0:1, :], side)
    own_copy.wait()
    own = mm(place, own_tokens[...])
    unit, _ = unit_rows(own)
    normed = (unit * row_of(first_gain) + row_of(first_shift)).astype(BF16)

    def into_groups(rows, target):
        fill = jnp.zeros((rows.shape[0], target.shape[2] - group_width), rows.dtype)
        for group in range(groups):
            piece = rows[:, group * group_width : (group + 1) * group_width]
            target[group] = jnp.concatenate([piece, fill], axis=1)

    copies[0].wait()
    query = mm(normed, weights[0])
    copies[1].wait()
    into_groups(mm(normed, weights[1]).astype(BF16), key_ref)
    key_ref.send()
    times_copy.wait()
    line = lax.broadcasted_iota(jnp.int32, times.shape, 0)
    chosen = jnp.where(line == step % 8, times[...].astype(F32), 0.0)
    embed = jnp.broadcast_to(jnp.sum(chosen, axis=0, keepdims=True), times.shape)
    embed_ref[...] = embed
    embed = embed.astype(BF16)
    copies[3].wait()
    into_groups((query + mm(embed, weights[3])[0:1]).astype(BF16), query_ref)
    query_ref.send()
    copies[2].wait()
    value = mm(normed, weights[2])
    copies[4].wait()
    into_groups((value + mm(embed, weights[4])[0:1]).astype(BF16), value_ref)
    value_ref.send()

    def one_group(group, carry):
        tiles = [None] * (query_ref.shape[2] // LANES)
        for slot in range(slots):
            head = group * slots + slot
            first, lanes, offset = head_window(slot, head_width)
            mask = head_mask(lanes, offset, head_width)
            window = windows[head]
            blocks = [None] * side
            steps = LANES // side
            for turn in range(steps):
                turned = window
                if turn:
                    turned = pltpu.roll(window, span_lanes - turn * side, 1)
                for jump in range(-(-side // steps)):
                    block = side - 1 - (jump * steps + turn)
                    if block >= 0:
                        blocks[block] = turned[:, jump * LANES : jump * LANES + length]
            bias = jnp.concatenate(blocks, axis=0)
            keys = key_ref[group, :, first : first + lanes]
            queries = query_ref[group, :, first : first + lanes] * mask
            scores = mm_nt(keys, queries) * scale + bias
            weights_now = jnp.exp(scores - jnp.max(scores, axis=0, keepdims=True))
            totals = jnp.sum(weights_now, axis=0, keepdims=True)
            probs = (weights_now * (1.0 / totals)).astype(BF16)
            probs_ref[head] = probs
            values = value_ref[group, :, first : first + lanes] * mask
            add_tiles(tiles, mm_tn(probs, values), first)
        mixed_ref[group] = jnp.concatenate(tiles, axis=1).astype(BF16)
        probs_ref.send_rows(group * slots, slots)
        return carry

    lax.fori_loop(0, groups, one_group, 0)
    for group in range(groups):
        flat[:, group * group_width : (group + 1) * group_width] = mixed_ref[group][:, :group_width]
    for away in (2, 3):
        mixed_far[away - 2] = mixed_ref[rank ^ away]
    mixed_far.send()
    mixed_1[...] = mixed_ref[rank ^ 1]
    mixed_1.send()
    mixed_0[...] = mixed_ref[rank]
    mixed_0.send()
    copies[5].wait()
    middle = own + mm(flat[...], weights[5]) + row_of(out_bias)
    middle_ref[...] = middle
    middle_ref.send()
    unit, _ = unit_rows(middle)
    normed_ref[...] = (unit * row_of(second_gain) + row_of(second_shift)).astype(BF16)


def normed_kernel(side, ranks, relative_ref, tokens_ref, gain, shift, normed_ref):
    unit, _ = unit_rows(mm(place_matrix(relative_ref[0:1, :], side), tokens_ref[...]))
    normed_ref[...] = (unit * row_of(gain) + row_of(shift)).astype(BF16)


def gelu_pair(hidden):
    root = math.sqrt(2.0 / math.pi)
    square = hidden * hidden
    bend = jnp.tanh(hidden * (root + (root * 0.044715) * square))
    half = 0.5 + 0.5 * bend
    slope = half + (0.5 * hidden) * (1.0 - bend * bend) * (root + (3.0 * root * 0.044715) * square)
    return hidden * half, slope


def feed_rows(side, relative_ref, normed, cotangent, up_ref, up_bias, down_ref, active, hidden, moved):
    place = place_matrix(relative_ref[0:1, :], side)
    rows = place.shape[0]
    for chunk in range(len(normed)):
        span = slice(chunk * rows, (chunk + 1) * rows)
        turned = mm(place, cotangent[chunk][...]).astype(BF16)
        moved[span, :] = turned
        gelu_out, slope = gelu_pair(mm(normed[chunk][...], up_ref[...]) + row_of(up_bias))
        active[span, :] = gelu_out.astype(BF16)
        hidden[span, :] = (mm_nt(turned, down_ref[...]) * slope).astype(BF16)


def feed_near_kernel(
    side,
    relative_ref,
    normed_own,
    normed_near,
    cot_own,
    cot_near,
    up_ref,
    up_bias,
    down_ref,
    active,
    hidden,
    moved,
    grad_own,
    grad_near,
):
    feed_rows(
        side,
        relative_ref,
        (normed_own, normed_near),
        (cot_own, cot_near),
        up_ref,
        up_bias,
        down_ref,
        active,
        hidden,
        moved,
    )
    active.send()
    moved.send()
    hidden.send()
    rows = grad_own.shape[0]
    grad_near[...] = mm_nt(hidden[rows:, :], up_ref[...]).astype(BF16)
    grad_near.send()
    grad_own[...] = mm_nt(hidden[:rows, :], up_ref[...]).astype(BF16)


def halves(values, bit):
    half = values.shape[0] // 2
    low, high = values[:half], values[half:]
    return jnp.where(bit == 0, low, high), jnp.where(bit == 0, high, low)


def feed_far_kernel(
    side,
    relative_ref,
    normed_far,
    normed_last,
    cot_far,
    cot_last,
    up_ref,
    up_bias,
    down_ref,
    near_hidden,
    active,
    hidden,
    moved,
    grad_far,
    grad_last,
    bias_ref,
):
    feed_rows(
        side,
        relative_ref,
        (normed_far, normed_last),
        (cot_far, cot_last),
        up_ref,
        up_bias,
        down_ref,
        active,
        hidden,
        moved,
    )
    rows = grad_far.shape[0]
    grad_last[...] = mm_nt(hidden[rows:, :], up_ref[...]).astype(BF16)
    grad_far[...] = mm_nt(hidden[:rows, :], up_ref[...]).astype(BF16)
    total = jnp.sum(hidden[...].astype(F32), axis=0, keepdims=True)
    total = total + jnp.sum(near_hidden[...].astype(F32), axis=0, keepdims=True)
    bias_ref[...] = jnp.broadcast_to(total, bias_ref.shape)


def down_grad_kernel(level, ranks, near_active, near_moved, active, moved, keep_ref, send_ref):
    grad = mm_tn(near_active[...], near_moved[...]) + mm_tn(active[...], moved[...])
    keep, send = halves(grad.astype(BF16), (ranks[1] >> level) & 1)
    send_ref[...] = send
    keep_ref[...] = keep


def up_grad_kernel(
    level, ranks, own, near, far, last, near_hidden, hidden, keep_ref, send_ref, normed
):
    rows = own.shape[0]
    for chunk, ref in enumerate((own, near, far, last)):
        normed[chunk * rows : (chunk + 1) * rows, :] = ref[...]
    grad = mm_tn(normed[: 2 * rows, :], near_hidden[...]) + mm_tn(normed[2 * rows :, :], hidden[...])
    keep, send = halves(grad.astype(BF16), (ranks[1] >> level) & 1)
    send_ref[...] = send
    send_ref.send()
    keep_ref[...] = keep


def out_kernel(near_active, active, down_ref, keep_ref, send_ref):
    rows = keep_ref.shape[1]
    keep_ref[0] = mm(near_active[:rows, :], down_ref[...]).astype(BF16)
    send_ref[0] = mm(near_active[rows:, :], down_ref[...]).astype(BF16)
    keep_ref[1] = mm(active[:rows, :], down_ref[...]).astype(BF16)
    send_ref[1] = mm(active[rows:, :], down_ref[...]).astype(BF16)


def add_kernel(left, right, out_ref):
    out_ref[...] = (left[...].astype(F32) + right[...].astype(F32)).astype(out_ref.dtype)


def middle_kernel(
    own_ref,
    near_ref,
    far_ref,
    middle_ref,
    moved_ref,
    gain,
    branch_ref,
    grad_ref,
    sums_ref,
):
    rows = own_ref.shape[0]
    grad_normed = own_ref[...].astype(F32) + near_ref[...].astype(F32) + far_ref[...].astype(F32)
    unit, inverse = unit_rows(middle_ref[...])
    cotangent = moved_ref[:rows, :].astype(F32)
    grad_middle = cotangent + norm_back(grad_normed, unit, inverse, row_of(gain))
    branch_ref[...] = grad_middle.astype(BF16)
    branch_ref.send()
    grad_ref[...] = grad_middle
    grad_ref.send()
    sums_ref[...] = jnp.zeros(sums_ref.shape, F32)
    sums_ref[0:1, :] = jnp.sum(grad_normed * unit, axis=0, keepdims=True)
    sums_ref[1:2, :] = jnp.sum(grad_normed, axis=0, keepdims=True)
    sums_ref[2:3, :] = jnp.sum(grad_middle, axis=0, keepdims=True)
    sums_ref[3:4, :] = jnp.sum(cotangent, axis=0, keepdims=True)


def attend_back_kernel(
    dims,
    picks,
    ranks,
    *refs,
):
    groups, slots, head_width, side, scale = dims
    group_width = slots * head_width
    rank = ranks[0]
    length = side * side
    hbm = refs[1:5] if len(refs) == 14 else refs[2:6]
    nows = refs[-5:-1]

    def fetch(pick, item):
        group = (picks[0] + pick) ^ rank
        source = hbm[item].at[pl.ds(group * slots, slots)] if item == 3 else hbm[item].at[group]
        return pltpu.make_async_copy(source, nows[item].at[pick], refs[-1].at[pick, item])

    for pick in range(2):
        for item in (3, 2, 0, 1):
            fetch(pick, item).start()
    if len(refs) == 15:
        branch_ref, out_ref = refs[:2]
        packed_far, grads, grad_mixed, sheared, query_now, key_now, value_now, probs_now, _ = refs[6:]
        packed_all = [packed_far.ref.at[0], packed_far.ref.at[1]]
        fill = jnp.zeros((length, grad_mixed.shape[2] - group_width), BF16)
        product = mm_nt(branch_ref[...], out_ref[...]).astype(BF16)
        for group in range(groups):
            piece = product[:, group * group_width : (group + 1) * group_width]
            grad_mixed[group] = jnp.concatenate([piece, fill], axis=1)
        grad_mixed.send()
    else:
        grad_mixed = refs[0]
        packed_a, packed_b, grads, sheared, query_now, key_now, value_now, probs_now, _ = refs[5:]
        packed_all = [packed_a.ref, packed_b.ref]
        grad_mixed.ready()
    stride = 2 * side - 1
    span_lanes = sheared.shape[2]
    packed_lanes = packed_all[0].shape[1]
    table_lanes = round_up(stride * stride, LANES)

    def one_group(pick, carry):
        group = (picks[0] + pick) ^ rank
        for item in range(4):
            fetch(pick, item).wait()
        wide = grad_mixed.shape[2] // LANES
        query_tiles, key_tiles, value_tiles = [None] * wide, [None] * wide, [None] * wide
        for slot in range(slots):
            first, lanes, offset = head_window(slot, head_width)
            mask = head_mask(lanes, offset, head_width)
            span = slice(first, first + lanes)
            mixed_now = grad_mixed[group, :, span] * mask
            probs = probs_now[pick, slot]
            grad_probs = mm_nt(value_now[pick, :, span], mixed_now)
            probs_wide = probs.astype(F32)
            weighted = probs_wide * grad_probs
            grad_scores = weighted - probs_wide * jnp.sum(weighted, axis=0, keepdims=True)
            rounded = grad_scores.astype(BF16)
            add_tiles(value_tiles, mm(probs, mixed_now), first)
            add_tiles(key_tiles, mm(rounded, query_now[pick, :, span] * mask), first)
            add_tiles(query_tiles, mm_tn(rounded, key_now[pick, :, span] * mask), first)
            steps = LANES // side
            shear = jnp.zeros((side, span_lanes), F32)
            for turn in range(steps):
                summed = None
                for jump in range(-(-side // steps)):
                    block = side - 1 - (jump * steps + turn)
                    if block >= 0:
                        piece = grad_scores[block * side : (block + 1) * side, :]
                        parts = []
                        if jump:
                            parts.append(jnp.zeros((side, jump * LANES), F32))
                        parts.append(piece)
                        rest = span_lanes - jump * LANES - length
                        if rest:
                            parts.append(jnp.zeros((side, rest), F32))
                        piece = jnp.concatenate(parts, axis=1)
                        summed = piece if summed is None else summed + piece
                shear = shear + (pltpu.roll(summed, turn * side, 1) if turn else summed)
            sheared[:, pl.ds(pick * slots + slot, 1), :] = shear[:, None, :]
        query = (jnp.concatenate(query_tiles, axis=1) * scale).astype(BF16)
        key = (jnp.concatenate(key_tiles, axis=1) * scale).astype(BF16)
        value = jnp.concatenate(value_tiles, axis=1).astype(BF16)
        grads[0, pick] = query
        grads[1, pick] = key
        grads[2, pick] = value
        return carry

    lax.fori_loop(0, len(picks), one_group, 0)
    selections = [squeeze_part(part, side, stride) for part in range(span_lanes // LANES)]
    heads = 2 * slots
    tall = table_lanes // LANES
    total = [jnp.zeros((heads, LANES), F32)] * tall
    for column in range(side):
        high, low = split_two(sheared[column])
        tiles = [None] * tall
        for part, (first, lanes, squeeze) in enumerate(selections):
            span = slice(part * LANES, (part + 1) * LANES)
            add_tiles(tiles, mm_nt(high[:, span], squeeze) + mm_nt(low[:, span], squeeze), first)
        spread = jnp.concatenate(
            [jnp.zeros((heads, LANES), F32) if tile is None else tile for tile in tiles], axis=1
        )
        turn = side - 1 - column
        turned = pltpu.roll(spread, turn, 1) if turn else spread
        total = [
            old + turned[:, place * LANES : (place + 1) * LANES] for place, old in enumerate(total)
        ]
    for pick, packed_ref in enumerate(packed_all):
        for place in range(tall):
            packed_ref[length + place * slots : length + (place + 1) * slots, :LANES] = total[place][
                pick * slots : (pick + 1) * slots
            ].astype(BF16)
        pieces = [grads[item, pick][:, :group_width] for item in range(3)]
        if packed_lanes > 3 * group_width:
            pieces.append(jnp.zeros((length, packed_lanes - 3 * group_width), BF16))
        packed_ref[:length, :] = jnp.concatenate(pieces, axis=1)


def tokens_kernel(
    dims,
    ranks,
    near_grads,
    far_grads,
    query_ref,
    key_ref,
    value_ref,
    relative_ref,
    gain,
    middle_ref,
    middle_sums,
    tokens_hbm,
    image_ref,
    grad_ref,
    flat,
    own_tokens,
    sem,
):
    groups, slots, head_width, side, scale = dims
    group_width = slots * head_width
    rank = ranks[0]
    length = side * side
    own_copy = pltpu.make_async_copy(
        tokens_hbm.at[pl.ds(pl.multiple_of(rank * length, length), length)], own_tokens, sem
    )
    own_copy.start()
    for group in range(groups):
        away = group ^ rank
        for item in range(3):
            piece = jnp.where(away >= 2, far_grads[item, away & 1], near_grads[item, away & 1])
            flat[item, :, group * group_width : (group + 1) * group_width] = piece[:, :group_width]
    grad_normed = (
        mm_nt(flat[0], query_ref[...])
        + mm_nt(flat[1], key_ref[...])
        + mm_nt(flat[2], value_ref[...])
    )
    place = place_matrix(relative_ref[0:1, :], side)
    own_copy.wait()
    unit, inverse = unit_rows(mm(place, own_tokens[...]))
    total = middle_ref[...] + norm_back(grad_normed, unit, inverse, row_of(gain))
    high, low = split_two(total)
    grad_ref[...] = mm_tn(place, high) + mm_tn(place, low)
    grad_ref.send()
    sums = [
        jnp.sum(flat[0].astype(F32), axis=0, keepdims=True),
        jnp.sum(flat[2].astype(F32), axis=0, keepdims=True),
        jnp.sum(grad_normed * unit, axis=0, keepdims=True),
        jnp.sum(grad_normed, axis=0, keepdims=True),
        middle_sums[0:4, :],
    ]
    image_ref[...] = jnp.concatenate(sums, axis=0)
    image_ref.send()


def own_columns(rows, rank, groups):
    columns = rows.shape[1] // groups
    chosen = rows[:, :columns]
    for group in range(1, groups):
        chosen = jnp.where(rank == group, rows[:, group * columns : (group + 1) * columns], chosen)
    return chosen


def weights_kernel(dims, level, ranks, steps_ref, normed, *refs):
    groups, slots, head_width, side, scale = dims
    group_width = slots * head_width
    rows = side * side
    rank = ranks[0]
    lines_own, lines_far, lines_near, up_bias_ref, query_hbm, value_hbm = refs[
        3 * groups : 3 * groups + 6
    ]
    keep_first, keep_second, send_first, send_second = refs[3 * groups + 6 : 3 * groups + 10]
    packed, branch, mixed, tail, times, sems = refs[3 * groups + 10 :]
    start = pl.multiple_of(rank * group_width, 16)
    copies = []
    for item, source in enumerate((query_hbm, value_hbm)):
        copies.append(
            pltpu.make_async_copy(
                source.at[pl.ds(start, group_width)], times.at[item], sems.at[item]
            )
        )
        copies[item].start()
    table = None
    for chunk in range(groups):
        span = slice(chunk * rows, (chunk + 1) * rows)
        source, other = refs[chunk].ref, refs[2 * groups + chunk].ref
        if chunk >= 2:
            source, other = source.at[chunk - 2], other.at[chunk - 2]
        packed[span, :] = source[:rows, :]
        branch[span, :] = refs[groups + chunk][...]
        mixed[span, :] = other[...]
        part = source[rows:, :LANES].astype(F32)
        table = part if table is None else table + part
    bit = (ranks[1] >> level) & 1
    left = mm_tn(packed[...], normed[...]).astype(BF16)
    right = mm_tn(mixed[...], branch[...]).astype(BF16)
    value, out = left[2 * group_width : 3 * group_width], right[:group_width]
    keep_second[...] = jnp.where(bit == 0, value, out)
    send_second[...] = jnp.where(bit == 0, out, value)

    lines = [lines_own[...], lines_near[:8, :], lines_far[...], lines_near[8:, :]]
    embed = None
    for item in range(2):
        both = jnp.concatenate([line[item : item + 1, :] for line in lines] * 2, axis=0)
        high = both.astype(BF16).astype(F32)
        place = lax.broadcasted_iota(jnp.int32, both.shape, 0)
        both = jnp.where(place < groups, high, both - high).astype(BF16)
        copies[item].wait()
        product = mm_nt(both, times[item])
        product = product[:groups] + product[groups:]
        embed = product if embed is None else embed + product
    tail[...] = jnp.zeros_like(tail)
    tail[: table.shape[0], :LANES] = table
    each = group_width // 2
    for chunk in range(groups):
        total = jnp.sum(packed[chunk * rows : (chunk + 1) * rows, :].astype(F32), axis=0, keepdims=True)
        step = steps_ref[rank ^ chunk]
        fill = tail.shape[1] - LANES - 3 * group_width - 16
        line = [
            total[:, :group_width],
            total[:, 2 * group_width : 3 * group_width],
            embed[chunk : chunk + 1, :],
            jnp.zeros((1, fill), F32),
            jnp.full((1, 8), (step // 8).astype(F32)),
            jnp.full((1, 8), (step % 8).astype(F32)),
        ]
        image = ranks[1] * groups + (rank ^ chunk)
        tail[pl.ds(image, 1), LANES:] = jnp.concatenate(line, axis=1)
    vectors = lines[0] + lines[1] + lines[2] + lines[3]
    vectors = [own_columns(vectors[item : item + 1, :], rank, groups) for item in range(2, 8)]
    vectors += [
        up_bias_ref[0:1, part * group_width : (part + 1) * group_width]
        for part in range(up_bias_ref.shape[1] // group_width)
    ]
    first = LANES + 3 * group_width
    for item, vector in enumerate(vectors):
        tail[2 * item : 2 * item + 1, first : first + each] = vector[:, :each]
        tail[2 * item + 1 : 2 * item + 2, first : first + each] = vector[:, each:]
    keep, send = halves(left[: 2 * group_width], bit)
    keep_first[:group_width, :] = keep
    send_first[:group_width, :] = send
    keep, send = halves(tail[...].astype(BF16), bit)
    keep_first[group_width:, :] = keep
    send_first[group_width:, :] = send


def split_kernel(level, tail, ranks, kept, got, keep_ref, send_ref):
    total = (kept[...].astype(F32) + got[...].astype(F32)).astype(BF16)
    bit = (ranks[1] >> level) & 1
    body = total.shape[0] - tail
    keep, send = halves(total[:body], bit)
    send_ref[: body // 2, :] = send
    keep_ref[: body // 2, :] = keep
    if tail:
        keep, send = halves(total[body:], bit)
        send_ref[body // 2 :, :] = send
        keep_ref[body // 2 :, :] = keep


def join_kernel(level, tail, ranks, own, other, out_ref):
    body = own.shape[0] - tail
    bit = (ranks[1] >> level) & 1
    low = jnp.where(bit == 0, own[...], other[...])
    high = jnp.where(bit == 0, other[...], own[...])
    out_ref[:body, :] = low[:body]
    out_ref[body : 2 * body, :] = high[:body]
    if tail:
        out_ref[2 * body : 2 * body + tail, :] = low[body:]
        out_ref[2 * body + tail :, :] = high[body:]


def widen_kernel(level, cross, each, ranks, own, other, out_ref):
    bit = (ranks[1] >> level) & 1
    block = pl.program_id(0) // each
    first = (block % 2 if cross else block // 2) == bit

    @pl.when(first)
    def _():
        out_ref[...] = own[...].astype(F32)

    @pl.when(jnp.logical_not(first))
    def _():
        out_ref[...] = other[...].astype(F32)


def widen_pair_kernel(level, ranks, own, other, low_ref, high_ref, tail_ref):
    bit = (ranks[1] >> level) & 1
    low = jnp.where(bit == 0, own[...], other[...]).astype(F32)
    high = jnp.where(bit == 0, other[...], own[...]).astype(F32)
    body, half = low_ref.shape[0], tail_ref.shape[0] // 2
    tail_ref[:half, :] = low[body:]
    tail_ref[half:, :] = high[body:]
    low_ref[...] = low[:body]
    low_ref.send()
    high_ref[...] = high[:body]


def widen_plain_kernel(level, ranks, own, other, low_ref, high_ref):
    bit = (ranks[1] >> level) & 1
    low_ref[...] = jnp.where(bit == 0, own[...], other[...]).astype(F32)
    low_ref.send()
    high_ref[...] = jnp.where(bit == 0, other[...], own[...]).astype(F32)


def widen_cross_kernel(level, ranks, own, other, low_ref, high_ref):
    bit = (ranks[1] >> level) & 1
    body = own.shape[0] // 2
    even = jnp.where(bit == 0, own[...], other[...]).astype(F32)
    odd = jnp.where(bit == 0, other[...], own[...]).astype(F32)
    low_ref[:body, :] = even[:body]
    low_ref[body:, :] = odd[:body]
    low_ref.send()
    high_ref[:body, :] = even[body:]
    high_ref[body:, :] = odd[body:]


def finish_kernel(
    dims, images, tail, times, query_ref, value_ref, table_ref, bias_ref, sums_ref
):
    groups, slots, head_width, side, scale = dims
    group_width = slots * head_width
    for part in range(bias_ref.shape[1] // LANES):
        bias_ref[:, part * LANES : (part + 1) * LANES] = tail[
            part * slots : (part + 1) * slots, :LANES
        ]
    each = group_width // 2
    first = LANES + 3 * group_width
    sums_ref[...] = jnp.zeros(sums_ref.shape, F32)
    for item in range(10):
        for part in range(2):
            row = 2 * item + part
            sums_ref[item : item + 1, part * each : (part + 1) * each] = tail[
                row : row + 1, first : first + each
            ]
    last = tail.shape[1]
    steps = tail[:images, last - 16 : last - 15] * 8.0 + tail[:images, last - 8 : last - 7]
    step = lax.broadcasted_iota(jnp.int32, (images, table_ref.shape[1]), 1)
    chosen = jnp.where(step == steps.astype(jnp.int32), 1.0, 0.0).astype(BF16)
    total = tail[:images, LANES + 2 * group_width : LANES + 3 * group_width].astype(BF16)
    table_ref[...] = mm_tn(total, chosen)
    table_ref.send()
    embed = mm(chosen, times[...]).astype(BF16)
    for item, target in enumerate((query_ref, value_ref)):
        rows = tail[:images, LANES + item * group_width : LANES + (item + 1) * group_width]
        target[...] = mm_tn(rows.astype(BF16), embed)
        target.send()


def block_kernel(side, relative_ref, own, near, far, middle_ref, bias, out_ref):
    total = own[0].astype(F32) + near[0].astype(F32) + far[...].astype(F32)
    total = (middle_ref[...] + total + row_of(bias)).astype(BF16)
    place = place_matrix(relative_ref[0:1, :], side)
    out_ref[...] = mm_tn(place, total).astype(BF16)


def shape_of(*sizes, dtype=BF16):
    return jax.ShapeDtypeStruct(sizes, dtype)


VMEM = pl.BlockSpec(memory_space=pltpu.VMEM)
HBM = pl.BlockSpec(memory_space=pl.ANY)
SMEM = pl.BlockSpec(memory_space=pltpu.SMEM)
MIB = 1024 * 1024
FEED = 16


def cost(us):
    return pl.CostEstimate(flops=int(us * PACE * 1.15e9), bytes_accessed=1000, transcendentals=0)


class Staged:
    def __init__(self, source, target, sem):
        self.ref, self.waited = target, False
        self.copy = pltpu.make_async_copy(source, target, sem)
        self.copy.start()
        self.shape = target.shape

    def ready(self):
        if not self.waited:
            self.waited = True
            self.copy.wait()
        return self.ref

    def __getitem__(self, place):
        return self.ready()[place]


class Result:
    def __init__(self, ref, target=None, sem=None):
        self.ref, self.sent = ref, target is None
        self.copy = None if self.sent else pltpu.make_async_copy(ref, target, sem)
        self.shape, self.dtype = ref.shape, ref.dtype
        self.target, self.sem = target, sem

    def send_rows(self, start, count):
        self.sent = True
        rows = pl.ds(start, count)
        pltpu.make_async_copy(self.ref.at[rows], self.target.at[rows], self.sem).start()

    def __getitem__(self, place):
        return self.ref[place]

    def __setitem__(self, place, value):
        self.ref[place] = value

    def send(self):
        if not self.sent:
            self.sent = True
            self.copy.start()


class Held:
    def __init__(self, ref):
        self.ref, self.shape = ref, ref.shape

    def ready(self):
        return self.ref

    def __getitem__(self, place):
        return self.ref[place]


def run(kernel, outs, inputs, kinds=None, scratch=(), deps=(), us=2.5, away=(), vmem=16):
    kinds = "v" * len(inputs) if kinds is None else kinds
    assert len(kinds) == len(inputs)
    single = not isinstance(outs, (list, tuple))
    outs = [outs] if single else list(outs)
    staged = [place for place, kind in enumerate(kinds) if kind == "w"]
    count, results = len(inputs), len(outs)
    if deps:
        inputs = [after(inputs[0], *deps), *inputs[1:]]
    buffers = [pltpu.VMEM(inputs[place].shape, inputs[place].dtype) for place in staged]
    buffers += [pltpu.VMEM(outs[place].shape, outs[place].dtype) for place in away]
    if buffers:
        buffers.append(pltpu.SemaphoreType.DMA((len(buffers),)))

    def body(*refs):
        given = list(refs[:count])
        targets = refs[count : count + results]
        rest = refs[count + results :]
        for place, kind in enumerate(kinds):
            if kind == "v":
                given[place] = Held(given[place])
        for order, place in enumerate(staged):
            sem = rest[len(buffers) - 1].at[order]
            given[place] = Staged(given[place], rest[order], sem)
        made = []
        for place, target in enumerate(targets):
            if place in away:
                order = len(staged) + away.index(place)
                made.append(Result(rest[order], target, rest[len(buffers) - 1].at[order]))
            else:
                made.append(Result(target))
        kernel(*given, *made, *rest[len(buffers) :])
        for result in made:
            result.send()
        for place in staged:
            given[place].ready()
        for result in made:
            if result.copy is not None:
                result.copy.wait()

    space = {"s": SMEM, "h": HBM, "v": VMEM, "w": HBM}
    found = pl.pallas_call(
        body,
        out_shape=outs,
        in_specs=[space[kind] for kind in kinds],
        out_specs=[HBM if place in away else VMEM for place in range(results)],
        scratch_shapes=buffers + list(scratch),
        compiler_params=pltpu.CompilerParams(vmem_limit_bytes=vmem * MIB),
        cost_estimate=cost(us),
    )(*inputs)
    return found[0] if single else found


def quick(kernel, outs, inputs, deps=(), us=1.2):
    if deps:
        inputs = [after(inputs[0], *deps), *inputs[1:]]
    return pl.pallas_call(
        kernel,
        out_shape=outs,
        in_specs=[SMEM if given.shape == (2,) else VMEM for given in inputs],
        out_specs=jax.tree.map(lambda _: VMEM, outs),
        compiler_params=pltpu.CompilerParams(vmem_limit_bytes=4 * MIB),
        cost_estimate=cost(us),
    )(*inputs)


def widen(ranks, level, own, other, last, cross=False):
    half, columns = own.shape
    each = 2
    block = half // (2 * each)
    parts = 4 * each

    def place_of(i, bit):
        quarter, inner = i // each, i % each
        if cross:
            return ((quarter // 2) * each + inner, 0)
        return (jnp.clip(i - 2 * each * bit, 0, 2 * each - 1), 0)

    def own_map(i, me):
        return place_of(i, (me[1] >> level) & 1)

    def other_map(i, me):
        return place_of(i, 1 - ((me[1] >> level) & 1))

    return pl.pallas_call(
        partial(widen_kernel, level, cross, each),
        out_shape=shape_of(2 * half, columns, dtype=F32),
        grid_spec=pltpu.PrefetchScalarGridSpec(
            num_scalar_prefetch=1,
            grid=(parts,),
            in_specs=[
                pl.BlockSpec((block, columns), own_map),
                pl.BlockSpec((block, columns), other_map),
            ],
            out_specs=pl.BlockSpec((block, columns), lambda i, me: (i, 0)),
        ),
        compiler_params=pltpu.CompilerParams(vmem_limit_bytes=16 * MIB),
        cost_estimate=cost(3.5),
    )(after(ranks, last), own, other)


def swap(array, axis, distance):
    size = lax.axis_size(axis)
    return lax.ppermute(array, axis, [(i, i ^ distance) for i in range(size)])


def after(array, *others):
    return lax.optimization_barrier((array, *others))[0]


class Total:
    def __init__(self, ranks, order, keep, send, tail=0, cross=False):
        self.ranks, self.order, self.tail = ranks, order, tail
        self.back = (0, 1) if cross else (1, 0)
        self.keep = keep
        self.got = self.swap(0, send)

    def swap(self, place, array):
        return swap(array, "dp", 1 << self.order[place])

    def split(self, deps=(), us=1.2):
        half, columns = self.keep.shape
        part = shape_of(half // 2, columns)
        self.keep, send = quick(
            partial(split_kernel, self.order[1], self.tail),
            [part, part],
            [self.ranks, self.keep, self.got],
            deps,
            us,
        )
        self.got = self.swap(1, send)
        return self.keep

    def add(self, place, deps=()):
        self.keep = quick(add_kernel, shape_of(*self.keep.shape), [self.keep, self.got], deps)
        self.got = self.swap(place, self.keep)
        return self.keep

    def join(self, deps=()):
        half, columns = self.keep.shape
        self.keep = quick(
            partial(join_kernel, self.order[self.back[0]], self.tail // 2),
            shape_of(2 * half, columns),
            [self.ranks, self.keep, self.got],
            deps,
        )
        self.got = self.swap(self.back[1], self.keep)
        return self.keep

    def exchange(self, deps=()):
        for place in range(2, len(self.order)):
            self.add(place, deps)
        return self.keep

    def finish(self, deps=()):
        return self.add(self.back[0], deps)


def add_low(left, right):
    return (left.astype(F32) + right.astype(F32)).astype(BF16)


def on_device(
    tokens,
    timesteps,
    relative_index,
    time_table,
    query_weight,
    key_weight,
    value_weight,
    time_query_weight,
    time_value_weight,
    out_weight,
    out_bias,
    first_gain,
    first_shift,
    second_gain,
    second_shift,
    up_weight,
    up_bias,
    down_weight,
    down_bias,
    bias_table,
    cotangent,
):
    length = relative_index.shape[0]
    width = tokens.shape[1]
    heads = bias_table.shape[1]
    head_width = width // heads
    side = math.isqrt(length)
    stride = 2 * side - 1
    groups = lax.axis_size("mp")
    dp_size = lax.axis_size("dp")
    rank = lax.axis_index("mp")
    ranks = jnp.stack([rank, lax.axis_index("dp")]).astype(jnp.int32)
    slots = heads // groups
    group_width = slots * head_width
    group_lanes = round_up(group_width, LANES)
    packed_lanes = round_up(3 * group_width, LANES)
    table_lanes = round_up(stride * stride, LANES)
    span_lanes = round_up(stride * side, LANES)
    hidden_width = up_weight.shape[1]
    rows = groups * length
    dims = (groups, slots, head_width, side, head_width ** (-0.5))
    levels = list(range(dp_size.bit_length() - 1))
    other_order = levels[1::-1] + levels[2:]

    def grouped():
        return shape_of(groups, length, group_lanes)

    one_group = shape_of(length, group_lanes)

    cot_near = swap(cotangent, "mp", 1)
    cot_far = swap(cotangent, "mp", 2)
    steps = time_table.shape[0]
    outs = run(
        partial(attend_kernel, dims),
        [
            grouped(),
            grouped(),
            grouped(),
            shape_of(heads, length, length),
            one_group,
            one_group,
            shape_of(2, length, group_lanes),
            shape_of(length, width, dtype=F32),
            shape_of(length, width),
            shape_of(8, width, dtype=F32),
        ],
        [
            ranks,
            timesteps,
            relative_index,
            bias_table.T,
            first_gain,
            first_shift,
            second_gain,
            second_shift,
            out_bias,
            tokens,
            time_table.reshape(steps // 8, 8, width),
            query_weight,
            key_weight,
            value_weight,
            time_query_weight,
            time_value_weight,
            out_weight,
        ],
        "sswwwwwww" + "h" * 8,
        [
            pltpu.VMEM((6, width, width), BF16),
            pltpu.VMEM((length, width), BF16),
            pltpu.VMEM((8, width), BF16),
            pltpu.VMEM((heads, table_lanes), F32),
            pltpu.VMEM((heads * side, table_lanes), BF16),
            pltpu.VMEM((heads * side, table_lanes), BF16),
            pltpu.VMEM((heads, side, span_lanes), F32),
            pltpu.VMEM((length, width), BF16),
            pltpu.VMEM((groups, length, group_lanes), BF16),
            pltpu.SemaphoreType.DMA((8,)),
        ],
        us=60.0,
        away=(0, 1, 2, 3, 4, 5, 6, 7),
        vmem=56,
    )
    query_rows, key_rows, value_rows, probs = outs[:4]
    mixed_own, mixed_near, mixed_far, middle, normed_own, embed = outs[4:]
    normed_near = swap(normed_own, "mp", 1)
    normed_far = swap(normed_own, "mp", 2)

    normed_first = pl.pallas_call(
        partial(normed_kernel, side),
        out_shape=shape_of(rows, width),
        grid_spec=pltpu.PrefetchScalarGridSpec(
            num_scalar_prefetch=1,
            grid=(groups,),
            in_specs=[
                pl.BlockSpec((8, length), lambda i, me: (0, 0)),
                pl.BlockSpec((length, width), lambda i, me: (i ^ me[0], 0)),
                VMEM,
                VMEM,
            ],
            out_specs=pl.BlockSpec((length, width), lambda i, me: (i, 0)),
        ),
        compiler_params=pltpu.CompilerParams(vmem_limit_bytes=40 * MIB),
        cost_estimate=cost(4.0),
    )(after(ranks, normed_own, cot_far), relative_index, tokens, first_gain, first_shift)

    cot_last = swap(after(cot_far, normed_own), "mp", 1)
    pair = shape_of(2 * length, width)
    hidden_pair = shape_of(2 * length, hidden_width)
    chunk = shape_of(length, width)
    near_active, near_hidden, near_moved, grad_own, grad_near = run(
        partial(feed_near_kernel, side),
        [hidden_pair, hidden_pair, pair, chunk, chunk],
        [
            relative_index,
            normed_own,
            normed_near,
            cotangent,
            cot_near,
            up_weight,
            up_bias,
            down_weight,
        ],
        "vvvvvwvw",
        deps=[normed_first, cot_last],
        us=7.2,
        vmem=FEED,
    )
    near_got = swap(grad_near, "mp", 1)
    normed_last = swap(after(normed_far, grad_near), "mp", 1)
    mixed_far = swap(mixed_far, "mp", 2)
    active, hidden, moved, grad_far, grad_last, up_bias_sum = run(
        partial(feed_far_kernel, side),
        [hidden_pair, hidden_pair, pair, chunk, chunk, shape_of(8, hidden_width, dtype=F32)],
        [
            relative_index,
            normed_far,
            normed_last,
            cot_far,
            cot_last,
            up_weight,
            up_bias,
            down_weight,
            near_hidden,
        ],
        "vvvvvwvwv",
        us=7.5,
        deps=[near_got],
        vmem=FEED,
    )
    last_got = swap(grad_last, "mp", 1)
    half = shape_of(hidden_width // 2, width)
    keep, send = run(
        partial(down_grad_kernel, levels[0]),
        [half, half],
        [ranks, near_active, near_moved, active, moved],
        "svvvv",
        deps=[up_bias_sum, mixed_far],
        us=14.0,
        vmem=FEED,
    )
    down = Total(ranks, levels, keep, send)
    grad_sent = run(add_kernel, chunk, [grad_far, last_got], deps=[keep], vmem=4)
    far_got = swap(grad_sent, "mp", 2)
    mixed_last = swap(after(mixed_far, grad_sent), "mp", 1)
    mixed_near = swap(after(mixed_near, grad_sent), "mp", 1)
    half = shape_of(width // 2, hidden_width)
    keep, send = run(
        partial(up_grad_kernel, other_order[0]),
        [half, half],
        [ranks, normed_own, normed_near, normed_far, normed_last, near_hidden, hidden],
        "s" + "v" * 6,
        [pltpu.VMEM((rows, width), BF16)],
        deps=[grad_sent],
        us=4.9,
        vmem=FEED,
    )
    up = Total(ranks, other_order, keep, send, cross=True)
    chunks = shape_of(2, length, width)
    out_keep, out_send = run(
        out_kernel, [chunks, chunks], [near_active, active, down_weight], "vvw", deps=[keep], us=5.0, vmem=FEED
    )
    out_got = swap(out_send, "mp", 1)
    grad_branch, grad_middle, middle_sums = run(
        middle_kernel,
        [chunk, shape_of(length, width, dtype=F32), shape_of(8, width, dtype=F32)],
        [grad_own, near_got, far_got, middle, near_moved, second_gain],
        "vvvvvw",
        deps=[out_keep],
        vmem=8,
    )
    branch_near = swap(grad_branch, "mp", 1)
    branch_far = swap(grad_branch, "mp", 2)
    last = middle_sums

    tail = slots * table_lanes // LANES
    two_groups = pltpu.VMEM((2, length, group_lanes), BF16)
    back_scratch = [
        pltpu.VMEM((side, 2 * slots, span_lanes), F32),
        two_groups,
        two_groups,
        two_groups,
        pltpu.VMEM((2, slots, length, length), BF16),
        pltpu.SemaphoreType.DMA((2, 4)),
    ]
    grads_shape = shape_of(3, 2, length, group_lanes)
    packed_shape = shape_of(length + tail, packed_lanes)
    packed_pair = shape_of(2, length + tail, packed_lanes)
    heads_in = [query_rows, key_rows, value_rows, probs]
    packed_far, far_grads, grad_mixed = run(
        partial(attend_back_kernel, dims, (2, 3)),
        [packed_pair, grads_shape, grouped()],
        [ranks, grad_branch, out_weight] + heads_in,
        "svwhhhh",
        back_scratch,
        deps=[last, mixed_last, mixed_near],
        us=8.3,
    )
    packed_far = swap(packed_far, "mp", 2)
    last = grad_mixed
    packed_0, packed_1, near_grads = run(
        partial(attend_back_kernel, dims, (0, 1)),
        [packed_shape, packed_shape, grads_shape],
        [ranks, grad_mixed] + heads_in,
        "svhhhh",
        back_scratch,
        deps=[last],
        us=8.3,
    )
    last = down.split([packed_0, branch_far])
    branch_last = swap(after(branch_far, last), "mp", 1)
    last = up.split([last])
    image_rows, tokens_grad = run(
        partial(tokens_kernel, dims),
        [shape_of(8, width, dtype=F32), shape_of(length, width, dtype=F32)],
        [
            ranks,
            near_grads,
            far_grads,
            query_weight,
            key_weight,
            value_weight,
            relative_index,
            first_gain,
            grad_middle,
            middle_sums,
            tokens,
        ],
        "svvwwwwwvvh",
        [
            pltpu.VMEM((3, length, width), BF16),
            pltpu.VMEM((length, width), BF16),
            pltpu.SemaphoreType.DMA,
        ],
        deps=[last, branch_last],
        us=8.6,
        away=(1,),
        vmem=24,
    )
    lines_far = swap(image_rows, "mp", 2)
    last = down.exchange([image_rows, packed_far, lines_far, up.got])
    lines_near = swap(after(jnp.concatenate([image_rows, lines_far], axis=0), last), "mp", 1)
    packed_last = swap(after(packed_far, last), "mp", 1)
    packed_1 = swap(after(packed_1, last), "mp", 1)
    half = shape_of(group_width, width)
    images = dp_size * groups
    tail_rows = max(tail, images)
    more = shape_of(group_width + tail_rows // 2, width)
    keep_first, keep_second, send_first, send_second = run(
        partial(weights_kernel, dims, levels[0]),
        [more, half, more, half],
        [ranks, timesteps, normed_first, packed_0, packed_1, packed_far, packed_last]
        + [grad_branch, branch_near, branch_far, branch_last]
        + [mixed_own, mixed_near, mixed_far, mixed_last]
        + [image_rows, lines_far, lines_near, up_bias_sum, time_query_weight, time_value_weight],
        "ss" + "v" * 17 + "hh",
        [
            pltpu.VMEM((rows, packed_lanes), BF16),
            pltpu.VMEM((rows, width), BF16),
            pltpu.VMEM((rows, group_lanes), BF16),
            pltpu.VMEM((tail_rows, width), F32),
            pltpu.VMEM((2, group_width, width), BF16),
            pltpu.SemaphoreType.DMA((2,)),
        ],
        deps=[last],
        us=5.2,
    )
    first = Total(ranks, levels, keep_first, send_first, tail_rows // 2)
    last = down.finish([keep_second])
    last = first.split([last], 8.0)
    second = Total(ranks, levels, keep_second, send_second)
    last = up.exchange([last])
    out_far = swap(add_low(out_keep[1], out_got[1]), "mp", 2)
    last = second.split([last], 8.0)
    last = down.join([last])
    last = first.exchange([last])
    last = up.finish([last])
    last = up.join([last])
    last = first.finish([last])
    last = second.exchange([last])
    last = first.join([last])
    down_grad = widen(ranks, levels[0], down.keep, down.got, last)
    last = down_grad
    last = second.finish([last])
    last = second.join([last])
    up_grad = widen(ranks, other_order[1], up.keep, up.got, last, cross=True)
    wide = shape_of(group_width, width, dtype=F32)
    query_grad, key_grad, tail_sums = run(
        partial(widen_pair_kernel, levels[0]),
        [wide, wide, shape_of(tail_rows, width, dtype=F32)],
        [ranks, first.keep, first.got],
        "svv",
        away=(0, 1),
        deps=[up_grad],
    )
    value_grad, out_grad = run(
        partial(widen_plain_kernel, levels[0]),
        [wide, wide],
        [ranks, second.keep, second.got],
        "svv",
        away=(0, 1),
        deps=[query_grad],
    )

    time_query_grad, time_value_grad, time_table_grad, table_grad, sums = run(
        partial(finish_kernel, dims, images),
        [
            shape_of(group_width, width, dtype=F32),
            shape_of(group_width, width, dtype=F32),
            shape_of(group_width, steps, dtype=F32),
            shape_of(slots, table_lanes, dtype=F32),
            shape_of(16, group_width, dtype=F32),
        ],
        [tail_sums, time_table],
        "vw",
        away=(0, 1, 2),
        vmem=52,
    )
    first_gain_grad, first_shift_grad, second_gain_grad, second_shift_grad = sums[:4]
    out_bias_grad, down_bias_grad = sums[4], sums[5]
    up_bias_grad = sums[6 : 6 + hidden_width // group_width].reshape(-1)
    bias_table_grad = table_grad[:, : stride * stride].T

    block_out = run(
        partial(block_kernel, side),
        shape_of(length, width),
        [relative_index, out_keep, out_got, out_far, middle, down_bias],
        "wvvvvw",
    )
    return (
        block_out,
        tokens_grad,
        time_table_grad.T,
        query_grad.T,
        key_grad.T,
        value_grad.T,
        time_query_grad.T,
        time_value_grad.T,
        out_grad,
        out_bias_grad,
        first_gain_grad,
        first_shift_grad,
        second_gain_grad,
        second_shift_grad,
        up_grad,
        up_bias_grad,
        down_grad,
        down_bias_grad,
        bias_table_grad,
    )


def solution(mesh):
    whole = P()
    rows = P(("dp", "mp"), None)
    columns = P(None, "mp")
    split = P("mp")
    placed = (
        (P("dp", None), P("dp"))
        + (whole,) * 13
        + (columns, split, P("mp", None), whole, whole, rows)
    )
    return jax.shard_map(
        on_device,
        mesh=mesh,
        in_specs=placed,
        out_specs=(rows, rows)
        + (columns,) * 6
        + (P("mp", None),)
        + (split,) * 5
        + (columns, split, P("mp", None), split, columns),
        check_vma=False,
    )
```
